32 devices in a mesh: rep: 4 (over y, x), shard: 8 (over z, core).
Axes of the slice: x: 2, y: 2, z: 4, core: 2. Of those that a mesh axis runs over, the one named last changes fastest.
Arguments:
- tokens: bfloat16 [16384, 1536], P(('rep', 'shard')), may hold values from -6 to 6
- lengths: int32 [32], P(('rep', 'shard')), may hold values from 128 to 512, as said below
- buckets: int32 [1023], replicated, may hold values from 0 to 31, as said below
- w_query: bfloat16 [1536, 768], P('shard'), may hold values from -0.0390625 to 0.0390625
- w_key: bfloat16 [1536, 768], P('shard'), may hold values from -0.15625 to 0.15625
- w_value: bfloat16 [1536, 768], P('shard'), may hold values from -0.15625 to 0.15625
- w_out: bfloat16 [768, 1536], P('shard'), may hold values from -1.25 to 1.25
- w_gate: bfloat16 [1536, 3968], P('shard'), may hold values from -0.15625 to 0.15625
- w_up: bfloat16 [1536, 3968], P('shard'), may hold values from -0.15625 to 0.15625
- w_down: bfloat16 [3968, 1536], P('shard'), may hold values from -0.09375 to 0.09375
- bias_table: bfloat16 [32, 12], P('shard'), may hold values from -4 to 4
- norm_attn: bfloat16 [1536], P('shard'), may hold values from 0.099609375 to 1.8984375
- norm_ffn: bfloat16 [1536], P('shard'), may hold values from 0.099609375 to 1.8984375
- cotangent: bfloat16 [16384, 1536], P(('rep', 'shard')), may hold values from -6 to 6
Outputs:
- output: bfloat16 [16384, 1536], P(('rep', 'shard'))
- grad_tokens: bfloat16 [16384, 1536], P(('rep', 'shard'))
- grad_query: float32 [1536, 768], P('shard')
- grad_key: float32 [1536, 768], P('shard')
- grad_value: float32 [1536, 768], P('shard')
- grad_out: float32 [768, 1536], P('shard')
- grad_gate: float32 [1536, 3968], P('shard')
- grad_up: float32 [1536, 3968], P('shard')
- grad_down: float32 [3968, 1536], P('shard')
- grad_table: float32 [32, 12], P('shard')
- grad_norm_attn: float32 [1536], P('shard')
- grad_norm_ffn: float32 [1536], P('shard')
The draws below stay inside these ranges and needn't reach their ends.
Inputs may be any that keep to these rules, and one draw needn't show every extreme that they name: `lengths`: some sequence has exactly 512 valid bytes. `buckets`: non-decreasing in the absolute distance on each side; buckets 0 to 15 for distances of 0 or less, 16 to 31 for positive ones.
All inputs are finite; a program needn't handle non-finite values.
Results may differ from the reference program's by a relative error of at most 0.02.
Values may be sent and summed in bfloat16 or wider, within the bound.
No kernel may reach another device: no remote copies, remote signals or barrier semaphores. Data moves between devices by JAX's collectives and lax.ppermute only.
A program may use at most 320 MiB of HBM per device.

```python
import jax
import jax.numpy as jnp
from jax import lax

D = 1536
HEADS = 12
DK = 64
FF = 3968
BUCKETS = 32
LEN = 512
INNER = 768
SEQS = 32
TOKENS = 16384


def draw_lengths(key, part):
    first_key, second_key = jax.random.split(jax.random.fold_in(key, 11))
    drawn = jax.random.randint(first_key, (SEQS,), LEN // 4, LEN + 1)
    full_at = jax.random.randint(second_key, (), 0, SEQS)
    return jnp.where(jnp.arange(SEQS) == full_at, LEN, drawn).astype(jnp.int32)


def draw_buckets(key, part):
    shuffled = jax.random.permutation(jax.random.fold_in(key, 23), LEN - 8) + 8
    far_bounds = jnp.sort(shuffled[:8]).astype(jnp.int32)
    bounds_all = jnp.concatenate([jnp.arange(1, 8, dtype=jnp.int32), far_bounds])
    relative = jnp.arange(2 * LEN - 1, dtype=jnp.int32) - (LEN - 1)
    distance = jnp.abs(relative)
    counted = jnp.sum((bounds_all[None, :] <= distance[:, None]).astype(jnp.int32), axis=1)
    return (counted + jnp.where(relative > 0, 16, 0)).astype(jnp.int32)


def spiked(values, key, source, target, blocks, factor):
    owner, partner = [(jnp.arange(values.shape[axis_at]) // (values.shape[axis_at] // blocks)).reshape([-1 if axis == axis_at else 1 for axis in range(values.ndim)]) for axis_at in (source, target)]
    chosen = jax.random.permutation(key, blocks)[partner]
    strong = (owner == chosen) | (owner == (partner + blocks // 2) % blocks)
    return jnp.where(strong, factor * values, values)


def block_scale(key, extent, shards, low, high):
    def one(axis_at, blocks):
        steps = jax.random.uniform(jax.random.fold_in(jax.random.fold_in(key, 6), axis_at), (blocks,), jnp.float32, low / len(shards), high / len(shards))
        return jnp.repeat(jnp.exp(steps), extent[axis_at] // blocks).reshape((-1,) + (1,) * (len(extent) - axis_at - 1))

    loudness = one(*shards[0])
    for cut in shards[1:]:
        loudness = loudness * one(*cut)
    return loudness


def normal_values(rng, shape, spread, bound, cuts=(), kind=jnp.bfloat16):
    values = spread * jax.random.normal(rng, shape, jnp.float32)
    if cuts:
        values = values * block_scale(rng, shape, cuts, -0.22, 0.18)
    return jnp.clip(values, -bound, bound).astype(kind)


def heavy_noise(rng, extent, spread, bound, cuts, heavy, held_as=jnp.bfloat16):
    entries = spread * jax.random.normal(rng, extent, jnp.float32)
    if cuts:
        entries = entries * block_scale(rng, extent, cuts, -0.22, 0.18)
    return jnp.clip(spiked(entries, jax.random.fold_in(rng, 3), *heavy), -bound, bound).astype(held_as)


def setup_inputs(seed: int = 0) -> dict:
    keys = jax.random.split(jax.random.key(seed), 15)
    tokens = heavy_noise(keys[0], (TOKENS, D), 1.0, 6.0, ((0, 32),), (0, 1, 32, 2.75))
    lengths = draw_lengths(jax.random.fold_in(keys[14], 71), 0)
    buckets = draw_buckets(jax.random.fold_in(keys[14], 71), 0)
    w_query = normal_values(keys[3], (D, INNER), (D * DK // 4) ** -0.5, 0.0390625, ((0, 8),))
    w_key = normal_values(keys[4], (D, INNER), D ** -0.5, 0.15625, ((0, 8),))
    w_value = normal_values(keys[5], (D, INNER), D ** -0.5, 0.15625, ((0, 8),))
    w_out = normal_values(keys[6], (INNER, D), (max(INNER // 32, 1)) ** -0.5, 1.25, ((0, 8),))
    w_gate = normal_values(keys[7], (D, FF), D ** -0.5, 0.15625, ((0, 8),))
    w_up = normal_values(keys[8], (D, FF), D ** -0.5, 0.15625, ((0, 8),))
    w_down = normal_values(keys[9], (FF, D), FF ** -0.5, 0.09375, ((0, 8),))
    bias_table = normal_values(keys[10], (BUCKETS, HEADS), 1.0, 4.0, ((0, 8),))
    norm_attn = jnp.clip(1.0 + 0.18 * jax.random.normal(keys[11], (D,), jnp.float32), 0.099609375, 1.8984375).astype(jnp.bfloat16)
    norm_ffn = jnp.clip(1.0 + 0.18 * jax.random.normal(keys[12], (D,), jnp.float32), 0.099609375, 1.8984375).astype(jnp.bfloat16)
    cotangent = normal_values(keys[13], (TOKENS, D), 1.0, 6.0, ((0, 32),))
    return dict(tokens=tokens, lengths=lengths, buckets=buckets, w_query=w_query, w_key=w_key, w_value=w_value, w_out=w_out, w_gate=w_gate, w_up=w_up, w_down=w_down, bias_table=bias_table, norm_attn=norm_attn, norm_ffn=norm_ffn, cotangent=cotangent)


EPSILON = 1e-06
NEG_FILL = -1000000000.0

@jax.custom_vjp
def low(v):
    return lax.optimization_barrier(v.astype(jnp.bfloat16)).astype(jnp.float32)

@jax.custom_vjp
def low_back(v):
    return v

def low_keep(v):
    return (low(v), None)

def low_pass(kept, grad):
    return (grad,)

def back_keep(v):
    return (v, None)

def back_low(kept, grad):
    return (low(grad),)
low.defvjp(low_keep, low_pass)
low_back.defvjp(back_keep, back_low)

def matmul(left, right):
    return jnp.dot(left, right, precision=lax.Precision.HIGHEST)

def reference(tokens, lengths, buckets, w_query, w_key, w_value, w_out, w_gate, w_up, w_down, bias_table, norm_attn, norm_ffn, cotangent):
    weights = (w_query.astype(jnp.float32), w_key.astype(jnp.float32), w_value.astype(jnp.float32), w_out.astype(jnp.float32), w_gate.astype(jnp.float32), w_up.astype(jnp.float32), w_down.astype(jnp.float32), bias_table.astype(jnp.float32), norm_attn.astype(jnp.float32), norm_ffn.astype(jnp.float32))
    positions = jnp.arange(LEN, dtype=jnp.int32)
    rel_index = (positions[None, :] - positions[:, None] + (LEN - 1)).astype(jnp.int32)

    def layer_seq(seq_rows, valid_len, params):
        p_query, p_key, p_value, p_out, p_gate, p_up, p_down, p_table, gain_attn, gain_ffn = params
        scale_one = lax.rsqrt(lax.optimization_barrier(jnp.mean(seq_rows * seq_rows, axis=-1, keepdims=True)) + EPSILON)
        normed_one = low(seq_rows * scale_one * gain_attn)
        queries = low(low_back(matmul(normed_one, p_query))).reshape(LEN, HEADS, DK)
        key_rows = low(low_back(matmul(normed_one, p_key))).reshape(LEN, HEADS, DK)
        value_rows = low(low_back(matmul(normed_one, p_value))).reshape(LEN, HEADS, DK)
        rel_bias = jnp.take(p_table, buckets, axis=0)
        bias_full = jnp.transpose(jnp.take(rel_bias, rel_index, axis=0), (2, 0, 1))
        mask_row = jnp.where(positions < valid_len, jnp.float32(0.0), jnp.float32(NEG_FILL))
        scores = jnp.einsum('qhd,khd->hqk', queries, key_rows, precision=lax.Precision.HIGHEST)
        scores = low_back(scores + bias_full + mask_row[None, None, :])
        attn_prob = low(jax.nn.softmax(scores, axis=-1))
        context = jnp.einsum('hqk,khd->qhd', attn_prob, value_rows, precision=lax.Precision.HIGHEST)
        context = low(low_back(context.reshape(LEN, INNER)))
        attended = seq_rows + low_back(matmul(context, p_out))
        scale_two = lax.rsqrt(lax.optimization_barrier(jnp.mean(attended * attended, axis=-1, keepdims=True)) + EPSILON)
        normed_two = low(attended * scale_two * gain_ffn)
        gate_pre = low_back(matmul(normed_two, p_gate))
        up_pre = low_back(matmul(normed_two, p_up))
        hidden = low(jax.nn.gelu(gate_pre, approximate=True) * up_pre)
        return attended + low_back(matmul(hidden, p_down))

    def group_fn(seq_block, len_block, params):
        return jax.vmap(lambda seq_rows, valid_len: layer_seq(seq_rows, valid_len, params))(seq_block, len_block)
    checked = jax.checkpoint(group_fn)

    def forward(inputs, params):
        blocks = inputs.reshape(SEQS // 4, 4, LEN, D)
        len_blocks = lengths.reshape(SEQS // 4, 4)

        def one_block(element):
            return checked(element[0], element[1], params)
        outputs = lax.map(one_block, (blocks, len_blocks))
        return outputs.reshape(TOKENS, D)
    result, pullback = jax.vjp(forward, tokens.astype(jnp.float32), weights)
    grad_input, grads = pullback(cotangent.astype(jnp.float32))
    return (result.astype(jnp.bfloat16), grad_input.astype(jnp.bfloat16), grads[0], grads[1], grads[2], grads[3], grads[4], grads[5], grads[6], grads[7], grads[8], grads[9])
```

```python
import functools

import jax
import jax.numpy as jnp
from jax import lax
from jax.experimental import pallas as pl
from jax.experimental.pallas import tpu as pltpu
from jax.sharding import PartitionSpec as P

NEG_FILL = -1000000000.0
VMEM_LIMIT = 56 * 1024 * 1024
TOEP = 128


def dot_nn(a, b):
    return lax.dot_general(a, b, (((1,), (0,)), ((), ())), preferred_element_type=jnp.float32)


def dot_nt(a, b):
    return lax.dot_general(a, b, (((1,), (1,)), ((), ())), preferred_element_type=jnp.float32)


def dot_tn(a, b):
    return lax.dot_general(a, b, (((0,), (0,)), ((), ())), preferred_element_type=jnp.float32)


def biased_scores(rows_k, rows_q, bias_row, valid, length):
    steps = length // TOEP
    raw = dot_nt(rows_k, rows_q)
    width = bias_row.shape[-1]
    spread = jnp.broadcast_to(bias_row, (TOEP, width))
    table = pltpu.roll(spread, width - (TOEP - 1), 1, stride=1, stride_axis=0)
    blocks = []
    for step in range(steps):
        start = TOEP * (steps - 1 - step)
        row_at = lax.broadcasted_iota(jnp.int32, (TOEP, length), 0) + step * TOEP
        mask = jnp.where(row_at < valid, 0.0, NEG_FILL)
        blocks.append(
            raw[step * TOEP : (step + 1) * TOEP] + table[:, start : start + length] + mask
        )
    return jnp.concatenate(blocks, axis=0)


def attention_forward(valid_ref, bias_ref, q_ref, k_ref, v_ref, ctx_ref, lse_ref, *, head_size):
    length = q_ref.shape[1]
    pair = q_ref.shape[2] // head_size
    q, k, v = q_ref[0], k_ref[0], v_ref[0]
    lane_head = lax.broadcasted_iota(jnp.int32, q.shape, 1) // head_size
    v_turned = v.T
    outs = []
    for head in range(pair):
        own_q = jnp.where(lane_head == head, q, jnp.zeros_like(q))
        scores = biased_scores(k, own_q, bias_ref[0, head : head + 1], valid_ref[0], length)
        top = jnp.max(scores, axis=0, keepdims=True)
        terms = jnp.exp(scores - top)
        total = jnp.sum(terms, axis=0, keepdims=True)
        probs = (terms * (1.0 / total)).astype(jnp.bfloat16)
        lse_ref[0, head : head + 1] = top + jnp.log(total)
        outs.append(dot_nn(v_turned, probs)[head * head_size : (head + 1) * head_size])
    ctx_ref[...] = jnp.concatenate(outs, axis=0).T.astype(jnp.bfloat16)


def attention_backward(
    valid_ref, bias_ref, q_ref, k_ref, v_ref, dctx_ref, lse_ref, dq_ref, dk_ref, dv_ref, rel_ref, *, head_size
):
    length = q_ref.shape[1]
    pair = q_ref.shape[2] // head_size
    steps = length // TOEP
    q, k, v, dctx = q_ref[0], k_ref[0], v_ref[0], dctx_ref[...]
    lane_head = lax.broadcasted_iota(jnp.int32, q.shape, 1) // head_size
    k_turned = k.T
    width = bias_ref.shape[-1]
    flip = (
        lax.broadcasted_iota(jnp.int32, (TOEP, TOEP), 0)
        + lax.broadcasted_iota(jnp.int32, (TOEP, TOEP), 1)
        == TOEP - 1
    ).astype(jnp.bfloat16)
    dq_parts = []
    dk = dv = None
    for head in range(pair):
        mine = lane_head == head
        own_q = jnp.where(mine, q, jnp.zeros_like(q))
        own_d = jnp.where(mine, dctx, jnp.zeros_like(dctx))
        scores = biased_scores(k, own_q, bias_ref[0, head : head + 1], valid_ref[0], length)
        probs = jnp.exp(scores - lse_ref[0, head : head + 1])
        d_probs = dot_nt(v, own_d)
        inner = jnp.sum(d_probs * probs, axis=0, keepdims=True)
        d_scores = (probs * (d_probs - inner)).astype(jnp.bfloat16)
        part_v = dot_nn(probs.astype(jnp.bfloat16), own_d)
        part_k = dot_nn(d_scores, own_q)
        dv = part_v if dv is None else dv + part_v
        dk = part_k if dk is None else dk + part_k
        dq_parts.append(dot_nn(k_turned, d_scores)[head * head_size : (head + 1) * head_size])
        fold = None
        for step in range(steps):
            start = TOEP * (steps - 1 - step)
            turned = dot_nn(flip, d_scores[step * TOEP : (step + 1) * TOEP])
            pieces = []
            if start:
                pieces.append(jnp.zeros((TOEP, start), jnp.float32))
            pieces.append(turned)
            if width - start - length:
                pieces.append(jnp.zeros((TOEP, width - start - length), jnp.float32))
            padded = jnp.concatenate(pieces, axis=1)
            fold = padded if fold is None else fold + padded
        lined = pltpu.roll(fold, 0, 1, stride=1, stride_axis=0)
        rel_ref[0, head : head + 1] = jnp.sum(lined, axis=0, keepdims=True)
    dq_ref[0] = jnp.concatenate(dq_parts, axis=0).T.astype(jnp.bfloat16)
    dk_ref[0] = dk.astype(jnp.bfloat16)
    dv_ref[0] = dv.astype(jnp.bfloat16)


def run_forward(valid, bias_rows, qkv, head_size):
    halves, length, wide = qkv.shape
    half = wide // 3
    per = half // 128
    pairs = halves * per
    width = bias_rows.shape[-1]
    spec = lambda kind: pl.BlockSpec((1, length, 128), lambda p: (p // per, 0, kind * per + p % per))
    return pl.pallas_call(
        functools.partial(attention_forward, head_size=head_size),
        grid=(pairs,),
        in_specs=[
            pl.BlockSpec(memory_space=pltpu.SMEM),
            pl.BlockSpec((1, 2, width), lambda p: (p, 0, 0)),
            spec(0), spec(1), spec(2),
        ],
        out_specs=[
            pl.BlockSpec((length, 128), lambda p: (0, p)),
            pl.BlockSpec((1, 2, length), lambda p: (p, 0, 0)),
        ],
        out_shape=[
            jax.ShapeDtypeStruct((length, halves * half), jnp.bfloat16),
            jax.ShapeDtypeStruct((pairs, 2, length), jnp.float32),
        ],
        compiler_params=pltpu.CompilerParams(vmem_limit_bytes=VMEM_LIMIT),
        cost_estimate=pl.CostEstimate(
            flops=8 * pairs * 2 * length * length * 128,
            bytes_accessed=2 * qkv.size * 2,
            transcendentals=pairs * 2 * length * length,
        ),
    )(valid, bias_rows, qkv, qkv, qkv)


def run_backward(valid, bias_rows, qkv, d_context, lse, head_size):
    halves, length, wide = qkv.shape
    half = wide // 3
    per = half // 128
    pairs = halves * per
    width = bias_rows.shape[-1]
    spec = lambda kind: pl.BlockSpec((1, length, 128), lambda p: (p // per, 0, kind * per + p % per))
    out_spec = pl.BlockSpec((1, length, 128), lambda p: (p // per, 0, p % per))
    grad = jax.ShapeDtypeStruct((halves, length, half), jnp.bfloat16)
    row = pl.BlockSpec((1, 2, width), lambda p: (p, 0, 0))
    return pl.pallas_call(
        functools.partial(attention_backward, head_size=head_size),
        grid=(pairs,),
        in_specs=[
            pl.BlockSpec(memory_space=pltpu.SMEM),
            row,
            spec(0), spec(1), spec(2),
            pl.BlockSpec((length, 128), lambda p: (0, p)),
            pl.BlockSpec((1, 2, length), lambda p: (p, 0, 0)),
        ],
        out_specs=[out_spec, out_spec, out_spec, row],
        out_shape=[grad, grad, grad, jax.ShapeDtypeStruct((pairs, 2, width), jnp.float32)],
        compiler_params=pltpu.CompilerParams(vmem_limit_bytes=VMEM_LIMIT),
        cost_estimate=pl.CostEstimate(
            flops=16 * pairs * 2 * length * length * 128,
            bytes_accessed=4 * qkv.size * 2,
            transcendentals=pairs * 2 * length * length,
        ),
    )(valid, bias_rows, qkv, qkv, qkv, d_context, lse)


EPSILON = 1e-06
AXES = ("rep", "shard")


def split_kernel(core_ref, w_ref, keep_ref, send_ref, *, cuts, piece, padded):
    rows = w_ref.shape[0]
    first = core_ref[0] == 0
    w = w_ref[...].astype(jnp.float32)
    filler = jnp.zeros((rows, padded - piece), jnp.float32)
    for cut in range(cuts):
        even, odd = [
            jnp.concatenate(
                [w[:, (2 * cut + side) * piece : (2 * cut + side + 1) * piece], filler], axis=1
            )
            for side in (0, 1)
        ]
        keep_ref[:, cut * padded : (cut + 1) * padded] = jnp.where(first, even, odd).astype(
            jnp.bfloat16
        )
        send_ref[:, cut * padded : (cut + 1) * padded] = jnp.where(first, odd, even).astype(
            jnp.bfloat16
        )


def split_columns(core, w, piece, padded):
    rows, wide = w.shape
    cuts = wide // (2 * piece)
    out = jax.ShapeDtypeStruct((rows, cuts * padded), jnp.bfloat16)
    return pl.pallas_call(
        functools.partial(split_kernel, cuts=cuts, piece=piece, padded=padded),
        in_specs=[
            pl.BlockSpec(memory_space=pltpu.SMEM),
            pl.BlockSpec(memory_space=pltpu.VMEM),
        ],
        out_specs=[pl.BlockSpec(memory_space=pltpu.VMEM)] * 2,
        out_shape=[out, out],
        compiler_params=pltpu.CompilerParams(vmem_limit_bytes=VMEM_LIMIT),
        cost_estimate=pl.CostEstimate(flops=w.size, bytes_accessed=4 * w.size, transcendentals=0),
    )(core[None], w)


def join_kernel(core_ref, keep_ref, recv_ref, out_ref, *, cuts, piece, padded):
    first = core_ref[0] == 0
    for cut in range(cuts):
        mine = keep_ref[:, cut * padded : (cut + 1) * padded].astype(jnp.float32)
        other = recv_ref[:, cut * padded : (cut + 1) * padded].astype(jnp.float32)
        even = jnp.where(first, mine, other)
        odd = jnp.where(first, other, mine)
        out_ref[:, 2 * cut * piece : (2 * cut + 1) * piece] = even[:, :piece]
        out_ref[:, (2 * cut + 1) * piece : (2 * cut + 2) * piece] = odd[:, :piece]


def join_columns(core, keep, recv, piece, padded):
    rows = keep.shape[0]
    cuts = keep.shape[1] // padded
    return pl.pallas_call(
        functools.partial(join_kernel, cuts=cuts, piece=piece, padded=padded),
        in_specs=[
            pl.BlockSpec(memory_space=pltpu.SMEM),
            pl.BlockSpec(memory_space=pltpu.VMEM),
            pl.BlockSpec(memory_space=pltpu.VMEM),
        ],
        out_specs=pl.BlockSpec(memory_space=pltpu.VMEM),
        out_shape=jax.ShapeDtypeStruct((rows, 2 * cuts * piece), jnp.float32),
        compiler_params=pltpu.CompilerParams(vmem_limit_bytes=VMEM_LIMIT),
        cost_estimate=pl.CostEstimate(
            flops=keep.size, bytes_accessed=12 * keep.size, transcendentals=0
        ),
    )(core[None], keep, recv)


def place_kernel(at_ref, *refs, cuts):
    sources, out_ref, sems = refs[:-2], refs[-2], refs[-1]
    copies = []
    for number, (source, start, rows) in enumerate(cuts):
        to = pl.multiple_of(at_ref[number], 16)
        copies.append(
            pltpu.make_async_copy(
                sources[source].at[pl.ds(start, rows)],
                out_ref.at[pl.ds(to, rows)],
                sems.at[number],
            )
        )
    for copy in copies:
        copy.start()
    for copy in copies:
        copy.wait()


def place_rows(sources, cuts, total):
    wide = sources[0].shape[1]
    if any(cut[2] % 16 or cut[1] % 16 for cut in cuts):
        out = jnp.zeros((total, wide), sources[0].dtype)
        for source, start, rows, to in cuts:
            out = lax.dynamic_update_slice(out, sources[source][start : start + rows], (to, 0))
        return out
    places = jnp.stack([jnp.asarray(cut[3], jnp.int32) for cut in cuts])
    return pl.pallas_call(
        functools.partial(place_kernel, cuts=[cut[:3] for cut in cuts]),
        in_specs=[pl.BlockSpec(memory_space=pltpu.SMEM)]
        + [pl.BlockSpec(memory_space=pl.ANY)] * len(sources),
        out_specs=pl.BlockSpec(memory_space=pltpu.VMEM),
        out_shape=jax.ShapeDtypeStruct((total, wide), sources[0].dtype),
        scratch_shapes=[pltpu.SemaphoreType.DMA((len(cuts),))],
        compiler_params=pltpu.CompilerParams(vmem_limit_bytes=VMEM_LIMIT),
        cost_estimate=pl.CostEstimate(
            flops=0, bytes_accessed=4 * total * wide, transcendentals=0
        ),
    )(places, *sources)


def norm_back(upstream, unit_rows, scale_rows, gain_rows):
    scaled = upstream * gain_rows
    return scale_rows * (scaled - unit_rows * jnp.mean(scaled * unit_rows, axis=-1, keepdims=True))


def tied(value, *after):
    return lax.optimization_barrier((value, *after))[0]


class Links:
    def __init__(self, reps, group):
        self.reps, self.group, self.planes = reps, group, group // 2
        self.stages = reps.bit_length() - 1
        self.q = lax.axis_index("rep")
        self.place = lax.axis_index("shard")
        self.core = self.place % 2
        self.plane = self.place // 2

    def move(self, value, target):
        pairs = []
        for r in range(self.reps):
            for s in range(self.group):
                to_r, to_s = target(r, s)
                pairs.append((r * self.group + s, to_r * self.group + to_s))
        return lax.ppermute(value, AXES, pairs)

    def across(self, value):
        return self.move(value, lambda r, s: (r, s ^ 1))

    def along(self, value, step):
        return self.move(value, lambda r, s: (r, (s + 2 * step) % self.group))

    def bit_of(self, stage, core):
        return 1 << (stage if core == 0 else self.stages - 1 - stage)

    def swap(self, value, stage):
        return self.move(value, lambda r, s: (r ^ self.bit_of(stage, s % 2), s))

    def bit(self, stage):
        return jnp.where(self.core == 0, self.bit_of(stage, 0), self.bit_of(stage, 1))

    def gathered(self, value):
        parts, offsets = [value], [jnp.int32(0)]
        for stage in range(self.stages):
            parts += [self.swap(part, stage) for part in parts]
            offsets += [offset ^ self.bit(stage) for offset in offsets]
        return parts, [self.q ^ offset for offset in offsets]

    def slot_owners(self):
        owners = []
        for slot in range(self.reps):
            owner = self.q
            for stage in range(self.stages):
                if (slot >> (self.stages - 1 - stage)) & 1:
                    owner = owner ^ self.bit(stage)
            owners.append(owner)
        return owners

    def in_slots(self, value):
        wide = value.shape[1] // self.reps
        blocks = [value[:, k * wide : (k + 1) * wide] for k in range(self.reps)]
        return jnp.concatenate([pick(blocks, owner) for owner in self.slot_owners()], axis=1)

    def from_other_core(self, value, axis):
        blocks = jnp.split(value, self.reps, axis=axis)
        turned = []
        for slot in range(self.reps):
            other = sum(((slot >> k) & 1) << (self.stages - 1 - k) for k in range(self.stages))
            turned.append(blocks[other])
        return jnp.concatenate(turned, axis=axis)

    def scattered(self, make, axis, rows):
        low, high = self.reps // 2, self.reps
        arrived = []

        def summed(first, last):
            value = make(first, last)
            for block in arrived:
                size = value.shape[axis] // (last - first)
                value = value + lax.slice_in_dim(
                    block, first * size, last * size, axis=axis
                ).astype(jnp.float32)
            return value.astype(jnp.bfloat16)

        for stage in range(self.stages):
            arrived.append(self.swap(summed(low, high), stage))
            low, high = low // 2, low
        mine = summed(0, 1)
        total = lax.dynamic_slice_in_dim(mine, self.plane * rows, rows).astype(jnp.float32)
        for step in range(1, self.planes):
            to = (self.plane + step) % self.planes
            part = lax.dynamic_slice_in_dim(mine, to * rows, rows)
            total = total + self.along(part, step).astype(jnp.float32)
        parts, owners = self.gathered(total.astype(jnp.bfloat16))
        return in_order(parts, owners)

    def summed_everywhere(self, value):
        step = 1
        while step < self.reps:
            value = value + self.move(value, lambda r, s: (r ^ step, s))
            step *= 2
        step = 1
        while step < self.group:
            value = value + self.move(value, lambda r, s: (r, s ^ step))
            step *= 2
        return value


def pick(blocks, index):
    value = blocks[0]
    for k in range(1, len(blocks)):
        value = jnp.where(index == k, blocks[k], value)
    return value


def in_order(parts, owners):
    ordered = []
    for k in range(len(parts)):
        value = parts[0]
        for part, owner in zip(parts[1:], owners[1:]):
            value = jnp.where(owner == k, part, value)
        ordered.append(value)
    return ordered


def nn(left, right):
    return jnp.dot(left, right, preferred_element_type=jnp.float32)


def nt(left, right):
    return lax.dot_general(
        left, right, (((1,), (1,)), ((), ())), preferred_element_type=jnp.float32
    )


def tn(left, right):
    return lax.dot_general(
        left, right, (((0,), (0,)), ((), ())), preferred_element_type=jnp.float32
    )


def layer(
    reps,
    group,
    tokens,
    lengths,
    buckets,
    w_query,
    w_key,
    w_value,
    w_out,
    w_gate,
    w_up,
    w_down,
    bias_table,
    norm_attn,
    norm_ffn,
    cotangent,
):
    links = Links(reps, group)
    planes, core, plane, q = links.planes, links.core, links.plane, links.q
    first_core = core == 0
    length, width = tokens.shape
    shard_rows, inner = w_query.shape
    head_count = bias_table.shape[1]
    head_size = inner // head_count
    bucket_count = bias_table.shape[0] * group
    half = inner // 2
    piece = w_down.shape[0]
    unit = max(128, 16 * reps)
    padded = (piece + unit - 1) // unit * unit

    def by_core(zero, one):
        return jnp.where(first_core, zero, one)

    def gather_planes(share):
        return [links.along(share, step) for step in range(1, planes)]

    def gather_rows(share, own_plane, plane_rows, after=()):
        share = tied(share, *after) if after else share
        rows = share.shape[0]
        others = jnp.concatenate(gather_planes(share), axis=0)
        parts, owners = links.gathered(others)
        sources, cuts = list(parts), []
        for value, at in own_plane:
            sources.append(value)
            cuts.append((len(sources) - 1, 0, value.shape[0], plane * plane_rows + at))
        for number, owner in enumerate(owners):
            for step in range(1, planes):
                start = (plane + planes - step) % planes * plane_rows
                cuts.append((number, (step - 1) * rows, rows, start + owner * rows))
        return place_rows(sources, cuts, planes * plane_rows), others

    def gather_halved(keep, send, after=()):
        recv = links.across(tied(send, *after) if after else send)
        rows = 2 * shard_rows // reps
        per = reps // 2
        share = lax.dynamic_slice_in_dim(
            jnp.where(q // per == core, keep, recv), q % per * rows, rows
        )
        own = [(keep, core * shard_rows), (recv, (1 - core) * shard_rows)]
        return gather_rows(share, own, 2 * shard_rows, after)

    small = jnp.concatenate([norm_attn, norm_ffn, bias_table.reshape(-1)])
    small_size = small.shape[0]
    small = jnp.pad(small, (0, -small_size % 128)).reshape(1, -1)
    small = lax.all_gather(small, "shard", axis=0, tiled=True)[:, :small_size]
    gain_one = small[:, :shard_rows].reshape(1, width).astype(jnp.float32)
    gain_two = small[:, shard_rows : 2 * shard_rows].reshape(1, width).astype(jnp.float32)
    full_table = small[:, 2 * shard_rows :].reshape(bucket_count, head_count)

    def column_half(side):
        return jnp.concatenate(
            [w[:, side * half : (side + 1) * half] for w in (w_query, w_key, w_value)], axis=1
        )

    half_zero, half_one = column_half(0), column_half(1)
    qkv_half, qkv_seen = gather_halved(
        by_core(half_zero, half_one), by_core(half_one, half_zero)
    )
    qkv_other = links.across(qkv_half)

    out_share = tied(w_out, qkv_seen)
    out_mine = jnp.concatenate([out_share] + gather_planes(out_share), axis=0)
    out_theirs = links.across(out_mine)
    out_rows = w_out.shape[0]
    f_out = place_rows(
        [out_mine, out_theirs],
        [
            (
                side,
                step * out_rows,
                out_rows,
                ((plane + planes - step) % planes * 2 + (core if side == 0 else 1 - core))
                * out_rows,
            )
            for side in (0, 1)
            for step in range(planes)
        ],
        inner,
    )

    f_gate, gate_seen = gather_halved(*split_columns(core, w_gate, piece, padded), (qkv_seen,))
    f_up, up_seen = gather_halved(*split_columns(core, w_up, piece, padded), (gate_seen,))
    down_rows = jnp.pad(w_down, ((0, padded - piece), (0, 0)))
    down_share = lax.dynamic_slice_in_dim(down_rows, q * (padded // reps), padded // reps)
    f_down, down_seen = gather_rows(down_share, [(down_rows, 0)], padded, (up_seen,))

    positions = lax.broadcasted_iota(jnp.int32, (bucket_count, buckets.shape[0]), 0)
    one_hot = (buckets[None, :] == positions).astype(jnp.float32)
    rel_bias = lax.dot_general(
        full_table.astype(jnp.float32),
        one_hot,
        (((0,), (0,)), ((), ())),
        precision=lax.Precision.HIGHEST,
    )
    bias_rows = jnp.pad(rel_bias[:, ::-1], ((0, 0), (0, 1))).reshape(head_count // 2, 2, -1)

    floats_in = tokens.astype(jnp.float32)
    scale_one = lax.rsqrt(jnp.mean(floats_in * floats_in, axis=-1, keepdims=True) + EPSILON)
    normed_one = (floats_in * scale_one * gain_one).astype(jnp.bfloat16)
    own_qkv = nn(normed_one, qkv_half).astype(jnp.bfloat16)
    other_qkv = nn(normed_one, qkv_other).astype(jnp.bfloat16)
    qkv = jnp.stack([by_core(own_qkv, other_qkv), by_core(other_qkv, own_qkv)])
    context, lse = run_forward(lengths, bias_rows, qkv, head_size)
    attended = floats_in + nn(context, f_out)
    scale_two = lax.rsqrt(jnp.mean(attended * attended, axis=-1, keepdims=True) + EPSILON)
    unit_two = attended * scale_two
    normed_two = (unit_two * gain_two).astype(jnp.bfloat16)

    both = jnp.concatenate([normed_two, links.across(normed_two)], axis=0)
    both_up = jnp.concatenate([cotangent, links.across(cotangent)], axis=0)
    gate_pre = nn(both, f_gate)
    up_pre = nn(both, f_up)
    gelu_out, gelu_pull = jax.vjp(lambda v: jax.nn.gelu(v, approximate=True), gate_pre)
    hidden = (gelu_out * up_pre).astype(jnp.bfloat16)
    gate_slope = gelu_pull(up_pre)[0].astype(jnp.bfloat16)
    up_slope = gelu_out.astype(jnp.bfloat16)
    ffn_out = nn(hidden, f_down)
    ffn_theirs = links.across(ffn_out[length:].astype(jnp.bfloat16))
    output = (attended + ffn_out[:length] + ffn_theirs.astype(jnp.float32)).astype(jnp.bfloat16)

    columns = width // reps
    up_slots = links.in_slots(both_up)
    down_parts = links.scattered(
        lambda first, last: tn(hidden, up_slots[:, first * columns : last * columns]), 1, padded
    )
    grad_down = jnp.concatenate(down_parts, axis=1)[:piece].astype(jnp.float32)

    owners = links.slot_owners()
    share_rows = 2 * shard_rows // reps
    inside = jnp.arange(share_rows, dtype=jnp.int32)
    order = jnp.concatenate(
        [p * 2 * shard_rows + owner * share_rows + inside for owner in owners for p in range(planes)]
    )
    ordering = (lax.broadcasted_iota(jnp.int32, (width, width), 0) == order[None, :]).astype(
        jnp.bfloat16
    )
    slot_rows = width // reps

    def width_scattered(left, right):
        return links.scattered(
            lambda first, last: nn(left[first * slot_rows : last * slot_rows], right),
            0,
            share_rows,
        )

    def own_rows(parts):
        per = reps // 2
        low = jnp.concatenate(parts[:per], axis=0)
        high = jnp.concatenate(parts[per:], axis=0)
        return by_core(low, high), links.across(by_core(high, low))

    d_hidden = nt(both_up, f_down)
    d_gate = (d_hidden * gate_slope.astype(jnp.float32)).astype(jnp.bfloat16)
    d_up = (d_hidden * up_slope.astype(jnp.float32)).astype(jnp.bfloat16)
    both_turned = nt(ordering.T, both).astype(jnp.bfloat16)
    gate_parts = own_rows(width_scattered(both_turned, d_gate))
    up_parts = own_rows(width_scattered(both_turned, d_up))
    grad_gate = join_columns(core, *gate_parts, piece, padded)
    grad_up = join_columns(core, *up_parts, piece, padded)
    d_both = nt(d_gate, f_gate) + nt(d_up, f_up)
    d_theirs = links.across(d_both[length:].astype(jnp.bfloat16))
    d_normed_two = d_both[:length] + d_theirs.astype(jnp.float32)
    ffn_gain_term = jnp.sum(d_normed_two * unit_two, axis=0)
    grad_in = cotangent.astype(jnp.float32)
    d_attended = grad_in + norm_back(d_normed_two, unit_two, scale_two, gain_two)
    d_branch = d_attended.astype(jnp.bfloat16)

    out_term = tn(context, links.in_slots(d_branch)).astype(jnp.bfloat16)
    out_term = out_term.reshape(planes, 2, out_rows, width)
    out_keep = by_core(out_term[:, 0], out_term[:, 1]).reshape(planes * out_rows, width)
    out_send = by_core(out_term[:, 1], out_term[:, 0]).reshape(planes * out_rows, width)
    out_sum = out_keep.astype(jnp.float32) + links.across(
        links.from_other_core(out_send, 1)
    ).astype(jnp.float32)
    out_parts = links.scattered(
        lambda first, last: out_sum[:, first * columns : last * columns], 1, out_rows
    )
    grad_out = jnp.concatenate(out_parts, axis=1).astype(jnp.float32)

    d_context = nt(d_branch, f_out).astype(jnp.bfloat16)
    d_query, d_key, d_value, d_lined = run_backward(
        lengths, bias_rows, qkv, d_context, lse, head_size
    )
    d_qkv = jnp.concatenate([d_query, d_key, d_value], axis=2)
    d_own = by_core(d_qkv[0], d_qkv[1])
    d_other = by_core(d_qkv[1], d_qkv[0])
    one_turned = nt(ordering.T, normed_one).astype(jnp.bfloat16)
    qkv_theirs = links.across(
        links.from_other_core(nn(one_turned, d_other), 0).astype(jnp.bfloat16)
    )
    qkv_parts = links.scattered(
        lambda first, last: nn(one_turned[first * slot_rows : last * slot_rows], d_own)
        + qkv_theirs[first * slot_rows : last * slot_rows].astype(jnp.float32),
        0,
        share_rows,
    )
    qkv_mine, qkv_recv = own_rows(qkv_parts)
    grad_halves = (by_core(qkv_mine, qkv_recv), by_core(qkv_recv, qkv_mine))
    grad_query, grad_key, grad_value = [
        jnp.concatenate(
            [value[:, kind * half : (kind + 1) * half] for value in grad_halves], axis=1
        ).astype(jnp.float32)
        for kind in range(3)
    ]

    d_normed_one = nt(d_own, qkv_half) + nt(d_other, qkv_other)
    unit_one = floats_in * scale_one
    attn_gain_term = jnp.sum(d_normed_one * unit_one, axis=0)
    grad_tokens = (d_attended + norm_back(d_normed_one, unit_one, scale_one, gain_one)).astype(
        jnp.bfloat16
    )

    d_relative = d_lined.reshape(head_count, -1)[:, : buckets.shape[0]][:, ::-1]
    table_term = lax.dot_general(
        one_hot, d_relative, (((1,), (1,)), ((), ())), precision=lax.Precision.HIGHEST
    )
    terms = jnp.concatenate([attn_gain_term, ffn_gain_term, table_term.reshape(-1)])
    terms = jnp.pad(terms, (0, -terms.shape[0] % 1024)).reshape(-1, 128)
    terms = links.summed_everywhere(terms).reshape(-1)
    grad_norm_attn = lax.dynamic_slice_in_dim(terms, links.place * shard_rows, shard_rows)
    grad_norm_ffn = lax.dynamic_slice_in_dim(terms, width + links.place * shard_rows, shard_rows)
    table_size = bias_table.size
    grad_table = lax.dynamic_slice_in_dim(
        terms, 2 * width + links.place * table_size, table_size
    ).reshape(bias_table.shape)
    return (
        output,
        grad_tokens,
        grad_query,
        grad_key,
        grad_value,
        grad_out,
        grad_gate,
        grad_up,
        grad_down,
        grad_table,
        grad_norm_attn,
        grad_norm_ffn,
    )


def solution(mesh):
    rows, group = P("shard", None), P("shard")
    tokens = P(("rep", "shard"), None)
    return jax.shard_map(
        functools.partial(layer, mesh.shape["rep"], mesh.shape["shard"]),
        mesh=mesh,
        in_specs=(tokens, P(AXES), P()) + (rows,) * 8 + (group, group, tokens),
        out_specs=(tokens, tokens) + (rows,) * 8 + (group, group),
        check_vma=False,
    )
```

```python
import functools

import jax
import jax.numpy as jnp
from jax import lax
from jax.experimental import pallas as pl
from jax.experimental.pallas import tpu as pltpu
from jax.sharding import PartitionSpec as P

NEG_FILL = -1000000000.0
VMEM_LIMIT = 56 * 1024 * 1024
TOEP = 128
COST_SHARE = 0.25


def cost(flops):
    flops = int(flops * COST_SHARE)
    return pl.CostEstimate(flops=flops, bytes_accessed=flops // 512, transcendentals=0)


def dot_nn(a, b):
    return lax.dot_general(a, b, (((1,), (0,)), ((), ())), preferred_element_type=jnp.float32)


def dot_nt(a, b):
    return lax.dot_general(a, b, (((1,), (1,)), ((), ())), preferred_element_type=jnp.float32)


def dot_tn(a, b):
    return lax.dot_general(a, b, (((0,), (0,)), ((), ())), preferred_element_type=jnp.float32)


def biased_scores(rows_k, rows_q, bias_row, valid, length):
    steps = length // TOEP
    raw = dot_nt(rows_k, rows_q)
    width = bias_row.shape[-1]
    spread = jnp.broadcast_to(bias_row, (TOEP, width))
    table = pltpu.roll(spread, width - (TOEP - 1), 1, stride=1, stride_axis=0)
    blocks = []
    for step in range(steps):
        start = TOEP * (steps - 1 - step)
        row_at = lax.broadcasted_iota(jnp.int32, (TOEP, length), 0) + step * TOEP
        mask = jnp.where(row_at < valid, 0.0, NEG_FILL)
        blocks.append(
            raw[step * TOEP : (step + 1) * TOEP] + table[:, start : start + length] + mask
        )
    return jnp.concatenate(blocks, axis=0)


def attention_forward(valid_ref, bias_ref, q_ref, k_ref, v_ref, ctx_ref, turned_ref, lse_ref, *, head_size):
    length = q_ref.shape[1]
    pair = q_ref.shape[2] // head_size
    q, k, v = q_ref[0], k_ref[0], v_ref[0]
    lane_head = lax.broadcasted_iota(jnp.int32, q.shape, 1) // head_size
    v_turned = v.T
    outs = []
    for head in range(pair):
        own_q = jnp.where(lane_head == head, q, jnp.zeros_like(q))
        scores = biased_scores(k, own_q, bias_ref[0, head : head + 1], valid_ref[0], length)
        top = jnp.max(scores, axis=0, keepdims=True)
        terms = jnp.exp(scores - top)
        total = jnp.sum(terms, axis=0, keepdims=True)
        probs = (terms * (1.0 / total)).astype(jnp.bfloat16)
        lse_ref[0, head : head + 1] = top + jnp.log(total)
        outs.append(dot_nn(v_turned, probs)[head * head_size : (head + 1) * head_size])
    turned = jnp.concatenate(outs, axis=0)
    turned_ref[...] = turned.astype(jnp.bfloat16)
    ctx_ref[...] = turned.T.astype(jnp.bfloat16)


def attention_backward(
    valid_ref, bias_ref, q_ref, k_ref, v_ref, dctx_ref, lse_ref, dq_ref, dk_ref, dv_ref, rel_ref, *, head_size
):
    length = q_ref.shape[1]
    pair = q_ref.shape[2] // head_size
    steps = length // TOEP
    q, k, v, dctx = q_ref[0], k_ref[0], v_ref[0], dctx_ref[...]
    lane_head = lax.broadcasted_iota(jnp.int32, q.shape, 1) // head_size
    k_turned = k.T
    width = bias_ref.shape[-1]
    flip = (
        lax.broadcasted_iota(jnp.int32, (TOEP, TOEP), 0)
        + lax.broadcasted_iota(jnp.int32, (TOEP, TOEP), 1)
        == TOEP - 1
    ).astype(jnp.bfloat16)
    dq_parts = []
    dk = dv = None
    for head in range(pair):
        mine = lane_head == head
        own_q = jnp.where(mine, q, jnp.zeros_like(q))
        own_d = jnp.where(mine, dctx, jnp.zeros_like(dctx))
        scores = biased_scores(k, own_q, bias_ref[0, head : head + 1], valid_ref[0], length)
        probs = jnp.exp(scores - lse_ref[0, head : head + 1])
        d_probs = dot_nt(v, own_d)
        inner = jnp.sum(d_probs * probs, axis=0, keepdims=True)
        d_scores = (probs * (d_probs - inner)).astype(jnp.bfloat16)
        part_v = dot_nn(probs.astype(jnp.bfloat16), own_d)
        part_k = dot_nn(d_scores, own_q)
        dv = part_v if dv is None else dv + part_v
        dk = part_k if dk is None else dk + part_k
        dq_parts.append(dot_nn(k_turned, d_scores)[head * head_size : (head + 1) * head_size])
        fold = None
        for step in range(steps):
            start = TOEP * (steps - 1 - step)
            turned = dot_nn(flip, d_scores[step * TOEP : (step + 1) * TOEP])
            pieces = []
            if start:
                pieces.append(jnp.zeros((TOEP, start), jnp.float32))
            pieces.append(turned)
            if width - start - length:
                pieces.append(jnp.zeros((TOEP, width - start - length), jnp.float32))
            padded = jnp.concatenate(pieces, axis=1)
            fold = padded if fold is None else fold + padded
        lined = pltpu.roll(fold, 0, 1, stride=1, stride_axis=0)
        rel_ref[0, head : head + 1] = jnp.sum(lined, axis=0, keepdims=True)
    dq_ref[0] = jnp.concatenate(dq_parts, axis=0).T.astype(jnp.bfloat16)
    dk_ref[0] = dk.astype(jnp.bfloat16)
    dv_ref[0] = dv.astype(jnp.bfloat16)


def run_forward(valid, bias_rows, qkv, head_size):
    halves, length, wide = qkv.shape
    half = wide // 3
    per = half // 128
    pairs = halves * per
    width = bias_rows.shape[-1]
    spec = lambda kind: pl.BlockSpec((1, length, 128), lambda p: (p // per, 0, kind * per + p % per))
    return pl.pallas_call(
        functools.partial(attention_forward, head_size=head_size),
        grid=(pairs,),
        in_specs=[
            pl.BlockSpec(memory_space=pltpu.SMEM),
            pl.BlockSpec((1, 2, width), lambda p: (p, 0, 0)),
            spec(0), spec(1), spec(2),
        ],
        out_specs=[
            pl.BlockSpec((length, 128), lambda p: (0, p)),
            pl.BlockSpec((128, length), lambda p: (p, 0)),
            pl.BlockSpec((1, 2, length), lambda p: (p, 0, 0)),
        ],
        out_shape=[
            jax.ShapeDtypeStruct((length, halves * half), jnp.bfloat16),
            jax.ShapeDtypeStruct((halves * half, length), jnp.bfloat16),
            jax.ShapeDtypeStruct((pairs, 2, length), jnp.float32),
        ],
        compiler_params=pltpu.CompilerParams(vmem_limit_bytes=VMEM_LIMIT),
        name="attend",
        cost_estimate=cost(8 * pairs * 2 * length * length * 128),
    )(valid, bias_rows, qkv, qkv, qkv)


def run_backward(valid, bias_rows, qkv, d_context, lse, head_size):
    halves, length, wide = qkv.shape
    half = wide // 3
    per = half // 128
    pairs = halves * per
    width = bias_rows.shape[-1]
    spec = lambda kind: pl.BlockSpec((1, length, 128), lambda p: (p // per, 0, kind * per + p % per))
    out_spec = pl.BlockSpec((1, length, 128), lambda p: (p // per, 0, p % per))
    grad = jax.ShapeDtypeStruct((halves, length, half), jnp.bfloat16)
    row = pl.BlockSpec((1, 2, width), lambda p: (p, 0, 0))
    return pl.pallas_call(
        functools.partial(attention_backward, head_size=head_size),
        grid=(pairs,),
        in_specs=[
            pl.BlockSpec(memory_space=pltpu.SMEM),
            row,
            spec(0), spec(1), spec(2),
            pl.BlockSpec((length, 128), lambda p: (0, p)),
            pl.BlockSpec((1, 2, length), lambda p: (p, 0, 0)),
        ],
        out_specs=[out_spec, out_spec, out_spec, row],
        out_shape=[grad, grad, grad, jax.ShapeDtypeStruct((pairs, 2, width), jnp.float32)],
        compiler_params=pltpu.CompilerParams(vmem_limit_bytes=VMEM_LIMIT),
        name="attend_back",
        cost_estimate=cost(16 * pairs * 2 * length * length * 128),
    )(valid, bias_rows, qkv, qkv, qkv, d_context, lse)


EPSILON = 1e-06
AXES = ("team", "wing", "plane", "core")


def split_kernel(at_ref, gate_ref, up_ref, keep_ref, send_ref, *, cuts, piece, padded):
    rows = gate_ref.shape[0]
    first_wing, first_core = at_ref[0] == 0, at_ref[1] == 0
    filler = jnp.zeros((rows, padded - piece), jnp.float32)
    for number, ref in enumerate((gate_ref, up_ref)):
        w = ref[...].astype(jnp.float32)
        for cut in range(cuts):
            sides = []
            for side in (0, 1):
                zero, one = [
                    w[:, (4 * cut + 2 * side + wing) * piece :][:, :piece] for wing in (0, 1)
                ]
                chosen = jnp.where(first_wing, zero, one)
                sides.append(jnp.concatenate([chosen, filler], axis=1).astype(jnp.bfloat16))
            start = (number * cuts + cut) * padded
            to = slice(start, start + padded)
            keep_ref[:, to] = jnp.where(first_core, sides[0], sides[1])
            send_ref[:, to] = jnp.where(first_core, sides[1], sides[0])


def split_columns(at, w_gate, w_up, piece, padded):
    rows, wide = w_gate.shape
    cuts = wide // (4 * piece)
    out = jax.ShapeDtypeStruct((rows, 2 * cuts * padded), jnp.bfloat16)
    whole = pl.BlockSpec(memory_space=pltpu.VMEM)
    return pl.pallas_call(
        functools.partial(split_kernel, cuts=cuts, piece=piece, padded=padded),
        in_specs=[pl.BlockSpec(memory_space=pltpu.SMEM), whole, whole],
        out_specs=[whole, whole],
        out_shape=[out, out],
        compiler_params=pltpu.CompilerParams(vmem_limit_bytes=VMEM_LIMIT),
        name="split",
        cost_estimate=cost(512 * w_gate.size),
    )(at, w_gate, w_up)


def join_kernel(core_ref, mine_ref, other_ref, gate_ref, up_ref, *, cuts, piece, padded):
    rows = gate_ref.shape[0]
    first_core = core_ref[0] == 0
    for number, out_ref in enumerate((gate_ref, up_ref)):
        for cut in range(cuts):
            start = (number * cuts + cut) * padded
            at = slice(start, start + padded)
            for wing in (0, 1):
                of = slice(wing * rows, (wing + 1) * rows)
                mine, other = mine_ref[of, at], other_ref[of, at]
                for side in (0, 1):
                    value = jnp.where(first_core, *((mine, other) if side == 0 else (other, mine)))
                    to = (4 * cut + 2 * side + wing) * piece
                    out_ref[:, to : to + piece] = value.astype(jnp.float32)[:, :piece]


def join_columns(core, mine, other, piece, padded):
    rows = mine.shape[0] // 2
    cuts = mine.shape[1] // (2 * padded)
    out = jax.ShapeDtypeStruct((rows, 4 * cuts * piece), jnp.float32)
    whole = pl.BlockSpec(memory_space=pltpu.VMEM)
    return pl.pallas_call(
        functools.partial(join_kernel, cuts=cuts, piece=piece, padded=padded),
        in_specs=[pl.BlockSpec(memory_space=pltpu.SMEM), whole, whole],
        out_specs=[whole, whole],
        out_shape=[out, out],
        compiler_params=pltpu.CompilerParams(vmem_limit_bytes=VMEM_LIMIT),
        name="join",
        cost_estimate=cost(512 * mine.size),
    )(core[None], mine, other)


def turn_kernel(owners_ref, x_ref, out_ref, turned_ref, *, slots, rows):
    turned_ref[...] = x_ref[...].T
    for slot in range(slots):
        start = pl.multiple_of(owners_ref[slot] * rows, 16)
        out_ref[slot, 0] = turned_ref[pl.ds(start, rows)]


def turn(x, owners, planes):
    tokens, width = x.shape
    slots = len(owners)
    plane = width // planes
    rows = plane // slots
    if plane % 128 or rows % 16:
        blocks = x.T.reshape(planes, slots, rows, tokens)
        picked = [lax.dynamic_slice_in_dim(blocks, owner, 1, axis=1) for owner in owners]
        return jnp.concatenate(picked, axis=1).transpose(1, 0, 2, 3).reshape(width, tokens)
    return pl.pallas_call(
        functools.partial(turn_kernel, slots=slots, rows=rows),
        grid=(planes,),
        in_specs=[
            pl.BlockSpec(memory_space=pltpu.SMEM),
            pl.BlockSpec((tokens, plane), lambda p: (0, p)),
        ],
        out_specs=pl.BlockSpec((slots, 1, rows, tokens), lambda p: (0, p, 0, 0)),
        out_shape=jax.ShapeDtypeStruct((slots, planes, rows, tokens), x.dtype),
        scratch_shapes=[pltpu.VMEM((plane, tokens), x.dtype)],
        compiler_params=pltpu.CompilerParams(vmem_limit_bytes=VMEM_LIMIT),
        name="turn",
        cost_estimate=cost(512 * x.size),
    )(jnp.stack(owners), x).reshape(width, tokens)


def turn_team_kernel(*refs):
    out_ref = refs[-1]
    for number, ref in enumerate(refs[:-1]):
        rows = ref.shape[0]
        out_ref[:, number * rows : (number + 1) * rows] = ref[...].T


def turn_team(blocks):
    rows, width = blocks[0].shape
    tile = tile_of(width, 256)
    tokens = rows * len(blocks)
    return pl.pallas_call(
        turn_team_kernel,
        grid=(width // tile,),
        in_specs=[pl.BlockSpec((rows, tile), lambda j: (0, j))] * len(blocks),
        out_specs=pl.BlockSpec((tile, tokens), lambda j: (j, 0)),
        out_shape=jax.ShapeDtypeStruct((width, tokens), blocks[0].dtype),
        compiler_params=pltpu.CompilerParams(vmem_limit_bytes=VMEM_LIMIT),
        name="turn_team",
        cost_estimate=cost(512 * tokens * width),
    )(*blocks)


def place_kernel(at_ref, *refs, cuts, outs):
    sources, out_refs, sems = refs[: -1 - outs], refs[-1 - outs : -1], refs[-1]
    copies = []
    for number, (source, start, rows, of, column, wide) in enumerate(cuts):
        row_to = pl.multiple_of(at_ref[0, number], 16)
        column_to = pl.multiple_of(at_ref[1, number], 128)
        copies.append(
            pltpu.make_async_copy(
                sources[source].at[pl.ds(start, rows), pl.ds(column, wide)],
                out_refs[of].at[pl.ds(row_to, rows), pl.ds(column_to, wide)],
                sems.at[number],
            )
        )
    for copy in copies:
        copy.start()
    for copy in copies:
        copy.wait()


def place(sources, cuts, shapes):
    low = sources[0].dtype
    if any(cut[1] % 16 or cut[2] % 16 or cut[4] % 128 or cut[5] % 128 for cut in cuts):
        outs = [jnp.zeros(shape, low) for shape in shapes]
        for source, start, rows, of, column, wide, row_to, column_to in cuts:
            part = sources[source][start : start + rows, column : column + wide]
            outs[of] = lax.dynamic_update_slice(outs[of], part, (row_to, column_to))
        return outs
    places = jnp.stack(
        [jnp.stack([jnp.asarray(cut[k], jnp.int32) for cut in cuts]) for k in (6, 7)]
    )
    return pl.pallas_call(
        functools.partial(place_kernel, cuts=[cut[:6] for cut in cuts], outs=len(shapes)),
        in_specs=[pl.BlockSpec(memory_space=pltpu.SMEM)]
        + [pl.BlockSpec(memory_space=pl.ANY)] * len(sources),
        out_specs=[pl.BlockSpec(memory_space=pltpu.VMEM)] * len(shapes),
        out_shape=[jax.ShapeDtypeStruct(shape, low) for shape in shapes],
        scratch_shapes=[pltpu.SemaphoreType.DMA((len(cuts),))],
        compiler_params=pltpu.CompilerParams(vmem_limit_bytes=VMEM_LIMIT),
        name="place",
        cost_estimate=cost(512 * sum(a * b for a, b in shapes)),
    )(places, *sources)


def tile_of(size, most):
    for count in range(1, size // 128 + 1):
        if size % count == 0 and size // count % 128 == 0 and size // count <= most:
            return size // count
    return size


def product_kernel(*refs, pairs, across, kind):
    total = None
    for number in range(pairs):
        left, right = refs[2 * number][...], refs[2 * number + 1][...]
        term = dot_nt(left, right) if across else dot_nn(left, right)
        total = term if total is None else total + term
    outs = refs[2 * pairs :]
    if kind == "team":
        rows = outs[0].shape[0]
        outs[0][...] = total[:rows]
        outs[1][...] = total[rows : 2 * rows]
        outs[2][...] = total[2 * rows :].astype(jnp.bfloat16)
    else:
        outs[0][...] = total.astype(outs[0].dtype)


def product(lefts, rights, across=False, kind="low", most=256):
    rows = lefts[0].shape[0]
    wide = rights[0].shape[0 if across else 1]
    tile = tile_of(wide, most)
    operands, specs = [], []
    for left, right in zip(lefts, rights):
        depth = left.shape[1]
        operands += [left, right]
        specs.append(pl.BlockSpec((rows, depth), lambda j: (0, 0)))
        if across:
            specs.append(pl.BlockSpec((tile, depth), lambda j: (j, 0)))
        else:
            specs.append(pl.BlockSpec((depth, tile), lambda j: (0, j)))
    if kind == "team":
        shapes = [(rows // 4, jnp.float32), (rows // 4, jnp.float32), (rows // 2, jnp.bfloat16)]
    else:
        shapes = [(rows, jnp.bfloat16 if kind == "low" else jnp.float32)]
    outs = pl.pallas_call(
        functools.partial(product_kernel, pairs=len(lefts), across=across, kind=kind),
        grid=(wide // tile,),
        in_specs=specs,
        out_specs=[pl.BlockSpec((size, tile), lambda j: (0, j)) for size, _ in shapes],
        out_shape=[jax.ShapeDtypeStruct((size, wide), kept) for size, kept in shapes],
        compiler_params=pltpu.CompilerParams(vmem_limit_bytes=VMEM_LIMIT),
        name="product",
        cost_estimate=cost(2 * rows * depth * wide * len(lefts)),
    )(*operands)
    return outs if kind == "team" else outs[0]


def column_slot_kernel(at_ref, left_ref, *refs, count, added):
    left = left_ref[...]
    depth = left.shape[1] // count
    total = None
    for number in range(count):
        term = dot_nn(left[:, number * depth : (number + 1) * depth], refs[number][...])
        total = term if total is None else total + term
    for ref in refs[count : count + added]:
        total = total + ref[...].astype(jnp.float32)
    refs[-1][...] = total.astype(jnp.bfloat16)


def column_slots(left, blocks, owners, wide, added=()):
    rows = left.shape[0]
    if wide % 128:
        whole = jnp.concatenate(blocks, axis=0)
        value = jnp.concatenate(
            [nn(left, lax.dynamic_slice_in_dim(whole, owner * wide, wide, axis=1)) for owner in owners],
            axis=1,
        )
        for array, first in added:
            value = value + array[:, first * wide : (first + len(owners)) * wide].astype(jnp.float32)
        return value.astype(jnp.bfloat16)
    tile = tile_of(wide, 256)
    per = wide // tile
    return pl.pallas_call(
        functools.partial(column_slot_kernel, count=len(blocks), added=len(added)),
        grid_spec=pltpu.PrefetchScalarGridSpec(
            num_scalar_prefetch=1,
            grid=(len(owners) * per,),
            in_specs=[pl.BlockSpec(left.shape, lambda j, at: (0, 0))]
            + [
                pl.BlockSpec((block.shape[0], tile), lambda j, at: (0, at[j // per] * per + j % per))
                for block in blocks
            ]
            + [
                pl.BlockSpec((rows, tile), lambda j, at, first=first: (0, first * per + j))
                for _, first in added
            ],
            out_specs=pl.BlockSpec((rows, tile), lambda j, at: (0, j)),
        ),
        out_shape=jax.ShapeDtypeStruct((rows, len(owners) * wide), jnp.bfloat16),
        compiler_params=pltpu.CompilerParams(vmem_limit_bytes=VMEM_LIMIT),
        name="column_slots",
        cost_estimate=cost(2 * left.size * wide * len(owners)),
    )(jnp.stack(owners), left, *blocks, *[array for array, _ in added])


def packed_slot_kernel(row_ref, at_ref, turned_ref, grad_ref, context_ref, branch_ref, *refs):
    out_ref = refs[-1]
    first = dot_nn(turned_ref[...], grad_ref[...])
    second = dot_nn(context_ref[...], branch_ref[...])
    wide = first.shape[1]
    for ref in refs[:-1]:
        first = first + ref[:, :wide].astype(jnp.float32)
        second = second + ref[:, wide:].astype(jnp.float32)
    out_ref[:, :wide] = first.astype(jnp.bfloat16)
    out_ref[:, wide:] = second.astype(jnp.bfloat16)


def packed_slots(turned, grad, context, branch, slots, owners, reps, planes, added=()):
    rows = turned.shape[0] // reps
    columns = branch.shape[1] // reps
    fold = context.shape[0] // rows
    wide = grad.shape[1] + fold * columns
    if fold != 1 or columns % 128:
        outs = []
        for slot, owner in zip(slots, owners):
            first = nn(turned[slot * rows : (slot + 1) * rows], grad)
            second = nn(context, lax.dynamic_slice_in_dim(branch, owner * columns, columns, axis=1))
            outs.append(jnp.concatenate([first, folded(second, planes, fold)], axis=1))
        value = jnp.concatenate(outs, axis=0)
        for array, start in added:
            value = value + array[start * rows :][: value.shape[0]].astype(jnp.float32)
        return value.astype(jnp.bfloat16)
    block = lambda start: pl.BlockSpec((rows, wide), lambda i, row, at: (start + i, 0))
    return pl.pallas_call(
        packed_slot_kernel,
        grid_spec=pltpu.PrefetchScalarGridSpec(
            num_scalar_prefetch=2,
            grid=(len(slots),),
            in_specs=[
                pl.BlockSpec((rows, turned.shape[1]), lambda i, row, at: (row[i], 0)),
                pl.BlockSpec(grad.shape, lambda i, row, at: (0, 0)),
                pl.BlockSpec(context.shape, lambda i, row, at: (0, 0)),
                pl.BlockSpec((branch.shape[0], columns), lambda i, row, at: (0, at[i])),
            ]
            + [block(start) for _, start in added],
            out_specs=block(0),
        ),
        out_shape=jax.ShapeDtypeStruct((len(slots) * rows, wide), jnp.bfloat16),
        compiler_params=pltpu.CompilerParams(vmem_limit_bytes=VMEM_LIMIT),
        name="packed_slots",
        cost_estimate=cost(2 * len(slots) * rows * turned.shape[1] * wide),
    )(
        jnp.array(slots, jnp.int32),
        jnp.stack(owners),
        turned,
        grad,
        context,
        branch,
        *[array for array, _ in added],
    )


def folded(value, planes, fold):
    rows, wide = value.shape
    split = value.reshape(planes, fold, rows // (planes * fold), wide)
    return split.transpose(0, 2, 1, 3).reshape(rows // fold, fold * wide)


def unfolded(value, fold):
    rows, wide = value.shape
    return value.reshape(rows, fold, wide // fold).transpose(1, 0, 2).reshape(rows * fold, -1)


GELU_RATE = 0.7978845608028654
GELU_CUBE = 0.044715


def gated_kernel(*refs, count):
    gate_ref, up_ref, hidden_ref, turned_ref, gate_slope_ref, up_slope_ref = refs[count:]
    for number in range(count):
        x = refs[number][...]
        rows = x.shape[0]
        at = slice(number * rows, (number + 1) * rows)
        gate = dot_nn(x, gate_ref[...])
        up = dot_nn(x, up_ref[...])
        square = gate * gate
        bent = jnp.tanh(GELU_RATE * gate * (1.0 + GELU_CUBE * square))
        share = 0.5 * (1.0 + bent)
        gelu = gate * share
        slope = share + 0.5 * gate * (1.0 - bent * bent) * (
            GELU_RATE * (1.0 + 3.0 * GELU_CUBE * square)
        )
        hidden = (gelu * up).astype(jnp.bfloat16)
        hidden_ref[at] = hidden
        turned_ref[:, at] = hidden.T
        gate_slope_ref[at] = (slope * up).astype(jnp.bfloat16)
        up_slope_ref[at] = gelu.astype(jnp.bfloat16)


def gated(blocks, f_both):
    rows, depth = blocks[0].shape
    tokens = rows * len(blocks)
    wide = f_both.shape[1] // 2
    tile = tile_of(wide, 256)
    steps = wide // tile
    out = pl.BlockSpec((tokens, tile), lambda j: (0, j))
    kept = jax.ShapeDtypeStruct((tokens, wide), jnp.bfloat16)
    return pl.pallas_call(
        functools.partial(gated_kernel, count=len(blocks)),
        grid=(steps,),
        in_specs=[pl.BlockSpec((rows, depth), lambda j: (0, 0))] * len(blocks)
        + [
            pl.BlockSpec((depth, tile), lambda j: (0, j)),
            pl.BlockSpec((depth, tile), lambda j: (0, steps + j)),
        ],
        out_specs=[out, pl.BlockSpec((tile, tokens), lambda j: (j, 0)), out, out],
        out_shape=[kept, jax.ShapeDtypeStruct((wide, tokens), jnp.bfloat16), kept, kept],
        compiler_params=pltpu.CompilerParams(vmem_limit_bytes=VMEM_LIMIT),
        name="gated",
        cost_estimate=cost(4 * tokens * depth * wide),
    )(*blocks, f_both, f_both)


def gated_back_kernel(*refs, count):
    down_ref, gate_slope_ref, up_slope_ref, out_ref = refs[count:]
    for number in range(count):
        rows = refs[number].shape[0]
        at = slice(number * rows, (number + 1) * rows)
        d_hidden = dot_nt(refs[number][...], down_ref[...])
        out_ref[0, at] = (d_hidden * gate_slope_ref[at].astype(jnp.float32)).astype(jnp.bfloat16)
        out_ref[1, at] = (d_hidden * up_slope_ref[at].astype(jnp.float32)).astype(jnp.bfloat16)


def gated_back(blocks, f_down, gate_slope, up_slope):
    rows, depth = blocks[0].shape
    tokens = rows * len(blocks)
    wide = f_down.shape[0]
    tile = tile_of(wide, 256)
    column = pl.BlockSpec((tokens, tile), lambda j: (0, j))
    return pl.pallas_call(
        functools.partial(gated_back_kernel, count=len(blocks)),
        grid=(wide // tile,),
        in_specs=[pl.BlockSpec((rows, depth), lambda j: (0, 0))] * len(blocks)
        + [pl.BlockSpec((tile, depth), lambda j: (j, 0)), column, column],
        out_specs=pl.BlockSpec((2, tokens, tile), lambda j: (0, 0, j)),
        out_shape=jax.ShapeDtypeStruct((2, tokens, wide), jnp.bfloat16),
        compiler_params=pltpu.CompilerParams(vmem_limit_bytes=VMEM_LIMIT),
        name="gated_back",
        cost_estimate=cost(2 * tokens * depth * wide),
    )(*blocks, f_down, gate_slope, up_slope)


def pair_grad_kernel(left_ref, right_ref, out_ref):
    out_ref[...] = dot_nn(left_ref[...], right_ref[0]).astype(jnp.bfloat16)


def pair_grad(left, pair):
    rows, depth = left.shape
    wide = pair.shape[2]
    tile = tile_of(wide, 256)
    steps = wide // tile
    return pl.pallas_call(
        pair_grad_kernel,
        grid=(2 * steps,),
        in_specs=[
            pl.BlockSpec((rows, depth), lambda j: (0, 0)),
            pl.BlockSpec((1, depth, tile), lambda j: (j // steps, 0, j % steps)),
        ],
        out_specs=pl.BlockSpec((rows, tile), lambda j: (0, j)),
        out_shape=jax.ShapeDtypeStruct((rows, 2 * wide), jnp.bfloat16),
        compiler_params=pltpu.CompilerParams(vmem_limit_bytes=VMEM_LIMIT),
        name="pair_grad",
        cost_estimate=cost(4 * rows * depth * wide),
    )(left, pair)


def pair_back_kernel(pair_ref, right_ref, own_ref, side_ref, sent_ref):
    wide = pair_ref.shape[2]
    rows = own_ref.shape[0]
    right = right_ref[...]
    total = dot_nt(pair_ref[0], right[:, :wide]) + dot_nt(pair_ref[1], right[:, wide:])
    own_ref[...] = total[:rows]
    side_ref[...] = total[rows : 2 * rows]
    sent_ref[...] = total[2 * rows :].astype(jnp.bfloat16)


def pair_back(pair, f_both):
    tokens, wide = pair.shape[1:]
    width = f_both.shape[0]
    tile = tile_of(width, 256)
    shapes = [(tokens // 4, jnp.float32), (tokens // 4, jnp.float32), (tokens // 2, jnp.bfloat16)]
    return pl.pallas_call(
        pair_back_kernel,
        grid=(width // tile,),
        in_specs=[
            pl.BlockSpec(pair.shape, lambda j: (0, 0, 0), pipeline_mode=pl.Buffered(1)),
            pl.BlockSpec((tile, 2 * wide), lambda j: (j, 0)),
        ],
        out_specs=[pl.BlockSpec((size, tile), lambda j: (0, j)) for size, _ in shapes],
        out_shape=[jax.ShapeDtypeStruct((size, width), kept) for size, kept in shapes],
        compiler_params=pltpu.CompilerParams(vmem_limit_bytes=VMEM_LIMIT),
        name="pair_back",
        cost_estimate=cost(4 * tokens * wide * width),
    )(pair, f_both)


def norm_back(upstream, unit_rows, scale_rows, gain_rows):
    scaled = upstream * gain_rows
    return scale_rows * (scaled - unit_rows * jnp.mean(scaled * unit_rows, axis=-1, keepdims=True))


def tied(value, *after):
    return lax.optimization_barrier((value, *after))[0]


class Order:
    def __init__(self):
        self.last = ()

    def __call__(self, value, *after):
        return tied(value, *self.last, *after) if self.last or after else value

    def mark(self, value):
        self.last = (value,)
        return value


class Links:
    def __init__(self, reps, group):
        self.reps, self.group, self.planes = reps, group, group // 2
        self.team, self.wing, self.plane, self.core = map(lax.axis_index, AXES)
        self.q = 2 * self.team + self.wing
        self.place = 2 * self.plane + self.core

    def move(self, value, target):
        pairs = []
        for r in range(self.reps):
            for s in range(self.group):
                to_r, to_s = target(r, s)
                pairs.append((r * self.group + s, to_r * self.group + to_s))
        return lax.ppermute(value, AXES, pairs)

    def across(self, value):
        return self.move(value, lambda r, s: (r, s ^ 1))

    def sideways(self, value):
        return self.move(value, lambda r, s: (r ^ 1, s))

    def along(self, value, step):
        return self.move(value, lambda r, s: (r, (s + 2 * step) % self.group))

    def along_parts(self, value, rows):
        parts = [lax.dynamic_slice_in_dim(value, self.plane * rows, rows)]
        for step in range(1, self.planes):
            to = (self.plane + step) % self.planes
            parts.append(self.along(lax.dynamic_slice_in_dim(value, to * rows, rows), step))
        return parts

    def along_steps(self, share):
        return [self.along(share, k) for k in range(1, self.planes)]

    def summed_everywhere(self, value):
        step = 1
        while step < self.reps:
            value = value + self.move(value, lambda r, s: (r ^ step, s))
            step *= 2
        step = 1
        while step < self.group:
            value = value + self.move(value, lambda r, s: (r, s ^ step))
            step *= 2
        return value


class Spread:
    def __init__(self, links, low):
        self.links, self.low = links, low
        self.count = links.reps >> low
        self.stages = self.count.bit_length() - 1
        self.own = links.q >> low

    def bit_of(self, stage, core):
        return 1 << (stage if core == 0 else self.stages - 1 - stage)

    def swap(self, value, stage):
        return self.links.move(
            value, lambda r, s: (r ^ (self.bit_of(stage, s % 2) << self.low), s)
        )

    def bit(self, stage):
        return jnp.where(self.links.core == 0, self.bit_of(stage, 0), self.bit_of(stage, 1))

    def gathered(self, value):
        parts, offsets = [value], [jnp.int32(0)]
        for stage in range(self.stages):
            parts += [self.swap(part, stage) for part in parts]
            offsets += [offset ^ self.bit(stage) for offset in offsets]
        return parts, [self.own ^ offset for offset in offsets]

    def turned_slot(self, slot):
        return sum(((slot >> k) & 1) << (self.stages - 1 - k) for k in range(self.stages))

    def slot_owners(self):
        owners = []
        for slot in range(self.count):
            owner = self.own
            for stage in range(self.stages):
                if (slot >> (self.stages - 1 - stage)) & 1:
                    owner = owner ^ self.bit(stage)
            owners.append(owner)
        return owners


def pick(blocks, index):
    value = blocks[0]
    for k in range(1, len(blocks)):
        value = jnp.where(index == k, blocks[k], value)
    return value


def in_order(parts, owners):
    ordered = []
    for k in range(len(parts)):
        value = parts[0]
        for part, owner in zip(parts[1:], owners[1:]):
            value = jnp.where(owner == k, part, value)
        ordered.append(value)
    return ordered


def nn(left, right):
    return jnp.dot(left, right, preferred_element_type=jnp.float32)


def layer(
    reps,
    group,
    tokens,
    lengths,
    buckets,
    w_query,
    w_key,
    w_value,
    w_out,
    w_gate,
    w_up,
    w_down,
    bias_table,
    norm_attn,
    norm_ffn,
    cotangent,
):
    links = Links(reps, group)
    planes, core, plane, wing, q = links.planes, links.core, links.plane, links.wing, links.q
    spread, team = Spread(links, 0), Spread(links, 1)
    first_core = core == 0
    length, width = tokens.shape
    shard_rows, inner = w_query.shape
    head_count = bias_table.shape[1]
    head_size = inner // head_count
    bucket_count = bias_table.shape[0] * group
    half = inner // 2
    piece = w_down.shape[0] // 2
    unit = max(128, 16 * team.count)
    padded = (piece + unit - 1) // unit * unit
    at = jnp.stack([wing, core])
    share_rows = 2 * shard_rows // reps
    team_rows = 2 * shard_rows // team.count
    down_rows = padded // team.count
    out_rows = w_out.shape[0]
    fold = out_rows // share_rows
    order = Order()
    mark = order.mark

    def by_core(zero, one):
        return jnp.where(first_core, zero, one)

    def row_share(over, keep, recv):
        rows = 2 * shard_rows // over.count
        per = max(over.count // 2, 1)
        return lax.dynamic_slice_in_dim(
            jnp.where(over.own // per == core, keep, recv), over.own % per * rows, rows
        )

    def plane_of(step):
        return (plane + planes - step) % planes

    def column_half(side):
        return jnp.concatenate(
            [w[:, side * half : (side + 1) * half] for w in (w_query, w_key, w_value)], axis=1
        )

    half_zero, half_one = column_half(0), column_half(1)
    qkv_keep, qkv_send = by_core(half_zero, half_one), by_core(half_one, half_zero)
    qkv_recv = links.across(mark(qkv_send))
    ffn_keep, ffn_send = split_columns(at, order(w_gate), w_up, piece, padded)
    ffn_recv = links.across(mark(ffn_send))
    columns = width // reps
    out_share = pick([w_out[:, k * columns : (k + 1) * columns] for k in range(reps)], q)
    out_share = folded(out_share, 1, fold)
    packed_share = jnp.concatenate(
        [row_share(spread, order(qkv_keep), qkv_recv), out_share], axis=1
    )
    packed_steps = links.along_steps(mark(packed_share))
    small = jnp.concatenate([norm_attn, norm_ffn, bias_table.reshape(-1)])
    small_size = small.shape[0]
    small = jnp.pad(small, (0, -small_size % 1024)).reshape(-1, 128)
    small = mark(order(small))
    small_steps = links.along_steps(small)

    floats_in = order(tokens).astype(jnp.float32)
    scale_one = mark(
        lax.rsqrt(jnp.mean(floats_in * floats_in, axis=-1, keepdims=True) + EPSILON)
    )
    down_half = jnp.pad(
        lax.dynamic_slice_in_dim(order(w_down), wing * piece, piece), ((0, padded - piece), (0, 0))
    )
    down_share = mark(lax.dynamic_slice_in_dim(down_half, team.own * down_rows, down_rows))
    positions = lax.broadcasted_iota(jnp.int32, (bucket_count, buckets.shape[0] + 1), 0)
    turned_buckets = jnp.concatenate([order(buckets)[::-1], jnp.full((1,), -1, jnp.int32)])
    one_hot = mark((turned_buckets[None, :] == positions).astype(jnp.float32))

    small = mark(jnp.stack([order(small)] + small_steps))
    small_recv = links.across(small)
    packed_others = mark(jnp.concatenate([order(packed_steps[0])] + packed_steps[1:], axis=0))
    packed_shares, packed_owners = spread.gathered(packed_others)
    ffn_share = mark(row_share(team, order(ffn_keep), ffn_recv))
    f_ffn = lax.all_gather(ffn_share, ("plane", "team"), axis=0, tiled=True)

    small = jnp.stack([order(small), small_recv])
    small = by_core(small, small[::-1])
    small = jnp.concatenate([small, small], axis=1)[:, ::-1]
    small = lax.dynamic_slice_in_dim(small, planes - 1 - plane, planes, axis=1)
    small = small.transpose(1, 0, 2, 3).reshape(group, -1)[:, :small_size]
    gain_one = small[:, :shard_rows].reshape(1, width).astype(jnp.float32)
    gain_two = small[:, shard_rows : 2 * shard_rows].reshape(1, width).astype(jnp.float32)
    full_table = small[:, 2 * shard_rows :].reshape(bucket_count, head_count)
    rel_bias = lax.dot_general(
        full_table.astype(jnp.float32),
        one_hot,
        (((0,), (0,)), ((), ())),
        precision=lax.Precision.HIGHEST,
    )
    bias_rows = mark(rel_bias.reshape(head_count // 2, 2, -1))
    normed_one = mark((order(floats_in) * scale_one * gain_one).astype(jnp.bfloat16))
    one_turned = mark(turn(normed_one, spread.slot_owners(), planes))

    wide = 3 * half
    cuts = [
        (0, 0, shard_rows, 0, 0, wide, (2 * plane + core) * shard_rows, 0),
        (1, 0, shard_rows, 0, 0, wide, (2 * plane + 1 - core) * shard_rows, 0),
        (2, 0, out_rows, 1, 0, width, plane * out_rows, 0),
    ]
    for number, owner in enumerate(packed_owners):
        for step in range(1, planes):
            start = (step - 1) * share_rows
            to = plane_of(step)
            row = to * 2 * shard_rows + owner * share_rows
            cuts.append((number + 3, start, share_rows, 0, 0, wide, row, 0))
            for k in range(fold):
                row = to * out_rows + k * share_rows
                cuts.append(
                    (
                        number + 3,
                        start,
                        share_rows,
                        1,
                        wide + k * columns,
                        columns,
                        row,
                        owner * columns,
                    )
                )
    qkv_half, out_mine = place(
        [order(qkv_keep), qkv_recv, w_out] + packed_shares,
        cuts,
        [(width, wide), (planes * out_rows, width)],
    )
    mark(qkv_half)
    qkv_other = links.across(qkv_half)
    out_theirs = links.across(out_mine)
    g_side = links.sideways(order(cotangent))
    own_qkv = mark(product([order(normed_one)], [qkv_half], most=384))
    other_qkv = mark(product([order(normed_one)], [qkv_other], most=384))
    qkv = mark(jnp.stack([by_core(order(own_qkv), other_qkv), by_core(other_qkv, own_qkv)]))
    context, context_turned, lse = run_forward(
        lengths, bias_rows, order(qkv, g_side), head_size
    )
    mark(context)
    (f_out,) = place(
        [order(out_mine), out_theirs],
        [
            (
                side,
                p * out_rows,
                out_rows,
                0,
                0,
                width,
                (2 * p + (core if side == 0 else 1 - core)) * out_rows,
                0,
            )
            for side in (0, 1)
            for p in range(planes)
        ],
        [(inner, width)],
    )
    attended = floats_in + nn(context, f_out)
    scale_two = lax.rsqrt(jnp.mean(attended * attended, axis=-1, keepdims=True) + EPSILON)
    unit_two = attended * scale_two
    normed_two = mark((unit_two * gain_two).astype(jnp.bfloat16))

    side_two = links.sideways(order(normed_two, g_side))
    core_two = links.across(normed_two)
    down_steps = links.along_steps(down_share)
    by_sides = context_turned.reshape(planes, 2, out_rows, length)
    context_own = by_core(order(by_sides)[:, 0], by_sides[:, 1]).reshape(-1, length)
    context_other = by_core(by_sides[:, 1], by_sides[:, 0]).reshape(-1, length)
    mark(context_own)
    g_core = links.across(order(cotangent))
    g_both = links.across(order(g_side))
    team_g = [cotangent, g_side, g_core, g_both]
    down_others = mark(jnp.concatenate([order(down_steps[0])] + down_steps[1:], axis=0))
    down_shares, down_owners = team.gathered(down_others)
    both_two = links.across(order(side_two))
    team_two = [normed_two, side_two, core_two, both_two]
    mark(order(both_two))
    hidden, hidden_turned, gate_slope, up_slope = gated([order(normed_two)] + team_two[1:], f_ffn)
    mark(hidden)

    cuts = [(0, 0, padded, 0, 0, width, plane * padded, 0)]
    for number, owner in enumerate(down_owners):
        for step in range(1, planes):
            row = plane_of(step) * padded + owner * down_rows
            cuts.append((number + 1, (step - 1) * down_rows, down_rows, 0, 0, width, row, 0))
    (f_down,) = place([order(down_half)] + down_shares, cuts, [(planes * padded, width)])
    mark(f_down)
    two_turned = mark(turn_team([order(normed_two)] + team_two[1:]))
    d_pair = mark(gated_back([order(cotangent)] + team_g[1:], f_down, gate_slope, up_slope))
    ffn_sum = lax.psum_scatter(
        mark(pair_grad(order(two_turned), d_pair)),
        ("plane", "team"),
        scatter_dimension=0,
        tiled=True,
    )
    d_own, d_side, d_sent = pair_back(order(d_pair), f_ffn)
    d_recv = links.across(mark(d_sent))

    team_owners = team.slot_owners()
    team_wide = width // team.count
    down_arrived = []

    def down_slots(low, high):
        return mark(
            column_slots(
                order(hidden_turned),
                team_g,
                team_owners[low:high],
                team_wide,
                [(value, low) for value in down_arrived],
            )
        )

    low, high = team.count // 2, team.count
    down_sent = down_slots(low, high)
    d_side = mark((order(d_side) + d_recv[length:].astype(jnp.float32)).astype(jnp.bfloat16))
    d_theirs = links.sideways(d_side)
    down_arrived.append(team.swap(order(down_sent), 0))
    ffn_own, ffn_side, ffn_sent = product([order(hidden)], [f_down], kind="team")
    ffn_their = links.across(mark(ffn_sent))
    ffn_side = mark((order(ffn_side) + ffn_their[length:].astype(jnp.float32)).astype(jnp.bfloat16))

    d_normed_two = (
        order(d_own) + d_recv[:length].astype(jnp.float32) + d_theirs.astype(jnp.float32)
    )
    ffn_theirs = links.sideways(order(ffn_side, d_theirs))
    ffn_gain_term = jnp.sum(d_normed_two * unit_two, axis=0)
    grad_in = cotangent.astype(jnp.float32)
    d_attended = grad_in + norm_back(d_normed_two, unit_two, scale_two, gain_two)
    d_branch = d_attended.astype(jnp.bfloat16)
    d_context = mark(product([d_branch], [f_out], across=True))

    d_query, d_key, d_value, d_lined = run_backward(
        lengths, bias_rows, qkv, order(d_context), lse, head_size
    )
    d_qkv = mark(jnp.concatenate([d_query, d_key, d_value], axis=2))
    d_mine = by_core(order(d_qkv)[0], d_qkv[1])
    d_other = by_core(d_qkv[1], d_qkv[0])
    owners = spread.slot_owners()

    def packed(slots, grad, context_rows, added):
        return mark(
            packed_slots(
                one_turned,
                order(grad),
                context_rows,
                d_branch,
                slots,
                [owners[slot] for slot in slots],
                reps,
                planes,
                added,
            )
        )

    output = mark(
        (
            order(attended)
            + ffn_own
            + ffn_their[:length].astype(jnp.float32)
            + ffn_theirs.astype(jnp.float32)
        ).astype(jnp.bfloat16)
    )
    for stage in range(1, team.stages):
        low, high = low // 2, low
        down_arrived.append(team.swap(down_slots(low, high), stage))
    down_parts = links.along_parts(down_slots(0, 1), padded)
    back = packed([spread.turned_slot(slot) for slot in range(reps)], d_other, context_other, [])
    arrived = [links.across(back)]
    mark(order(ffn_sum))
    packed_low, packed_high = reps // 2, reps
    sent = packed(
        range(packed_low, packed_high), d_mine, context_own, [(value, packed_low) for value in arrived]
    )
    arrived.append(spread.swap(sent, 0))
    ffn_shares = spread.gathered(order(ffn_sum))
    d_normed_one = product(
        [order(d_mine), d_other], [qkv_half, qkv_other], across=True, kind="wide"
    )
    unit_one = floats_in * scale_one
    attn_gain_term = jnp.sum(d_normed_one * unit_one, axis=0)
    grad_tokens = mark(
        (d_attended + norm_back(d_normed_one, unit_one, scale_one, gain_one)).astype(jnp.bfloat16)
    )
    table_term = lax.dot_general(
        one_hot,
        order(d_lined).reshape(head_count, -1),
        (((1,), (1,)), ((), ())),
        precision=lax.Precision.HIGHEST,
    )
    terms = jnp.concatenate([attn_gain_term, ffn_gain_term, table_term.reshape(-1)])
    terms = mark(jnp.pad(terms, (0, -terms.shape[0] % 1024)).reshape(-1, 128))
    for stage in range(1, spread.stages):
        packed_low, packed_high = packed_low // 2, packed_low
        sent = packed(
            range(packed_low, packed_high),
            d_mine,
            context_own,
            [(value, packed_low) for value in arrived],
        )
        arrived.append(spread.swap(sent, stage))
    down_total = sum(part.astype(jnp.float32) for part in [order(down_parts[0])] + down_parts[1:])
    down_total = mark(down_total.astype(jnp.bfloat16))
    down_shares = spread.gathered(down_total)
    sent = packed([0], d_mine, context_own, [(value, 0) for value in arrived])
    packed_parts = links.along_parts(sent, share_rows)
    packed_total = sum(part.astype(jnp.float32) for part in packed_parts).astype(jnp.bfloat16)

    parts = in_order(*down_shares)
    grad_down = jnp.concatenate(
        [jnp.concatenate(parts[w::2], axis=1)[:piece] for w in (0, 1)], axis=0
    ).astype(jnp.float32)
    terms = links.summed_everywhere(terms).reshape(-1)

    def by_owner(parts):
        per = len(parts) // 2
        low = jnp.concatenate(parts[:per], axis=0)
        high = jnp.concatenate(parts[per:], axis=0)
        return by_core(low, high), by_core(high, low)

    def wings_apart(parts):
        return parts[0::2] + parts[1::2]

    parts = in_order(*ffn_shares)
    per = reps // 2
    low, high = wings_apart(parts[:per]), wings_apart(parts[per:])
    low, high = jnp.concatenate(low, axis=0), jnp.concatenate(high, axis=0)
    ffn_mine, ffn_send = by_core(low, high), by_core(high, low)
    ffn_other = links.across(ffn_send)
    grad_gate, grad_up = join_columns(core, ffn_mine, ffn_other, piece, padded)

    parts = in_order(*spread.gathered(packed_total))
    grad_out = jnp.concatenate(
        [unfolded(part[:, wide:], fold) for part in parts], axis=1
    ).astype(jnp.float32)
    qkv_mine, qkv_send = by_owner([part[:, :wide] for part in parts])
    qkv_recv = links.across(qkv_send)
    grad_halves = (by_core(qkv_mine, qkv_recv), by_core(qkv_recv, qkv_mine))
    grad_query, grad_key, grad_value = [
        jnp.concatenate(
            [value[:, kind * half : (kind + 1) * half] for value in grad_halves], axis=1
        ).astype(jnp.float32)
        for kind in range(3)
    ]
    grad_norm_attn = lax.dynamic_slice_in_dim(terms, links.place * shard_rows, shard_rows)
    grad_norm_ffn = lax.dynamic_slice_in_dim(terms, width + links.place * shard_rows, shard_rows)
    table_size = bias_table.size
    grad_table = lax.dynamic_slice_in_dim(
        terms, 2 * width + links.place * table_size, table_size
    ).reshape(bias_table.shape)
    return (
        output,
        grad_tokens,
        grad_query,
        grad_key,
        grad_value,
        grad_out,
        grad_gate,
        grad_up,
        grad_down,
        grad_table,
        grad_norm_attn,
        grad_norm_ffn,
    )


def solution(mesh):
    reps, group = mesh.shape["rep"], mesh.shape["shard"]
    devices = mesh.devices.reshape(reps // 2, 2, group // 2, 2)
    rows, part = P(AXES[2:], None), P(AXES[2:])
    tokens = P(AXES, None)
    return jax.shard_map(
        functools.partial(layer, reps, group),
        mesh=jax.sharding.Mesh(devices, AXES),
        in_specs=(tokens, P(AXES), P()) + (rows,) * 8 + (part, part, tokens),
        out_specs=(tokens, tokens) + (rows,) * 8 + (part, part),
        check_vma=False,
    )
```

```python
import functools

import jax
import jax.numpy as jnp
from jax import lax
from jax.experimental import pallas as pl
from jax.experimental.pallas import tpu as pltpu
from jax.sharding import PartitionSpec as P

NEG_FILL = -1000000000.0
VMEM_LIMIT = 56 * 1024 * 1024
TOEP = 128
COST_SHARE = 1.0


def cost(flops):
    flops = int(flops * COST_SHARE)
    return pl.CostEstimate(flops=flops, bytes_accessed=flops // 512, transcendentals=0)


def dot_nn(a, b):
    return lax.dot_general(a, b, (((1,), (0,)), ((), ())), preferred_element_type=jnp.float32)


def dot_nt(a, b):
    return lax.dot_general(a, b, (((1,), (1,)), ((), ())), preferred_element_type=jnp.float32)


def dot_tn(a, b):
    return lax.dot_general(a, b, (((0,), (0,)), ((), ())), preferred_element_type=jnp.float32)


def biased_scores(rows_k, rows_q, bias_row, valid, length):
    steps = length // TOEP
    raw = dot_nt(rows_k, rows_q)
    width = bias_row.shape[-1]
    spread = jnp.broadcast_to(bias_row, (TOEP, width))
    table = pltpu.roll(spread, width - (TOEP - 1), 1, stride=1, stride_axis=0)
    blocks = []
    for step in range(steps):
        start = TOEP * (steps - 1 - step)
        row_at = lax.broadcasted_iota(jnp.int32, (TOEP, length), 0) + step * TOEP
        mask = jnp.where(row_at < valid, 0.0, NEG_FILL)
        blocks.append(
            raw[step * TOEP : (step + 1) * TOEP] + table[:, start : start + length] + mask
        )
    return jnp.concatenate(blocks, axis=0)


def attention_forward(valid_ref, bias_ref, q_ref, k_ref, v_ref, ctx_ref, turned_ref, lse_ref, *, head_size):
    length = q_ref.shape[1]
    pair = q_ref.shape[2] // head_size
    q, k, v = q_ref[0], k_ref[0], v_ref[0]
    lane_head = lax.broadcasted_iota(jnp.int32, q.shape, 1) // head_size
    v_turned = v.T
    outs = []
    for head in range(pair):
        own_q = jnp.where(lane_head == head, q, jnp.zeros_like(q))
        scores = biased_scores(k, own_q, bias_ref[0, head : head + 1], valid_ref[0], length)
        top = jnp.max(scores, axis=0, keepdims=True)
        terms = jnp.exp(scores - top)
        total = jnp.sum(terms, axis=0, keepdims=True)
        probs = (terms * (1.0 / total)).astype(jnp.bfloat16)
        lse_ref[0, head : head + 1] = top + jnp.log(total)
        outs.append(dot_nn(v_turned, probs)[head * head_size : (head + 1) * head_size])
    turned = jnp.concatenate(outs, axis=0)
    turned_ref[...] = turned.astype(jnp.bfloat16)
    ctx_ref[...] = turned.T.astype(jnp.bfloat16)


def attention_backward(
    valid_ref, bias_ref, q_ref, k_ref, v_ref, dctx_ref, lse_ref, dq_ref, dk_ref, dv_ref, rel_ref, *, head_size
):
    length = q_ref.shape[1]
    pair = q_ref.shape[2] // head_size
    steps = length // TOEP
    q, k, v, dctx = q_ref[0], k_ref[0], v_ref[0], dctx_ref[...]
    lane_head = lax.broadcasted_iota(jnp.int32, q.shape, 1) // head_size
    k_turned = k.T
    width = bias_ref.shape[-1]
    flip = (
        lax.broadcasted_iota(jnp.int32, (TOEP, TOEP), 0)
        + lax.broadcasted_iota(jnp.int32, (TOEP, TOEP), 1)
        == TOEP - 1
    ).astype(jnp.bfloat16)
    dq_parts = []
    dk = dv = None
    for head in range(pair):
        mine = lane_head == head
        own_q = jnp.where(mine, q, jnp.zeros_like(q))
        own_d = jnp.where(mine, dctx, jnp.zeros_like(dctx))
        scores = biased_scores(k, own_q, bias_ref[0, head : head + 1], valid_ref[0], length)
        probs = jnp.exp(scores - lse_ref[0, head : head + 1])
        d_probs = dot_nt(v, own_d)
        inner = jnp.sum(d_probs * probs, axis=0, keepdims=True)
        d_scores = (probs * (d_probs - inner)).astype(jnp.bfloat16)
        part_v = dot_nn(probs.astype(jnp.bfloat16), own_d)
        part_k = dot_nn(d_scores, own_q)
        dv = part_v if dv is None else dv + part_v
        dk = part_k if dk is None else dk + part_k
        dq_parts.append(dot_nn(k_turned, d_scores)[head * head_size : (head + 1) * head_size])
        fold = None
        for step in range(steps):
            start = TOEP * (steps - 1 - step)
            turned = dot_nn(flip, d_scores[step * TOEP : (step + 1) * TOEP])
            pieces = []
            if start:
                pieces.append(jnp.zeros((TOEP, start), jnp.float32))
            pieces.append(turned)
            if width - start - length:
                pieces.append(jnp.zeros((TOEP, width - start - length), jnp.float32))
            padded = jnp.concatenate(pieces, axis=1)
            fold = padded if fold is None else fold + padded
        lined = pltpu.roll(fold, 0, 1, stride=1, stride_axis=0)
        rel_ref[0, head : head + 1] = jnp.sum(lined, axis=0, keepdims=True)
    dq_ref[0] = jnp.concatenate(dq_parts, axis=0).T.astype(jnp.bfloat16)
    dk_ref[0] = dk.astype(jnp.bfloat16)
    dv_ref[0] = dv.astype(jnp.bfloat16)


def run_forward(valid, bias_rows, qkv, head_size):
    halves, length, wide = qkv.shape
    half = wide // 3
    per = half // 128
    pairs = halves * per
    width = bias_rows.shape[-1]
    spec = lambda kind: pl.BlockSpec((1, length, 128), lambda p: (p // per, 0, kind * per + p % per))
    return pl.pallas_call(
        functools.partial(attention_forward, head_size=head_size),
        grid=(pairs,),
        in_specs=[
            pl.BlockSpec(memory_space=pltpu.SMEM),
            pl.BlockSpec((1, 2, width), lambda p: (p, 0, 0)),
            spec(0), spec(1), spec(2),
        ],
        out_specs=[
            pl.BlockSpec((length, 128), lambda p: (0, p)),
            pl.BlockSpec((128, length), lambda p: (p, 0)),
            pl.BlockSpec((1, 2, length), lambda p: (p, 0, 0)),
        ],
        out_shape=[
            jax.ShapeDtypeStruct((length, halves * half), jnp.bfloat16),
            jax.ShapeDtypeStruct((halves * half, length), jnp.bfloat16),
            jax.ShapeDtypeStruct((pairs, 2, length), jnp.float32),
        ],
        compiler_params=pltpu.CompilerParams(vmem_limit_bytes=VMEM_LIMIT),
        name="attend",
        cost_estimate=cost(8 * pairs * 2 * length * length * 128),
    )(valid, bias_rows, qkv, qkv, qkv)


def run_backward(valid, bias_rows, qkv, d_context, lse, head_size):
    halves, length, wide = qkv.shape
    half = wide // 3
    per = half // 128
    pairs = halves * per
    width = bias_rows.shape[-1]
    spec = lambda kind: pl.BlockSpec((1, length, 128), lambda p: (p // per, 0, kind * per + p % per))
    out_spec = pl.BlockSpec((1, length, 128), lambda p: (p // per, 0, p % per))
    grad = jax.ShapeDtypeStruct((halves, length, half), jnp.bfloat16)
    row = pl.BlockSpec((1, 2, width), lambda p: (p, 0, 0))
    return pl.pallas_call(
        functools.partial(attention_backward, head_size=head_size),
        grid=(pairs,),
        in_specs=[
            pl.BlockSpec(memory_space=pltpu.SMEM),
            row,
            spec(0), spec(1), spec(2),
            pl.BlockSpec((length, 128), lambda p: (0, p)),
            pl.BlockSpec((1, 2, length), lambda p: (p, 0, 0)),
        ],
        out_specs=[out_spec, out_spec, out_spec, row],
        out_shape=[grad, grad, grad, jax.ShapeDtypeStruct((pairs, 2, width), jnp.float32)],
        compiler_params=pltpu.CompilerParams(vmem_limit_bytes=VMEM_LIMIT),
        name="attend_back",
        cost_estimate=cost(16 * pairs * 2 * length * length * 128),
    )(valid, bias_rows, qkv, qkv, qkv, d_context, lse)


EPSILON = 1e-06
AXES = ("team", "wing", "plane", "core")


def split_kernel(at_ref, gate_ref, up_ref, keep_ref, send_ref, *, cuts, piece, padded):
    rows = gate_ref.shape[0]
    first_wing, first_core = at_ref[0] == 0, at_ref[1] == 0
    filler = jnp.zeros((rows, padded - piece), jnp.float32)
    for number, ref in enumerate((gate_ref, up_ref)):
        w = ref[...].astype(jnp.float32)
        for cut in range(cuts):
            sides = []
            for side in (0, 1):
                zero, one = [
                    w[:, (4 * cut + 2 * side + wing) * piece :][:, :piece] for wing in (0, 1)
                ]
                chosen = jnp.where(first_wing, zero, one)
                sides.append(jnp.concatenate([chosen, filler], axis=1).astype(jnp.bfloat16))
            start = (number * cuts + cut) * padded
            to = slice(start, start + padded)
            keep_ref[:, to] = jnp.where(first_core, sides[0], sides[1])
            send_ref[:, to] = jnp.where(first_core, sides[1], sides[0])


def split_columns(at, w_gate, w_up, piece, padded):
    rows, wide = w_gate.shape
    cuts = wide // (4 * piece)
    out = jax.ShapeDtypeStruct((rows, 2 * cuts * padded), jnp.bfloat16)
    whole = pl.BlockSpec(memory_space=pltpu.VMEM)
    return pl.pallas_call(
        functools.partial(split_kernel, cuts=cuts, piece=piece, padded=padded),
        in_specs=[pl.BlockSpec(memory_space=pltpu.SMEM), whole, whole],
        out_specs=[whole, whole],
        out_shape=[out, out],
        compiler_params=pltpu.CompilerParams(vmem_limit_bytes=VMEM_LIMIT),
        name="split",
        cost_estimate=cost(512 * w_gate.size),
    )(at, w_gate, w_up)


def join_kernel(core_ref, mine_ref, other_ref, gate_ref, up_ref, *, cuts, piece, padded):
    rows = gate_ref.shape[0]
    first_core = core_ref[0] == 0
    for number, out_ref in enumerate((gate_ref, up_ref)):
        for cut in range(cuts):
            start = (number * cuts + cut) * padded
            at = slice(start, start + padded)
            for wing in (0, 1):
                of = slice(wing * rows, (wing + 1) * rows)
                mine, other = mine_ref[of, at], other_ref[of, at]
                for side in (0, 1):
                    value = jnp.where(first_core, *((mine, other) if side == 0 else (other, mine)))
                    to = (4 * cut + 2 * side + wing) * piece
                    out_ref[:, to : to + piece] = value.astype(jnp.float32)[:, :piece]


def join_columns(core, mine, other, piece, padded):
    rows = mine.shape[0] // 2
    cuts = mine.shape[1] // (2 * padded)
    out = jax.ShapeDtypeStruct((rows, 4 * cuts * piece), jnp.float32)
    whole = pl.BlockSpec(memory_space=pltpu.VMEM)
    return pl.pallas_call(
        functools.partial(join_kernel, cuts=cuts, piece=piece, padded=padded),
        in_specs=[pl.BlockSpec(memory_space=pltpu.SMEM), whole, whole],
        out_specs=[whole, whole],
        out_shape=[out, out],
        compiler_params=pltpu.CompilerParams(vmem_limit_bytes=VMEM_LIMIT),
        name="join",
        cost_estimate=cost(512 * mine.size),
    )(core[None], mine, other)


def turn_kernel(owners_ref, x_ref, out_ref, turned_ref, *, slots, rows):
    turned_ref[...] = x_ref[...].T
    for slot in range(slots):
        start = pl.multiple_of(owners_ref[slot] * rows, 16)
        out_ref[slot, 0] = turned_ref[pl.ds(start, rows)]


def turn(x, owners, planes):
    tokens, width = x.shape
    slots = len(owners)
    plane = width // planes
    rows = plane // slots
    if plane % 128 or rows % 16:
        blocks = x.T.reshape(planes, slots, rows, tokens)
        picked = [lax.dynamic_slice_in_dim(blocks, owner, 1, axis=1) for owner in owners]
        return jnp.concatenate(picked, axis=1).transpose(1, 0, 2, 3).reshape(width, tokens)
    return pl.pallas_call(
        functools.partial(turn_kernel, slots=slots, rows=rows),
        grid=(planes,),
        in_specs=[
            pl.BlockSpec(memory_space=pltpu.SMEM),
            pl.BlockSpec((tokens, plane), lambda p: (0, p)),
        ],
        out_specs=pl.BlockSpec((slots, 1, rows, tokens), lambda p: (0, p, 0, 0)),
        out_shape=jax.ShapeDtypeStruct((slots, planes, rows, tokens), x.dtype),
        scratch_shapes=[pltpu.VMEM((plane, tokens), x.dtype)],
        compiler_params=pltpu.CompilerParams(vmem_limit_bytes=VMEM_LIMIT),
        name="turn",
        cost_estimate=cost(512 * x.size),
    )(jnp.stack(owners), x).reshape(width, tokens)


def turn_team_kernel(*refs):
    out_ref = refs[-1]
    for number, ref in enumerate(refs[:-1]):
        rows = ref.shape[0]
        out_ref[:, number * rows : (number + 1) * rows] = ref[...].T


def turn_team(blocks):
    rows, width = blocks[0].shape
    tile = tile_of(width, 256)
    tokens = rows * len(blocks)
    return pl.pallas_call(
        turn_team_kernel,
        grid=(width // tile,),
        in_specs=[pl.BlockSpec((rows, tile), lambda j: (0, j))] * len(blocks),
        out_specs=pl.BlockSpec((tile, tokens), lambda j: (j, 0)),
        out_shape=jax.ShapeDtypeStruct((width, tokens), blocks[0].dtype),
        compiler_params=pltpu.CompilerParams(vmem_limit_bytes=VMEM_LIMIT),
        name="turn_team",
        cost_estimate=cost(512 * tokens * width),
    )(*blocks)


def place_kernel(at_ref, *refs, cuts, outs):
    sources, out_refs, sems = refs[: -1 - outs], refs[-1 - outs : -1], refs[-1]
    copies = []
    for number, (source, start, rows, of, column, wide) in enumerate(cuts):
        row_to = pl.multiple_of(at_ref[0, number], 16)
        column_to = pl.multiple_of(at_ref[1, number], 128)
        copies.append(
            pltpu.make_async_copy(
                sources[source].at[pl.ds(start, rows), pl.ds(column, wide)],
                out_refs[of].at[pl.ds(row_to, rows), pl.ds(column_to, wide)],
                sems.at[number],
            )
        )
    for copy in copies:
        copy.start()
    for copy in copies:
        copy.wait()


def place(sources, cuts, shapes):
    low = sources[0].dtype
    if any(cut[1] % 16 or cut[2] % 16 or cut[4] % 128 or cut[5] % 128 for cut in cuts):
        outs = [jnp.zeros(shape, low) for shape in shapes]
        for source, start, rows, of, column, wide, row_to, column_to in cuts:
            part = sources[source][start : start + rows, column : column + wide]
            outs[of] = lax.dynamic_update_slice(outs[of], part, (row_to, column_to))
        return outs
    places = jnp.stack(
        [jnp.stack([jnp.asarray(cut[k], jnp.int32) for cut in cuts]) for k in (6, 7)]
    )
    return pl.pallas_call(
        functools.partial(place_kernel, cuts=[cut[:6] for cut in cuts], outs=len(shapes)),
        in_specs=[pl.BlockSpec(memory_space=pltpu.SMEM)]
        + [pl.BlockSpec(memory_space=pl.ANY)] * len(sources),
        out_specs=[pl.BlockSpec(memory_space=pltpu.VMEM)] * len(shapes),
        out_shape=[jax.ShapeDtypeStruct(shape, low) for shape in shapes],
        scratch_shapes=[pltpu.SemaphoreType.DMA((len(cuts),))],
        compiler_params=pltpu.CompilerParams(vmem_limit_bytes=VMEM_LIMIT),
        name="place",
        cost_estimate=cost(512 * sum(a * b for a, b in shapes)),
    )(places, *sources)


def tile_of(size, most):
    for count in range(1, size // 128 + 1):
        if size % count == 0 and size // count % 128 == 0 and size // count <= most:
            return size // count
    return size


def product_kernel(*refs, pairs, across, kind):
    total = None
    for number in range(pairs):
        left, right = refs[2 * number][...], refs[2 * number + 1][...]
        term = dot_nt(left, right) if across else dot_nn(left, right)
        total = term if total is None else total + term
    outs = refs[2 * pairs :]
    if kind == "team":
        rows = outs[0].shape[0]
        outs[0][...] = total[:rows]
        outs[1][...] = total[rows : 2 * rows]
        outs[2][...] = total[2 * rows :].astype(jnp.bfloat16)
    else:
        outs[0][...] = total.astype(outs[0].dtype)


def product(lefts, rights, across=False, kind="low", most=256):
    rows = lefts[0].shape[0]
    wide = rights[0].shape[0 if across else 1]
    tile = tile_of(wide, most)
    operands, specs = [], []
    for left, right in zip(lefts, rights):
        depth = left.shape[1]
        operands += [left, right]
        specs.append(pl.BlockSpec((rows, depth), lambda j: (0, 0)))
        if across:
            specs.append(pl.BlockSpec((tile, depth), lambda j: (j, 0)))
        else:
            specs.append(pl.BlockSpec((depth, tile), lambda j: (0, j)))
    if kind == "team":
        shapes = [(rows // 4, jnp.float32), (rows // 4, jnp.float32), (rows // 2, jnp.bfloat16)]
    else:
        shapes = [(rows, jnp.bfloat16 if kind == "low" else jnp.float32)]
    outs = pl.pallas_call(
        functools.partial(product_kernel, pairs=len(lefts), across=across, kind=kind),
        grid=(wide // tile,),
        in_specs=specs,
        out_specs=[pl.BlockSpec((size, tile), lambda j: (0, j)) for size, _ in shapes],
        out_shape=[jax.ShapeDtypeStruct((size, wide), kept) for size, kept in shapes],
        compiler_params=pltpu.CompilerParams(vmem_limit_bytes=VMEM_LIMIT),
        name="product",
        cost_estimate=cost(2 * rows * depth * wide * len(lefts)),
    )(*operands)
    return outs if kind == "team" else outs[0]


def column_slot_kernel(at_ref, left_ref, *refs, count, added):
    left = left_ref[...]
    depth = left.shape[1] // count
    total = None
    for number in range(count):
        term = dot_nn(left[:, number * depth : (number + 1) * depth], refs[number][...])
        total = term if total is None else total + term
    for ref in refs[count : count + added]:
        total = total + ref[...].astype(jnp.float32)
    refs[-1][...] = total.astype(jnp.bfloat16)


def column_slots(left, blocks, owners, wide, added=()):
    rows = left.shape[0]
    if wide % 128:
        whole = jnp.concatenate(blocks, axis=0)
        value = jnp.concatenate(
            [nn(left, lax.dynamic_slice_in_dim(whole, owner * wide, wide, axis=1)) for owner in owners],
            axis=1,
        )
        for array, first in added:
            value = value + array[:, first * wide : (first + len(owners)) * wide].astype(jnp.float32)
        return value.astype(jnp.bfloat16)
    tile = tile_of(wide, 256)
    per = wide // tile
    return pl.pallas_call(
        functools.partial(column_slot_kernel, count=len(blocks), added=len(added)),
        grid_spec=pltpu.PrefetchScalarGridSpec(
            num_scalar_prefetch=1,
            grid=(len(owners) * per,),
            in_specs=[pl.BlockSpec(left.shape, lambda j, at: (0, 0))]
            + [
                pl.BlockSpec((block.shape[0], tile), lambda j, at: (0, at[j // per] * per + j % per))
                for block in blocks
            ]
            + [
                pl.BlockSpec((rows, tile), lambda j, at, first=first: (0, first * per + j))
                for _, first in added
            ],
            out_specs=pl.BlockSpec((rows, tile), lambda j, at: (0, j)),
        ),
        out_shape=jax.ShapeDtypeStruct((rows, len(owners) * wide), jnp.bfloat16),
        compiler_params=pltpu.CompilerParams(vmem_limit_bytes=VMEM_LIMIT),
        name="column_slots",
        cost_estimate=cost(2 * left.size * wide * len(owners)),
    )(jnp.stack(owners), left, *blocks, *[array for array, _ in added])


def packed_slot_kernel(row_ref, at_ref, turned_ref, grad_ref, context_ref, branch_ref, *refs):
    out_ref = refs[-1]
    first = dot_nn(turned_ref[...], grad_ref[...])
    second = dot_nn(context_ref[...], branch_ref[...])
    wide = first.shape[1]
    for ref in refs[:-1]:
        first = first + ref[:, :wide].astype(jnp.float32)
        second = second + ref[:, wide:].astype(jnp.float32)
    out_ref[:, :wide] = first.astype(jnp.bfloat16)
    out_ref[:, wide:] = second.astype(jnp.bfloat16)


def packed_slots(turned, grad, context, branch, slots, owners, reps, planes, added=()):
    rows = turned.shape[0] // reps
    columns = branch.shape[1] // reps
    fold = context.shape[0] // rows
    wide = grad.shape[1] + fold * columns
    if fold != 1 or columns % 128:
        outs = []
        for slot, owner in zip(slots, owners):
            first = nn(turned[slot * rows : (slot + 1) * rows], grad)
            second = nn(context, lax.dynamic_slice_in_dim(branch, owner * columns, columns, axis=1))
            outs.append(jnp.concatenate([first, folded(second, planes, fold)], axis=1))
        value = jnp.concatenate(outs, axis=0)
        for array, start in added:
            value = value + array[start * rows :][: value.shape[0]].astype(jnp.float32)
        return value.astype(jnp.bfloat16)
    block = lambda start: pl.BlockSpec((rows, wide), lambda i, row, at: (start + i, 0))
    return pl.pallas_call(
        packed_slot_kernel,
        grid_spec=pltpu.PrefetchScalarGridSpec(
            num_scalar_prefetch=2,
            grid=(len(slots),),
            in_specs=[
                pl.BlockSpec((rows, turned.shape[1]), lambda i, row, at: (row[i], 0)),
                pl.BlockSpec(grad.shape, lambda i, row, at: (0, 0)),
                pl.BlockSpec(context.shape, lambda i, row, at: (0, 0)),
                pl.BlockSpec((branch.shape[0], columns), lambda i, row, at: (0, at[i])),
            ]
            + [block(start) for _, start in added],
            out_specs=block(0),
        ),
        out_shape=jax.ShapeDtypeStruct((len(slots) * rows, wide), jnp.bfloat16),
        compiler_params=pltpu.CompilerParams(vmem_limit_bytes=VMEM_LIMIT),
        name="packed_slots",
        cost_estimate=cost(2 * len(slots) * rows * turned.shape[1] * wide),
    )(
        jnp.array(slots, jnp.int32),
        jnp.stack(owners),
        turned,
        grad,
        context,
        branch,
        *[array for array, _ in added],
    )


def folded(value, planes, fold):
    rows, wide = value.shape
    split = value.reshape(planes, fold, rows // (planes * fold), wide)
    return split.transpose(0, 2, 1, 3).reshape(rows // fold, fold * wide)


def unfolded(value, fold):
    rows, wide = value.shape
    return value.reshape(rows, fold, wide // fold).transpose(1, 0, 2).reshape(rows * fold, -1)


GELU_RATE = 0.7978845608028654
GELU_CUBE = 0.044715


def gated_kernel(*refs, count):
    gate_ref, up_ref, hidden_ref, turned_ref, gate_slope_ref, up_slope_ref = refs[count:]
    for number in range(count):
        x = refs[number][...]
        rows = x.shape[0]
        at = slice(number * rows, (number + 1) * rows)
        gate = dot_nn(x, gate_ref[...])
        up = dot_nn(x, up_ref[...])
        square = gate * gate
        bent = jnp.tanh(GELU_RATE * gate * (1.0 + GELU_CUBE * square))
        share = 0.5 * (1.0 + bent)
        gelu = gate * share
        slope = share + 0.5 * gate * (1.0 - bent * bent) * (
            GELU_RATE * (1.0 + 3.0 * GELU_CUBE * square)
        )
        hidden = (gelu * up).astype(jnp.bfloat16)
        hidden_ref[at] = hidden
        turned_ref[:, at] = hidden.T
        gate_slope_ref[at] = (slope * up).astype(jnp.bfloat16)
        up_slope_ref[at] = gelu.astype(jnp.bfloat16)


def gated(blocks, f_both):
    rows, depth = blocks[0].shape
    tokens = rows * len(blocks)
    wide = f_both.shape[1] // 2
    tile = tile_of(wide, 256)
    steps = wide // tile
    out = pl.BlockSpec((tokens, tile), lambda j: (0, j))
    kept = jax.ShapeDtypeStruct((tokens, wide), jnp.bfloat16)
    return pl.pallas_call(
        functools.partial(gated_kernel, count=len(blocks)),
        grid=(steps,),
        in_specs=[pl.BlockSpec((rows, depth), lambda j: (0, 0))] * len(blocks)
        + [
            pl.BlockSpec((depth, tile), lambda j: (0, j)),
            pl.BlockSpec((depth, tile), lambda j: (0, steps + j)),
        ],
        out_specs=[out, pl.BlockSpec((tile, tokens), lambda j: (j, 0)), out, out],
        out_shape=[kept, jax.ShapeDtypeStruct((wide, tokens), jnp.bfloat16), kept, kept],
        compiler_params=pltpu.CompilerParams(vmem_limit_bytes=VMEM_LIMIT),
        name="gated",
        cost_estimate=cost(4 * tokens * depth * wide),
    )(*blocks, f_both, f_both)


def gated_back_kernel(*refs, count):
    down_ref, gate_slope_ref, up_slope_ref, out_ref = refs[count:]
    for number in range(count):
        rows = refs[number].shape[0]
        at = slice(number * rows, (number + 1) * rows)
        d_hidden = dot_nt(refs[number][...], down_ref[...])
        out_ref[0, at] = (d_hidden * gate_slope_ref[at].astype(jnp.float32)).astype(jnp.bfloat16)
        out_ref[1, at] = (d_hidden * up_slope_ref[at].astype(jnp.float32)).astype(jnp.bfloat16)


def gated_back(blocks, f_down, gate_slope, up_slope):
    rows, depth = blocks[0].shape
    tokens = rows * len(blocks)
    wide = f_down.shape[0]
    tile = tile_of(wide, 256)
    column = pl.BlockSpec((tokens, tile), lambda j: (0, j))
    return pl.pallas_call(
        functools.partial(gated_back_kernel, count=len(blocks)),
        grid=(wide // tile,),
        in_specs=[pl.BlockSpec((rows, depth), lambda j: (0, 0))] * len(blocks)
        + [pl.BlockSpec((tile, depth), lambda j: (j, 0)), column, column],
        out_specs=pl.BlockSpec((2, tokens, tile), lambda j: (0, 0, j)),
        out_shape=jax.ShapeDtypeStruct((2, tokens, wide), jnp.bfloat16),
        compiler_params=pltpu.CompilerParams(vmem_limit_bytes=VMEM_LIMIT),
        name="gated_back",
        cost_estimate=cost(2 * tokens * depth * wide),
    )(*blocks, f_down, gate_slope, up_slope)


def pair_grad_kernel(left_ref, right_ref, out_ref):
    out_ref[...] = dot_nn(left_ref[...], right_ref[0]).astype(jnp.bfloat16)


def pair_grad(left, pair):
    rows, depth = left.shape
    wide = pair.shape[2]
    tile = tile_of(wide, 256)
    steps = wide // tile
    return pl.pallas_call(
        pair_grad_kernel,
        grid=(2 * steps,),
        in_specs=[
            pl.BlockSpec((rows, depth), lambda j: (0, 0)),
            pl.BlockSpec((1, depth, tile), lambda j: (j // steps, 0, j % steps)),
        ],
        out_specs=pl.BlockSpec((rows, tile), lambda j: (0, j)),
        out_shape=jax.ShapeDtypeStruct((rows, 2 * wide), jnp.bfloat16),
        compiler_params=pltpu.CompilerParams(vmem_limit_bytes=VMEM_LIMIT),
        name="pair_grad",
        cost_estimate=cost(4 * rows * depth * wide),
    )(left, pair)


def pair_back_kernel(pair_ref, right_ref, own_ref, side_ref, sent_ref):
    wide = pair_ref.shape[2]
    rows = own_ref.shape[0]
    right = right_ref[...]
    total = dot_nt(pair_ref[0], right[:, :wide]) + dot_nt(pair_ref[1], right[:, wide:])
    own_ref[...] = total[:rows]
    side_ref[...] = total[rows : 2 * rows]
    sent_ref[...] = total[2 * rows :].astype(jnp.bfloat16)


def pair_back(pair, f_both):
    tokens, wide = pair.shape[1:]
    width = f_both.shape[0]
    tile = tile_of(width, 256)
    shapes = [(tokens // 4, jnp.float32), (tokens // 4, jnp.float32), (tokens // 2, jnp.bfloat16)]
    return pl.pallas_call(
        pair_back_kernel,
        grid=(width // tile,),
        in_specs=[
            pl.BlockSpec(pair.shape, lambda j: (0, 0, 0), pipeline_mode=pl.Buffered(1)),
            pl.BlockSpec((tile, 2 * wide), lambda j: (j, 0)),
        ],
        out_specs=[pl.BlockSpec((size, tile), lambda j: (0, j)) for size, _ in shapes],
        out_shape=[jax.ShapeDtypeStruct((size, width), kept) for size, kept in shapes],
        compiler_params=pltpu.CompilerParams(vmem_limit_bytes=VMEM_LIMIT),
        name="pair_back",
        cost_estimate=cost(4 * tokens * wide * width),
    )(pair, f_both)


def norm_back(upstream, unit_rows, scale_rows, gain_rows):
    scaled = upstream * gain_rows
    return scale_rows * (scaled - unit_rows * jnp.mean(scaled * unit_rows, axis=-1, keepdims=True))


def tied(value, *after):
    return lax.optimization_barrier((value, *after))[0]


class Order:
    def __init__(self):
        self.last = ()

    def __call__(self, value, *after):
        return tied(value, *self.last, *after) if self.last or after else value

    def mark(self, value):
        self.last = (value,)
        return value


class Links:
    def __init__(self, reps, group):
        self.reps, self.group, self.planes = reps, group, group // 2
        self.team, self.wing, self.plane, self.core = map(lax.axis_index, AXES)
        self.q = 2 * self.team + self.wing
        self.place = 2 * self.plane + self.core

    def move(self, value, target):
        pairs = []
        for r in range(self.reps):
            for s in range(self.group):
                to_r, to_s = target(r, s)
                pairs.append((r * self.group + s, to_r * self.group + to_s))
        return lax.ppermute(value, AXES, pairs)

    def across(self, value):
        return self.move(value, lambda r, s: (r, s ^ 1))

    def sideways(self, value):
        return self.move(value, lambda r, s: (r ^ 1, s))

    def along(self, value, step):
        return self.move(value, lambda r, s: (r, (s + 2 * step) % self.group))

    def along_parts(self, value, rows):
        parts = [lax.dynamic_slice_in_dim(value, self.plane * rows, rows)]
        for step in range(1, self.planes):
            to = (self.plane + step) % self.planes
            parts.append(self.along(lax.dynamic_slice_in_dim(value, to * rows, rows), step))
        return parts

    def along_steps(self, share):
        return [self.along(share, k) for k in range(1, self.planes)]

    def spread_steps(self):
        steps = [(0, 1 << k) for k in range(1, self.group.bit_length() - 1)]
        steps += [(1 << k, 0) for k in range(self.reps.bit_length() - 1)] + [(0, 1)]
        return [
            lambda value, r_step=r_step, s_step=s_step: self.move(
                value, lambda r, s: (r ^ r_step, s ^ s_step)
            )
            for r_step, s_step in steps
        ]


class Spread:
    def __init__(self, links, low):
        self.links, self.low = links, low
        self.count = links.reps >> low
        self.stages = self.count.bit_length() - 1
        self.own = links.q >> low

    def bit_of(self, stage, core):
        return 1 << (stage if core == 0 else self.stages - 1 - stage)

    def swap(self, value, stage):
        return self.links.move(
            value, lambda r, s: (r ^ (self.bit_of(stage, s % 2) << self.low), s)
        )

    def bit(self, stage):
        return jnp.where(self.links.core == 0, self.bit_of(stage, 0), self.bit_of(stage, 1))

    def gathered(self, value):
        parts, offsets = [value], [jnp.int32(0)]
        for stage in range(self.stages):
            parts += [self.swap(part, stage) for part in parts]
            offsets += [offset ^ self.bit(stage) for offset in offsets]
        return parts, [self.own ^ offset for offset in offsets]

    def gather_steps(self, value):
        parts, offsets = [value], [jnp.int32(0)]
        for stage in range(self.stages):
            added = [self.swap(part, stage) for part in parts]
            parts, offsets = parts + added, offsets + [offset ^ self.bit(stage) for offset in offsets]
            yield parts, [self.own ^ offset for offset in offsets]

    def turned_slot(self, slot):
        return sum(((slot >> k) & 1) << (self.stages - 1 - k) for k in range(self.stages))

    def slot_owners(self):
        owners = []
        for slot in range(self.count):
            owner = self.own
            for stage in range(self.stages):
                if (slot >> (self.stages - 1 - stage)) & 1:
                    owner = owner ^ self.bit(stage)
            owners.append(owner)
        return owners


def pick(blocks, index):
    value = blocks[0]
    for k in range(1, len(blocks)):
        value = jnp.where(index == k, blocks[k], value)
    return value


def in_order(first, parts, owners):
    parts = [parts[0] if first is None else first] + parts[1:]
    ordered = []
    for k in range(len(parts)):
        value = parts[0]
        for part, owner in zip(parts[1:], owners[1:]):
            value = jnp.where(owner == k, part, value)
        ordered.append(value)
    return ordered


def nn(left, right):
    return jnp.dot(left, right, preferred_element_type=jnp.float32)


def layer(
    reps,
    group,
    tokens,
    lengths,
    buckets,
    w_query,
    w_key,
    w_value,
    w_out,
    w_gate,
    w_up,
    w_down,
    bias_table,
    norm_attn,
    norm_ffn,
    cotangent,
):
    links = Links(reps, group)
    planes, core, plane, wing, q = links.planes, links.core, links.plane, links.wing, links.q
    spread, team = Spread(links, 0), Spread(links, 1)
    first_core = core == 0
    length, width = tokens.shape
    shard_rows, inner = w_query.shape
    head_count = bias_table.shape[1]
    head_size = inner // head_count
    bucket_count = bias_table.shape[0] * group
    half = inner // 2
    piece = w_down.shape[0] // 2
    unit = max(128, 16 * team.count)
    padded = (piece + unit - 1) // unit * unit
    at = jnp.stack([wing, core])
    share_rows = 2 * shard_rows // reps
    team_rows = 2 * shard_rows // team.count
    down_rows = padded // team.count
    out_rows = w_out.shape[0]
    fold = out_rows // share_rows
    order = Order()
    mark = order.mark

    def by_core(zero, one):
        return jnp.where(first_core, zero, one)

    def row_share(over, keep, recv):
        rows = 2 * shard_rows // over.count
        per = max(over.count // 2, 1)
        return lax.dynamic_slice_in_dim(
            jnp.where(over.own // per == core, keep, recv), over.own % per * rows, rows
        )

    def plane_of(step):
        return (plane + planes - step) % planes

    def column_half(side):
        return jnp.concatenate(
            [w[:, side * half : (side + 1) * half] for w in (w_query, w_key, w_value)], axis=1
        )

    half_zero, half_one = column_half(0), column_half(1)
    qkv_keep, qkv_send = by_core(half_zero, half_one), by_core(half_one, half_zero)
    qkv_recv = links.across(mark(qkv_send))
    ffn_keep, ffn_send = split_columns(at, order(w_gate), w_up, piece, padded)
    ffn_recv = links.across(mark(ffn_send))
    columns = width // reps
    out_share = pick([w_out[:, k * columns : (k + 1) * columns] for k in range(reps)], q)
    out_share = folded(out_share, 1, fold)
    packed_share = jnp.concatenate(
        [row_share(spread, order(qkv_keep), qkv_recv), out_share], axis=1
    )
    packed_steps = links.along_steps(mark(packed_share))
    small = jnp.concatenate([norm_attn, norm_ffn, bias_table.reshape(-1)])
    small_size = small.shape[0]
    small = jnp.pad(small, (0, -small_size % 1024)).reshape(-1, 128)
    small = mark(order(small))
    small_steps = links.along_steps(small)

    floats_in = order(tokens).astype(jnp.float32)
    scale_one = mark(
        lax.rsqrt(jnp.mean(floats_in * floats_in, axis=-1, keepdims=True) + EPSILON)
    )
    down_half = jnp.pad(
        lax.dynamic_slice_in_dim(order(w_down), wing * piece, piece), ((0, padded - piece), (0, 0))
    )
    down_share = mark(lax.dynamic_slice_in_dim(down_half, team.own * down_rows, down_rows))
    positions = lax.broadcasted_iota(jnp.int32, (bucket_count, buckets.shape[0] + 1), 0)
    turned_buckets = jnp.concatenate([order(buckets)[::-1], jnp.full((1,), -1, jnp.int32)])
    one_hot = mark((turned_buckets[None, :] == positions).astype(jnp.float32))

    small = mark(jnp.stack([order(small)] + small_steps))
    small_recv = links.across(small)
    packed_others = mark(jnp.concatenate([order(packed_steps[0])] + packed_steps[1:], axis=0))
    packed_shares, packed_owners = spread.gathered(packed_others)
    ffn_share = mark(row_share(team, order(ffn_keep), ffn_recv))
    f_ffn = lax.all_gather(ffn_share, ("plane", "team"), axis=0, tiled=True)
    f_down = lax.all_gather(
        tied(down_share, ffn_share), ("plane", "team"), axis=0, tiled=True
    )

    small = jnp.stack([order(small), small_recv])
    small = by_core(small, small[::-1])
    small = jnp.concatenate([small, small], axis=1)[:, ::-1]
    small = lax.dynamic_slice_in_dim(small, planes - 1 - plane, planes, axis=1)
    small = small.transpose(1, 0, 2, 3).reshape(group, -1)[:, :small_size]
    gain_one = small[:, :shard_rows].reshape(1, width).astype(jnp.float32)
    gain_two = small[:, shard_rows : 2 * shard_rows].reshape(1, width).astype(jnp.float32)
    full_table = small[:, 2 * shard_rows :].reshape(bucket_count, head_count)
    rel_bias = lax.dot_general(
        full_table.astype(jnp.float32),
        one_hot,
        (((0,), (0,)), ((), ())),
        precision=lax.Precision.HIGHEST,
    )
    bias_rows = mark(rel_bias.reshape(head_count // 2, 2, -1))
    normed_one = mark((order(floats_in) * scale_one * gain_one).astype(jnp.bfloat16))
    one_turned = mark(turn(normed_one, spread.slot_owners(), planes))

    wide = 3 * half
    cuts = [
        (0, 0, shard_rows, 0, 0, wide, (2 * plane + core) * shard_rows, 0),
        (1, 0, shard_rows, 0, 0, wide, (2 * plane + 1 - core) * shard_rows, 0),
        (2, 0, out_rows, 1, 0, width, plane * out_rows, 0),
    ]
    for number, owner in enumerate(packed_owners):
        for step in range(1, planes):
            start = (step - 1) * share_rows
            to = plane_of(step)
            row = to * 2 * shard_rows + owner * share_rows
            cuts.append((number + 3, start, share_rows, 0, 0, wide, row, 0))
            for k in range(fold):
                row = to * out_rows + k * share_rows
                cuts.append(
                    (
                        number + 3,
                        start,
                        share_rows,
                        1,
                        wide + k * columns,
                        columns,
                        row,
                        owner * columns,
                    )
                )
    qkv_half, out_mine = place(
        [order(qkv_keep), qkv_recv, w_out] + packed_shares,
        cuts,
        [(width, wide), (planes * out_rows, width)],
    )
    mark(qkv_half)
    qkv_other = links.across(qkv_half)
    out_theirs = links.across(out_mine)
    g_side = links.sideways(tied(cotangent, one_turned))
    own_qkv = mark(product([order(normed_one)], [qkv_half], most=384))
    other_qkv = mark(product([order(normed_one)], [qkv_other], most=384))
    qkv = mark(jnp.stack([by_core(order(own_qkv), other_qkv), by_core(other_qkv, own_qkv)]))
    context, context_turned, lse = run_forward(
        lengths, bias_rows, order(qkv), head_size
    )
    mark(context)
    (f_out,) = place(
        [order(out_mine), out_theirs],
        [
            (
                side,
                p * out_rows,
                out_rows,
                0,
                0,
                width,
                (2 * p + (core if side == 0 else 1 - core)) * out_rows,
                0,
            )
            for side in (0, 1)
            for p in range(planes)
        ],
        [(inner, width)],
    )
    attended = floats_in + nn(context, f_out)
    scale_two = lax.rsqrt(jnp.mean(attended * attended, axis=-1, keepdims=True) + EPSILON)
    unit_two = attended * scale_two
    normed_two = mark((unit_two * gain_two).astype(jnp.bfloat16))

    side_two = links.sideways(order(normed_two, g_side))
    core_two = links.across(normed_two)
    by_sides = context_turned.reshape(planes, 2, out_rows, length)
    context_own = by_core(order(by_sides)[:, 0], by_sides[:, 1]).reshape(-1, length)
    context_other = by_core(by_sides[:, 1], by_sides[:, 0]).reshape(-1, length)
    mark(context_own)
    g_core = links.across(order(cotangent))
    g_both = links.across(order(g_side))
    team_g = [cotangent, g_side, g_core, g_both]
    both_two = links.across(order(side_two))
    team_two = [normed_two, side_two, core_two, both_two]
    mark(order(both_two))
    hidden, hidden_turned, gate_slope, up_slope = gated([order(normed_two)] + team_two[1:], f_ffn)
    mark(hidden)

    two_turned = mark(turn_team([order(normed_two)] + team_two[1:]))
    d_pair = mark(gated_back([order(cotangent)] + team_g[1:], f_down, gate_slope, up_slope))
    d_own, d_side, d_sent = pair_back(order(d_pair), f_ffn)
    d_recv = links.across(mark(d_sent))

    d_side = mark((order(d_side) + d_recv[length:].astype(jnp.float32)).astype(jnp.bfloat16))
    d_theirs = links.sideways(d_side)
    ffn_sum = lax.psum_scatter(
        mark(pair_grad(order(two_turned), d_pair)),
        ("plane", "team"),
        scatter_dimension=0,
        tiled=True,
    )
    ffn_own, ffn_side, ffn_sent = product([order(hidden)], [f_down], kind="team")
    ffn_their = links.across(mark(ffn_sent))

    d_normed_two = (
        order(d_own) + d_recv[:length].astype(jnp.float32) + d_theirs.astype(jnp.float32)
    )
    ffn_gain_term = jnp.sum(d_normed_two * unit_two, axis=0)
    grad_in = cotangent.astype(jnp.float32)
    d_attended = grad_in + norm_back(d_normed_two, unit_two, scale_two, gain_two)
    d_branch = d_attended.astype(jnp.bfloat16)
    d_context = mark(product([d_branch], [f_out], across=True))
    ffn_side = mark((order(ffn_side) + ffn_their[length:].astype(jnp.float32)).astype(jnp.bfloat16))
    ffn_theirs = links.sideways(ffn_side)

    d_query, d_key, d_value, d_lined = run_backward(
        lengths, bias_rows, qkv, tied(d_context, ffn_side), lse, head_size
    )
    d_qkv = mark(jnp.concatenate([d_query, d_key, d_value], axis=2))
    d_mine = by_core(order(d_qkv)[0], d_qkv[1])
    d_other = by_core(d_qkv[1], d_qkv[0])
    owners = spread.slot_owners()
    d_normed_one = product(
        [order(d_mine), d_other], [qkv_half, qkv_other], across=True, kind="wide"
    )
    unit_one = floats_in * scale_one
    attn_gain_term = jnp.sum(d_normed_one * unit_one, axis=0)
    grad_tokens = mark(
        (d_attended + norm_back(d_normed_one, unit_one, scale_one, gain_one)).astype(jnp.bfloat16)
    )
    table_term = lax.dot_general(
        one_hot,
        order(d_lined).reshape(head_count, -1),
        (((1,), (1,)), ((), ())),
        precision=lax.Precision.HIGHEST,
    )
    terms = jnp.concatenate([attn_gain_term, ffn_gain_term, table_term.reshape(-1)])
    terms = mark(jnp.pad(terms, (0, -terms.shape[0] % 1024)).reshape(-1, 128))
    output = mark(
        (
            order(attended)
            + ffn_own
            + ffn_their[:length].astype(jnp.float32)
            + ffn_theirs.astype(jnp.float32)
        ).astype(jnp.bfloat16)
    )

    def packed(slots, grad, context_rows, added):
        return mark(
            packed_slots(
                one_turned,
                order(grad),
                context_rows,
                d_branch,
                slots,
                [owners[slot] for slot in slots],
                reps,
                planes,
                added,
            )
        )

    exchanges = links.spread_steps()

    back = packed([spread.turned_slot(slot) for slot in range(reps)], d_other, context_other, [])
    arrived = [links.across(back)]
    low, high = reps // 2, reps
    for stage in range(spread.stages):
        sent = packed(range(low, high), d_mine, context_own, [(value, low) for value in arrived])
        if stage:
            terms = mark(order(terms) + came)
        came = exchanges.pop(0)(terms)
        arrived.append(spread.swap(sent, stage))
        if stage == 0:
            down_sum = lax.psum_scatter(
                mark(
                    column_slots(
                        order(hidden_turned), team_g, [jnp.int32(k) for k in range(reps)], width // reps
                    )
                ),
                ("plane", "team"),
                scatter_dimension=0,
                tiled=True,
            )
            order.last = (*order.last, ffn_sum)
        low, high = low // 2, low
    sent = packed([0], d_mine, context_own, [(value, 0) for value in arrived])
    terms = mark(order(terms) + came)
    packed_parts = links.along_parts(sent, share_rows)
    ffn_steps = spread.gather_steps(order(ffn_sum))
    ffn_shares = next(ffn_steps)
    came = exchanges.pop(0)(terms)
    packed_total = mark(
        sum(
            part.astype(jnp.float32)
            for part in [order(packed_parts[0], ffn_shares[0][1])] + packed_parts[1:]
        ).astype(jnp.bfloat16)
    )
    packed_shares = spread.gathered(packed_total)
    for ffn_shares in ffn_steps:
        pass
    terms = tied(terms, packed_total) + came
    came = exchanges.pop(0)(terms)
    down_shares = spread.gathered(tied(down_sum, packed_shares[0][1]))
    terms = tied(terms, *packed_shares[0]) + came
    for exchange in exchanges:
        terms = terms + exchange(terms)
    terms = terms.reshape(-1)

    def by_owner(parts):
        per = len(parts) // 2
        low = jnp.concatenate(parts[:per], axis=0)
        high = jnp.concatenate(parts[per:], axis=0)
        return by_core(low, high), by_core(high, low)

    def wings_apart(parts):
        return parts[0::2] + parts[1::2]

    parts = in_order(None, *down_shares)
    grad_down = jnp.concatenate(
        [jnp.concatenate(parts[w::2], axis=0)[:piece] for w in (0, 1)], axis=0
    ).astype(jnp.float32)
    parts = in_order(None, *ffn_shares)
    per = reps // 2
    low, high = wings_apart(parts[:per]), wings_apart(parts[per:])
    low, high = jnp.concatenate(low, axis=0), jnp.concatenate(high, axis=0)
    ffn_mine, ffn_send = by_core(low, high), by_core(high, low)
    ffn_other = links.across(ffn_send)
    grad_gate, grad_up = join_columns(core, ffn_mine, ffn_other, piece, padded)

    parts = in_order(None, *packed_shares)
    grad_out = jnp.concatenate(
        [unfolded(part[:, wide:], fold) for part in parts], axis=1
    ).astype(jnp.float32)
    qkv_mine, qkv_send = by_owner([part[:, :wide] for part in parts])
    qkv_recv = links.across(qkv_send)
    grad_halves = (by_core(qkv_mine, qkv_recv), by_core(qkv_recv, qkv_mine))
    grad_query, grad_key, grad_value = [
        jnp.concatenate(
            [value[:, kind * half : (kind + 1) * half] for value in grad_halves], axis=1
        ).astype(jnp.float32)
        for kind in range(3)
    ]
    grad_norm_attn = lax.dynamic_slice_in_dim(terms, links.place * shard_rows, shard_rows)
    grad_norm_ffn = lax.dynamic_slice_in_dim(terms, width + links.place * shard_rows, shard_rows)
    table_size = bias_table.size
    grad_table = lax.dynamic_slice_in_dim(
        terms, 2 * width + links.place * table_size, table_size
    ).reshape(bias_table.shape)
    return (
        output,
        grad_tokens,
        grad_query,
        grad_key,
        grad_value,
        grad_out,
        grad_gate,
        grad_up,
        grad_down,
        grad_table,
        grad_norm_attn,
        grad_norm_ffn,
    )


def solution(mesh):
    reps, group = mesh.shape["rep"], mesh.shape["shard"]
    devices = mesh.devices.reshape(reps // 2, 2, group // 2, 2)
    rows, part = P(AXES[2:], None), P(AXES[2:])
    tokens = P(AXES, None)
    return jax.shard_map(
        functools.partial(layer, reps, group),
        mesh=jax.sharding.Mesh(devices, AXES),
        in_specs=(tokens, P(AXES), P()) + (rows,) * 8 + (part, part, tokens),
        out_specs=(tokens, tokens) + (rows,) * 8 + (part, part),
        check_vma=False,
    )
```

```python
import functools

import jax
import jax.numpy as jnp
from jax import lax
from jax.experimental import pallas as pl
from jax.experimental.pallas import tpu as pltpu
from jax.sharding import PartitionSpec as P

NEG_FILL = -1000000000.0
VMEM_LIMIT = 56 * 1024 * 1024
TOEP = 128
COST_SHARE = 1.0


def cost(flops):
    flops = int(flops * COST_SHARE)
    return pl.CostEstimate(flops=flops, bytes_accessed=flops // 512, transcendentals=0)


def dot_nn(a, b):
    return lax.dot_general(a, b, (((1,), (0,)), ((), ())), preferred_element_type=jnp.float32)


def dot_nt(a, b):
    return lax.dot_general(a, b, (((1,), (1,)), ((), ())), preferred_element_type=jnp.float32)


def dot_tn(a, b):
    return lax.dot_general(a, b, (((0,), (0,)), ((), ())), preferred_element_type=jnp.float32)


def biased_scores(rows_k, rows_q, bias_row, valid, length):
    steps = length // TOEP
    raw = dot_nt(rows_k, rows_q)
    width = bias_row.shape[-1]
    spread = jnp.broadcast_to(bias_row, (TOEP, width))
    table = pltpu.roll(spread, width - (TOEP - 1), 1, stride=1, stride_axis=0)
    blocks = []
    for step in range(steps):
        start = TOEP * (steps - 1 - step)
        row_at = lax.broadcasted_iota(jnp.int32, (TOEP, length), 0) + step * TOEP
        mask = jnp.where(row_at < valid, 0.0, NEG_FILL)
        blocks.append(
            raw[step * TOEP : (step + 1) * TOEP] + table[:, start : start + length] + mask
        )
    return jnp.concatenate(blocks, axis=0)


def attention_forward(valid_ref, bias_ref, q_ref, k_ref, v_ref, ctx_ref, turned_ref, lse_ref, *, head_size):
    length = q_ref.shape[1]
    pair = q_ref.shape[2] // head_size
    q, k, v = q_ref[0], k_ref[0], v_ref[0]
    lane_head = lax.broadcasted_iota(jnp.int32, q.shape, 1) // head_size
    v_turned = v.T
    outs = []
    for head in range(pair):
        own_q = jnp.where(lane_head == head, q, jnp.zeros_like(q))
        scores = biased_scores(k, own_q, bias_ref[0, head : head + 1], valid_ref[0], length)
        top = jnp.max(scores, axis=0, keepdims=True)
        terms = jnp.exp(scores - top)
        total = jnp.sum(terms, axis=0, keepdims=True)
        probs = (terms * (1.0 / total)).astype(jnp.bfloat16)
        lse_ref[0, head : head + 1] = top + jnp.log(total)
        outs.append(dot_nn(v_turned, probs)[head * head_size : (head + 1) * head_size])
    turned = jnp.concatenate(outs, axis=0)
    turned_ref[...] = turned.astype(jnp.bfloat16)
    ctx_ref[...] = turned.T.astype(jnp.bfloat16)


def attention_backward(
    valid_ref, bias_ref, q_ref, k_ref, v_ref, dctx_ref, lse_ref, dq_ref, dk_ref, dv_ref, rel_ref, *, head_size
):
    length = q_ref.shape[1]
    pair = q_ref.shape[2] // head_size
    steps = length // TOEP
    q, k, v, dctx = q_ref[0], k_ref[0], v_ref[0], dctx_ref[...]
    lane_head = lax.broadcasted_iota(jnp.int32, q.shape, 1) // head_size
    k_turned = k.T
    width = bias_ref.shape[-1]
    flip = (
        lax.broadcasted_iota(jnp.int32, (TOEP, TOEP), 0)
        + lax.broadcasted_iota(jnp.int32, (TOEP, TOEP), 1)
        == TOEP - 1
    ).astype(jnp.bfloat16)
    dq_parts = []
    dk = dv = None
    for head in range(pair):
        mine = lane_head == head
        own_q = jnp.where(mine, q, jnp.zeros_like(q))
        own_d = jnp.where(mine, dctx, jnp.zeros_like(dctx))
        scores = biased_scores(k, own_q, bias_ref[0, head : head + 1], valid_ref[0], length)
        probs = jnp.exp(scores - lse_ref[0, head : head + 1])
        d_probs = dot_nt(v, own_d)
        inner = jnp.sum(d_probs * probs, axis=0, keepdims=True)
        d_scores = (probs * (d_probs - inner)).astype(jnp.bfloat16)
        part_v = dot_nn(probs.astype(jnp.bfloat16), own_d)
        part_k = dot_nn(d_scores, own_q)
        dv = part_v if dv is None else dv + part_v
        dk = part_k if dk is None else dk + part_k
        dq_parts.append(dot_nn(k_turned, d_scores)[head * head_size : (head + 1) * head_size])
        fold = None
        for step in range(steps):
            start = TOEP * (steps - 1 - step)
            turned = dot_nn(flip, d_scores[step * TOEP : (step + 1) * TOEP])
            pieces = []
            if start:
                pieces.append(jnp.zeros((TOEP, start), jnp.float32))
            pieces.append(turned)
            if width - start - length:
                pieces.append(jnp.zeros((TOEP, width - start - length), jnp.float32))
            padded = jnp.concatenate(pieces, axis=1)
            fold = padded if fold is None else fold + padded
        lined = pltpu.roll(fold, 0, 1, stride=1, stride_axis=0)
        rel_ref[0, head : head + 1] = jnp.sum(lined, axis=0, keepdims=True)
    dq_ref[0] = jnp.concatenate(dq_parts, axis=0).T.astype(jnp.bfloat16)
    dk_ref[0] = dk.astype(jnp.bfloat16)
    dv_ref[0] = dv.astype(jnp.bfloat16)


def run_forward(valid, bias_rows, qkv, head_size):
    halves, length, wide = qkv.shape
    half = wide // 3
    per = half // 128
    pairs = halves * per
    width = bias_rows.shape[-1]
    spec = lambda kind: pl.BlockSpec((1, length, 128), lambda p: (p // per, 0, kind * per + p % per))
    return pl.pallas_call(
        functools.partial(attention_forward, head_size=head_size),
        grid=(pairs,),
        in_specs=[
            pl.BlockSpec(memory_space=pltpu.SMEM),
            pl.BlockSpec((1, 2, width), lambda p: (p, 0, 0)),
            spec(0), spec(1), spec(2),
        ],
        out_specs=[
            pl.BlockSpec((length, 128), lambda p: (0, p)),
            pl.BlockSpec((128, length), lambda p: (p, 0)),
            pl.BlockSpec((1, 2, length), lambda p: (p, 0, 0)),
        ],
        out_shape=[
            jax.ShapeDtypeStruct((length, halves * half), jnp.bfloat16),
            jax.ShapeDtypeStruct((halves * half, length), jnp.bfloat16),
            jax.ShapeDtypeStruct((pairs, 2, length), jnp.float32),
        ],
        compiler_params=pltpu.CompilerParams(vmem_limit_bytes=VMEM_LIMIT),
        name="attend",
        cost_estimate=cost(8 * pairs * 2 * length * length * 128),
    )(valid, bias_rows, qkv, qkv, qkv)


def run_backward(valid, bias_rows, qkv, d_context, lse, head_size):
    halves, length, wide = qkv.shape
    half = wide // 3
    per = half // 128
    pairs = halves * per
    width = bias_rows.shape[-1]
    spec = lambda kind: pl.BlockSpec((1, length, 128), lambda p: (p // per, 0, kind * per + p % per))
    out_spec = pl.BlockSpec((1, length, 128), lambda p: (p // per, 0, p % per))
    grad = jax.ShapeDtypeStruct((halves, length, half), jnp.bfloat16)
    row = pl.BlockSpec((1, 2, width), lambda p: (p, 0, 0))
    return pl.pallas_call(
        functools.partial(attention_backward, head_size=head_size),
        grid=(pairs,),
        in_specs=[
            pl.BlockSpec(memory_space=pltpu.SMEM),
            row,
            spec(0), spec(1), spec(2),
            pl.BlockSpec((length, 128), lambda p: (0, p)),
            pl.BlockSpec((1, 2, length), lambda p: (p, 0, 0)),
        ],
        out_specs=[out_spec, out_spec, out_spec, row],
        out_shape=[grad, grad, grad, jax.ShapeDtypeStruct((pairs, 2, width), jnp.float32)],
        compiler_params=pltpu.CompilerParams(vmem_limit_bytes=VMEM_LIMIT),
        name="attend_back",
        cost_estimate=cost(16 * pairs * 2 * length * length * 128),
    )(valid, bias_rows, qkv, qkv, qkv, d_context, lse)


EPSILON = 1e-06
AXES = ("team", "wing", "plane", "core")


def split_kernel(at_ref, gate_ref, up_ref, keep_ref, send_ref, *, cuts, piece, padded):
    rows = gate_ref.shape[0]
    first_wing, first_core = at_ref[0] == 0, at_ref[1] == 0
    filler = jnp.zeros((rows, padded - piece), jnp.float32)
    for number, ref in enumerate((gate_ref, up_ref)):
        w = ref[...].astype(jnp.float32)
        for cut in range(cuts):
            sides = []
            for side in (0, 1):
                zero, one = [
                    w[:, (4 * cut + 2 * side + wing) * piece :][:, :piece] for wing in (0, 1)
                ]
                chosen = jnp.where(first_wing, zero, one)
                sides.append(jnp.concatenate([chosen, filler], axis=1).astype(jnp.bfloat16))
            start = (number * cuts + cut) * padded
            to = slice(start, start + padded)
            keep_ref[:, to] = jnp.where(first_core, sides[0], sides[1])
            send_ref[:, to] = jnp.where(first_core, sides[1], sides[0])


def split_columns(at, w_gate, w_up, piece, padded):
    rows, wide = w_gate.shape
    cuts = wide // (4 * piece)
    out = jax.ShapeDtypeStruct((rows, 2 * cuts * padded), jnp.bfloat16)
    whole = pl.BlockSpec(memory_space=pltpu.VMEM)
    return pl.pallas_call(
        functools.partial(split_kernel, cuts=cuts, piece=piece, padded=padded),
        in_specs=[pl.BlockSpec(memory_space=pltpu.SMEM), whole, whole],
        out_specs=[whole, whole],
        out_shape=[out, out],
        compiler_params=pltpu.CompilerParams(vmem_limit_bytes=VMEM_LIMIT),
        name="split",
        cost_estimate=cost(512 * w_gate.size),
    )(at, w_gate, w_up)


def join_kernel(core_ref, mine_ref, other_ref, gate_ref, up_ref, *, cuts, piece, padded):
    rows = gate_ref.shape[0]
    first_core = core_ref[0] == 0
    for number, out_ref in enumerate((gate_ref, up_ref)):
        for cut in range(cuts):
            start = (number * cuts + cut) * padded
            at = slice(start, start + padded)
            for wing in (0, 1):
                of = slice(wing * rows, (wing + 1) * rows)
                mine, other = mine_ref[of, at], other_ref[of, at]
                for side in (0, 1):
                    value = jnp.where(first_core, *((mine, other) if side == 0 else (other, mine)))
                    to = (4 * cut + 2 * side + wing) * piece
                    out_ref[:, to : to + piece] = value.astype(jnp.float32)[:, :piece]


def join_columns(core, mine, other, piece, padded):
    rows = mine.shape[0] // 2
    cuts = mine.shape[1] // (2 * padded)
    out = jax.ShapeDtypeStruct((rows, 4 * cuts * piece), jnp.float32)
    whole = pl.BlockSpec(memory_space=pltpu.VMEM)
    return pl.pallas_call(
        functools.partial(join_kernel, cuts=cuts, piece=piece, padded=padded),
        in_specs=[pl.BlockSpec(memory_space=pltpu.SMEM), whole, whole],
        out_specs=[whole, whole],
        out_shape=[out, out],
        compiler_params=pltpu.CompilerParams(vmem_limit_bytes=VMEM_LIMIT),
        name="join",
        cost_estimate=cost(512 * mine.size),
    )(core[None], mine, other)


def turn_kernel(owners_ref, x_ref, out_ref, turned_ref, *, slots, rows):
    turned_ref[...] = x_ref[...].T
    for slot in range(slots):
        start = pl.multiple_of(owners_ref[slot] * rows, 16)
        out_ref[slot, 0] = turned_ref[pl.ds(start, rows)]


def turn(x, owners, planes):
    tokens, width = x.shape
    slots = len(owners)
    plane = width // planes
    rows = plane // slots
    if plane % 128 or rows % 16:
        blocks = x.T.reshape(planes, slots, rows, tokens)
        picked = [lax.dynamic_slice_in_dim(blocks, owner, 1, axis=1) for owner in owners]
        return jnp.concatenate(picked, axis=1).transpose(1, 0, 2, 3).reshape(width, tokens)
    return pl.pallas_call(
        functools.partial(turn_kernel, slots=slots, rows=rows),
        grid=(planes,),
        in_specs=[
            pl.BlockSpec(memory_space=pltpu.SMEM),
            pl.BlockSpec((tokens, plane), lambda p: (0, p)),
        ],
        out_specs=pl.BlockSpec((slots, 1, rows, tokens), lambda p: (0, p, 0, 0)),
        out_shape=jax.ShapeDtypeStruct((slots, planes, rows, tokens), x.dtype),
        scratch_shapes=[pltpu.VMEM((plane, tokens), x.dtype)],
        compiler_params=pltpu.CompilerParams(vmem_limit_bytes=VMEM_LIMIT),
        name="turn",
        cost_estimate=cost(512 * x.size),
    )(jnp.stack(owners), x).reshape(width, tokens)


def turn_team_kernel(*refs):
    out_ref = refs[-1]
    for number, ref in enumerate(refs[:-1]):
        rows = ref.shape[0]
        out_ref[:, number * rows : (number + 1) * rows] = ref[...].T


def turn_team(blocks):
    rows, width = blocks[0].shape
    tile = tile_of(width, 256)
    tokens = rows * len(blocks)
    return pl.pallas_call(
        turn_team_kernel,
        grid=(width // tile,),
        in_specs=[pl.BlockSpec((rows, tile), lambda j: (0, j))] * len(blocks),
        out_specs=pl.BlockSpec((tile, tokens), lambda j: (j, 0)),
        out_shape=jax.ShapeDtypeStruct((width, tokens), blocks[0].dtype),
        compiler_params=pltpu.CompilerParams(vmem_limit_bytes=VMEM_LIMIT),
        name="turn_team",
        cost_estimate=cost(512 * tokens * width),
    )(*blocks)


def place_kernel(at_ref, *refs, cuts, outs):
    sources, out_refs, sems = refs[: -1 - outs], refs[-1 - outs : -1], refs[-1]
    copies = []
    for number, (source, start, rows, of, column, wide) in enumerate(cuts):
        row_to = pl.multiple_of(at_ref[0, number], 16)
        column_to = pl.multiple_of(at_ref[1, number], 128)
        copies.append(
            pltpu.make_async_copy(
                sources[source].at[pl.ds(start, rows), pl.ds(column, wide)],
                out_refs[of].at[pl.ds(row_to, rows), pl.ds(column_to, wide)],
                sems.at[number],
            )
        )
    for copy in copies:
        copy.start()
    for copy in copies:
        copy.wait()


def place(sources, cuts, shapes):
    low = sources[0].dtype
    if any(cut[1] % 16 or cut[2] % 16 or cut[4] % 128 or cut[5] % 128 for cut in cuts):
        outs = [jnp.zeros(shape, low) for shape in shapes]
        for source, start, rows, of, column, wide, row_to, column_to in cuts:
            part = sources[source][start : start + rows, column : column + wide]
            outs[of] = lax.dynamic_update_slice(outs[of], part, (row_to, column_to))
        return outs
    places = jnp.stack(
        [jnp.stack([jnp.asarray(cut[k], jnp.int32) for cut in cuts]) for k in (6, 7)]
    )
    return pl.pallas_call(
        functools.partial(place_kernel, cuts=[cut[:6] for cut in cuts], outs=len(shapes)),
        in_specs=[pl.BlockSpec(memory_space=pltpu.SMEM)]
        + [pl.BlockSpec(memory_space=pl.ANY)] * len(sources),
        out_specs=[pl.BlockSpec(memory_space=pltpu.VMEM)] * len(shapes),
        out_shape=[jax.ShapeDtypeStruct(shape, low) for shape in shapes],
        scratch_shapes=[pltpu.SemaphoreType.DMA((len(cuts),))],
        compiler_params=pltpu.CompilerParams(vmem_limit_bytes=VMEM_LIMIT),
        name="place",
        cost_estimate=cost(512 * sum(a * b for a, b in shapes)),
    )(places, *sources)


def tile_of(size, most):
    for count in range(1, size // 128 + 1):
        if size % count == 0 and size // count % 128 == 0 and size // count <= most:
            return size // count
    return size


def product_kernel(*refs, pairs, across, kind):
    total = None
    for number in range(pairs):
        left, right = refs[2 * number][...], refs[2 * number + 1][...]
        term = dot_nt(left, right) if across else dot_nn(left, right)
        total = term if total is None else total + term
    outs = refs[2 * pairs :]
    if kind == "team":
        rows = outs[0].shape[0]
        outs[0][...] = total[:rows]
        outs[1][...] = total[rows : 2 * rows]
        outs[2][...] = total[2 * rows :].astype(jnp.bfloat16)
    else:
        outs[0][...] = total.astype(outs[0].dtype)


def product(lefts, rights, across=False, kind="low", most=256):
    rows = lefts[0].shape[0]
    wide = rights[0].shape[0 if across else 1]
    tile = tile_of(wide, most)
    operands, specs = [], []
    for left, right in zip(lefts, rights):
        depth = left.shape[1]
        operands += [left, right]
        specs.append(pl.BlockSpec((rows, depth), lambda j: (0, 0)))
        if across:
            specs.append(pl.BlockSpec((tile, depth), lambda j: (j, 0)))
        else:
            specs.append(pl.BlockSpec((depth, tile), lambda j: (0, j)))
    if kind == "team":
        shapes = [(rows // 4, jnp.float32), (rows // 4, jnp.float32), (rows // 2, jnp.bfloat16)]
    else:
        shapes = [(rows, jnp.bfloat16 if kind == "low" else jnp.float32)]
    outs = pl.pallas_call(
        functools.partial(product_kernel, pairs=len(lefts), across=across, kind=kind),
        grid=(wide // tile,),
        in_specs=specs,
        out_specs=[pl.BlockSpec((size, tile), lambda j: (0, j)) for size, _ in shapes],
        out_shape=[jax.ShapeDtypeStruct((size, wide), kept) for size, kept in shapes],
        compiler_params=pltpu.CompilerParams(vmem_limit_bytes=VMEM_LIMIT),
        name="product",
        cost_estimate=cost(2 * rows * depth * wide * len(lefts)),
    )(*operands)
    return outs if kind == "team" else outs[0]


def column_slot_kernel(at_ref, left_ref, *refs, count, added):
    left = left_ref[...]
    depth = left.shape[1] // count
    total = None
    for number in range(count):
        term = dot_nn(left[:, number * depth : (number + 1) * depth], refs[number][...])
        total = term if total is None else total + term
    for ref in refs[count : count + added]:
        total = total + ref[...].astype(jnp.float32)
    refs[-1][...] = total.astype(jnp.bfloat16)


def column_slots(left, blocks, owners, wide, added=()):
    rows = left.shape[0]
    if wide % 128:
        whole = jnp.concatenate(blocks, axis=0)
        value = jnp.concatenate(
            [nn(left, lax.dynamic_slice_in_dim(whole, owner * wide, wide, axis=1)) for owner in owners],
            axis=1,
        )
        for array, first in added:
            value = value + array[:, first * wide : (first + len(owners)) * wide].astype(jnp.float32)
        return value.astype(jnp.bfloat16)
    tile = tile_of(wide, 512)
    per = wide // tile
    return pl.pallas_call(
        functools.partial(column_slot_kernel, count=len(blocks), added=len(added)),
        grid_spec=pltpu.PrefetchScalarGridSpec(
            num_scalar_prefetch=1,
            grid=(len(owners) * per,),
            in_specs=[pl.BlockSpec(left.shape, lambda j, at: (0, 0))]
            + [
                pl.BlockSpec((block.shape[0], tile), lambda j, at: (0, at[j // per] * per + j % per))
                for block in blocks
            ]
            + [
                pl.BlockSpec((rows, tile), lambda j, at, first=first: (0, first * per + j))
                for _, first in added
            ],
            out_specs=pl.BlockSpec((rows, tile), lambda j, at: (0, j)),
        ),
        out_shape=jax.ShapeDtypeStruct((rows, len(owners) * wide), jnp.bfloat16),
        compiler_params=pltpu.CompilerParams(vmem_limit_bytes=VMEM_LIMIT),
        name="column_slots",
        cost_estimate=cost(2 * left.size * wide * len(owners)),
    )(jnp.stack(owners), left, *blocks, *[array for array, _ in added])


def packed_slot_kernel(row_ref, at_ref, turned_ref, grad_ref, context_ref, branch_ref, *refs):
    out_ref = refs[-1]
    first = dot_nn(turned_ref[...], grad_ref[...])
    second = dot_nn(context_ref[...], branch_ref[...])
    wide = first.shape[1]
    for ref in refs[:-1]:
        first = first + ref[:, :wide].astype(jnp.float32)
        second = second + ref[:, wide:].astype(jnp.float32)
    out_ref[:, :wide] = first.astype(jnp.bfloat16)
    out_ref[:, wide:] = second.astype(jnp.bfloat16)


def packed_slots(turned, grad, context, branch, slots, owners, reps, planes, added=()):
    rows = turned.shape[0] // reps
    columns = branch.shape[1] // reps
    fold = context.shape[0] // rows
    wide = grad.shape[1] + fold * columns
    if fold != 1 or columns % 128:
        outs = []
        for slot, owner in zip(slots, owners):
            first = nn(turned[slot * rows : (slot + 1) * rows], grad)
            second = nn(context, lax.dynamic_slice_in_dim(branch, owner * columns, columns, axis=1))
            outs.append(jnp.concatenate([first, folded(second, planes, fold)], axis=1))
        value = jnp.concatenate(outs, axis=0)
        for array, start in added:
            value = value + array[start * rows :][: value.shape[0]].astype(jnp.float32)
        return value.astype(jnp.bfloat16)
    block = lambda start: pl.BlockSpec((rows, wide), lambda i, row, at: (start + i, 0))
    return pl.pallas_call(
        packed_slot_kernel,
        grid_spec=pltpu.PrefetchScalarGridSpec(
            num_scalar_prefetch=2,
            grid=(len(slots),),
            in_specs=[
                pl.BlockSpec((rows, turned.shape[1]), lambda i, row, at: (row[i], 0)),
                pl.BlockSpec(grad.shape, lambda i, row, at: (0, 0)),
                pl.BlockSpec(context.shape, lambda i, row, at: (0, 0)),
                pl.BlockSpec((branch.shape[0], columns), lambda i, row, at: (0, at[i])),
            ]
            + [block(start) for _, start in added],
            out_specs=block(0),
        ),
        out_shape=jax.ShapeDtypeStruct((len(slots) * rows, wide), jnp.bfloat16),
        compiler_params=pltpu.CompilerParams(vmem_limit_bytes=VMEM_LIMIT),
        name="packed_slots",
        cost_estimate=cost(2 * len(slots) * rows * turned.shape[1] * wide),
    )(
        jnp.array(slots, jnp.int32),
        jnp.stack(owners),
        turned,
        grad,
        context,
        branch,
        *[array for array, _ in added],
    )


def folded(value, planes, fold):
    rows, wide = value.shape
    split = value.reshape(planes, fold, rows // (planes * fold), wide)
    return split.transpose(0, 2, 1, 3).reshape(rows // fold, fold * wide)


def unfolded(value, fold):
    rows, wide = value.shape
    return value.reshape(rows, fold, wide // fold).transpose(1, 0, 2).reshape(rows * fold, -1)


GELU_RATE = 0.7978845608028654
GELU_CUBE = 0.044715


def gated_kernel(*refs, count):
    gate_ref, up_ref, hidden_ref, turned_ref, gate_slope_ref, up_slope_ref = refs[count:]
    for number in range(count):
        x = refs[number][...]
        rows = x.shape[0]
        at = slice(number * rows, (number + 1) * rows)
        gate = dot_nn(x, gate_ref[...])
        up = dot_nn(x, up_ref[...])
        square = gate * gate
        bent = jnp.tanh(GELU_RATE * gate * (1.0 + GELU_CUBE * square))
        share = 0.5 * (1.0 + bent)
        gelu = gate * share
        slope = share + 0.5 * gate * (1.0 - bent * bent) * (
            GELU_RATE * (1.0 + 3.0 * GELU_CUBE * square)
        )
        hidden = (gelu * up).astype(jnp.bfloat16)
        hidden_ref[at] = hidden
        turned_ref[:, at] = hidden.T
        gate_slope_ref[at] = (slope * up).astype(jnp.bfloat16)
        up_slope_ref[at] = gelu.astype(jnp.bfloat16)


def gated(blocks, f_both):
    rows, depth = blocks[0].shape
    tokens = rows * len(blocks)
    wide = f_both.shape[1] // 2
    tile = tile_of(wide, 256)
    steps = wide // tile
    out = pl.BlockSpec((tokens, tile), lambda j: (0, j))
    kept = jax.ShapeDtypeStruct((tokens, wide), jnp.bfloat16)
    return pl.pallas_call(
        functools.partial(gated_kernel, count=len(blocks)),
        grid=(steps,),
        in_specs=[pl.BlockSpec((rows, depth), lambda j: (0, 0))] * len(blocks)
        + [
            pl.BlockSpec((depth, tile), lambda j: (0, j)),
            pl.BlockSpec((depth, tile), lambda j: (0, steps + j)),
        ],
        out_specs=[out, pl.BlockSpec((tile, tokens), lambda j: (j, 0)), out, out],
        out_shape=[kept, jax.ShapeDtypeStruct((wide, tokens), jnp.bfloat16), kept, kept],
        compiler_params=pltpu.CompilerParams(vmem_limit_bytes=VMEM_LIMIT),
        name="gated",
        cost_estimate=cost(4 * tokens * depth * wide),
    )(*blocks, f_both, f_both)


def gated_back_kernel(*refs, count):
    down_ref, gate_slope_ref, up_slope_ref, out_ref = refs[count:]
    for number in range(count):
        rows = refs[number].shape[0]
        at = slice(number * rows, (number + 1) * rows)
        d_hidden = dot_nt(refs[number][...], down_ref[...])
        out_ref[0, at] = (d_hidden * gate_slope_ref[at].astype(jnp.float32)).astype(jnp.bfloat16)
        out_ref[1, at] = (d_hidden * up_slope_ref[at].astype(jnp.float32)).astype(jnp.bfloat16)


def gated_back(blocks, f_down, gate_slope, up_slope):
    rows, depth = blocks[0].shape
    tokens = rows * len(blocks)
    wide = f_down.shape[0]
    tile = tile_of(wide, 512)
    column = pl.BlockSpec((tokens, tile), lambda j: (0, j))
    return pl.pallas_call(
        functools.partial(gated_back_kernel, count=len(blocks)),
        grid=(wide // tile,),
        in_specs=[pl.BlockSpec((rows, depth), lambda j: (0, 0))] * len(blocks)
        + [pl.BlockSpec((tile, depth), lambda j: (j, 0)), column, column],
        out_specs=pl.BlockSpec((2, tokens, tile), lambda j: (0, 0, j)),
        out_shape=jax.ShapeDtypeStruct((2, tokens, wide), jnp.bfloat16),
        compiler_params=pltpu.CompilerParams(vmem_limit_bytes=VMEM_LIMIT),
        name="gated_back",
        cost_estimate=cost(2 * tokens * depth * wide),
    )(*blocks, f_down, gate_slope, up_slope)


def pair_grad_kernel(left_ref, right_ref, out_ref):
    out_ref[...] = dot_nn(left_ref[...], right_ref[0]).astype(jnp.bfloat16)


def pair_grad(left, pair):
    rows, depth = left.shape
    wide = pair.shape[2]
    tile = tile_of(wide, 512)
    steps = wide // tile
    return pl.pallas_call(
        pair_grad_kernel,
        grid=(2 * steps,),
        in_specs=[
            pl.BlockSpec((rows, depth), lambda j: (0, 0)),
            pl.BlockSpec((1, depth, tile), lambda j: (j // steps, 0, j % steps)),
        ],
        out_specs=pl.BlockSpec((rows, tile), lambda j: (0, j)),
        out_shape=jax.ShapeDtypeStruct((rows, 2 * wide), jnp.bfloat16),
        compiler_params=pltpu.CompilerParams(vmem_limit_bytes=VMEM_LIMIT),
        name="pair_grad",
        cost_estimate=cost(4 * rows * depth * wide),
    )(left, pair)


def pair_back_kernel(pair_ref, right_ref, own_ref, side_ref, sent_ref):
    wide = pair_ref.shape[2]
    rows = own_ref.shape[0]
    right = right_ref[...]
    total = dot_nt(pair_ref[0], right[:, :wide]) + dot_nt(pair_ref[1], right[:, wide:])
    own_ref[...] = total[:rows]
    side_ref[...] = total[rows : 2 * rows]
    sent_ref[...] = total[2 * rows :].astype(jnp.bfloat16)


def pair_back(pair, f_both):
    tokens, wide = pair.shape[1:]
    width = f_both.shape[0]
    tile = tile_of(width, 512)
    shapes = [(tokens // 4, jnp.float32), (tokens // 4, jnp.float32), (tokens // 2, jnp.bfloat16)]
    return pl.pallas_call(
        pair_back_kernel,
        grid=(width // tile,),
        in_specs=[
            pl.BlockSpec(pair.shape, lambda j: (0, 0, 0), pipeline_mode=pl.Buffered(1)),
            pl.BlockSpec((tile, 2 * wide), lambda j: (j, 0)),
        ],
        out_specs=[pl.BlockSpec((size, tile), lambda j: (0, j)) for size, _ in shapes],
        out_shape=[jax.ShapeDtypeStruct((size, width), kept) for size, kept in shapes],
        compiler_params=pltpu.CompilerParams(vmem_limit_bytes=VMEM_LIMIT),
        name="pair_back",
        cost_estimate=cost(4 * tokens * wide * width),
    )(pair, f_both)


def norm_back(upstream, unit_rows, scale_rows, gain_rows):
    scaled = upstream * gain_rows
    return scale_rows * (scaled - unit_rows * jnp.mean(scaled * unit_rows, axis=-1, keepdims=True))


def tied(value, *after):
    return lax.optimization_barrier((value, *after))[0]


class Order:
    def __init__(self):
        self.last = ()

    def __call__(self, value, *after):
        return tied(value, *self.last, *after) if self.last or after else value

    def mark(self, value):
        self.last = (value,)
        return value


class Links:
    def __init__(self, reps, group):
        self.reps, self.group, self.planes = reps, group, group // 2
        self.team, self.wing, self.plane, self.core = map(lax.axis_index, AXES)
        self.q = 2 * self.team + self.wing
        self.place = 2 * self.plane + self.core

    def move(self, value, target):
        pairs = []
        for r in range(self.reps):
            for s in range(self.group):
                to_r, to_s = target(r, s)
                pairs.append((r * self.group + s, to_r * self.group + to_s))
        return lax.ppermute(value, AXES, pairs)

    def across(self, value):
        return self.move(value, lambda r, s: (r, s ^ 1))

    def sideways(self, value):
        return self.move(value, lambda r, s: (r ^ 1, s))

    def along(self, value, step):
        return self.move(value, lambda r, s: (r, (s + 2 * step) % self.group))

    def along_parts(self, value, rows):
        parts = [lax.dynamic_slice_in_dim(value, self.plane * rows, rows)]
        for step in range(1, self.planes):
            to = (self.plane + step) % self.planes
            parts.append(self.along(lax.dynamic_slice_in_dim(value, to * rows, rows), step))
        return parts

    def along_steps(self, share):
        return [self.along(share, k) for k in range(1, self.planes)]

    def spread_steps(self):
        steps = [(0, 1 << k) for k in range(self.group.bit_length() - 1)]
        steps += [(1 << k, 0) for k in range(self.reps.bit_length() - 1)]
        return [
            lambda value, r_step=r_step, s_step=s_step: self.move(
                value, lambda r, s: (r ^ r_step, s ^ s_step)
            )
            for r_step, s_step in steps
        ]


class Spread:
    def __init__(self, links, low):
        self.links, self.low = links, low
        self.count = links.reps >> low
        self.stages = self.count.bit_length() - 1
        self.own = links.q >> low

    def bit_of(self, stage, core):
        return 1 << (stage if core == 0 else self.stages - 1 - stage)

    def swap(self, value, stage):
        return self.links.move(
            value, lambda r, s: (r ^ (self.bit_of(stage, s % 2) << self.low), s)
        )

    def bit(self, stage):
        return jnp.where(self.links.core == 0, self.bit_of(stage, 0), self.bit_of(stage, 1))

    def gathered(self, value):
        parts, offsets = [value], [jnp.int32(0)]
        for stage in range(self.stages):
            parts += [self.swap(part, stage) for part in parts]
            offsets += [offset ^ self.bit(stage) for offset in offsets]
        return parts, [self.own ^ offset for offset in offsets]

    def gather_steps(self, value):
        parts, offsets = [value], [jnp.int32(0)]
        for stage in range(self.stages):
            added = [self.swap(part, stage) for part in parts]
            parts, offsets = parts + added, offsets + [offset ^ self.bit(stage) for offset in offsets]
            yield parts, [self.own ^ offset for offset in offsets]

    def turned_slot(self, slot):
        return sum(((slot >> k) & 1) << (self.stages - 1 - k) for k in range(self.stages))

    def slot_owners(self):
        owners = []
        for slot in range(self.count):
            owner = self.own
            for stage in range(self.stages):
                if (slot >> (self.stages - 1 - stage)) & 1:
                    owner = owner ^ self.bit(stage)
            owners.append(owner)
        return owners


def pick(blocks, index):
    value = blocks[0]
    for k in range(1, len(blocks)):
        value = jnp.where(index == k, blocks[k], value)
    return value


def in_order(first, parts, owners):
    parts = [parts[0] if first is None else first] + parts[1:]
    ordered = []
    for k in range(len(parts)):
        value = parts[0]
        for part, owner in zip(parts[1:], owners[1:]):
            value = jnp.where(owner == k, part, value)
        ordered.append(value)
    return ordered


def nn(left, right):
    return jnp.dot(left, right, preferred_element_type=jnp.float32)


def layer(
    reps,
    group,
    tokens,
    lengths,
    buckets,
    w_query,
    w_key,
    w_value,
    w_out,
    w_gate,
    w_up,
    w_down,
    bias_table,
    norm_attn,
    norm_ffn,
    cotangent,
):
    links = Links(reps, group)
    planes, core, plane, wing, q = links.planes, links.core, links.plane, links.wing, links.q
    spread, team = Spread(links, 0), Spread(links, 1)
    first_core = core == 0
    length, width = tokens.shape
    shard_rows, inner = w_query.shape
    head_count = bias_table.shape[1]
    head_size = inner // head_count
    bucket_count = bias_table.shape[0] * group
    half = inner // 2
    piece = w_down.shape[0] // 2
    unit = max(128, 16 * team.count)
    padded = (piece + unit - 1) // unit * unit
    at = jnp.stack([wing, core])
    share_rows = 2 * shard_rows // reps
    team_rows = 2 * shard_rows // team.count
    down_rows = padded // team.count
    out_rows = w_out.shape[0]
    fold = out_rows // share_rows
    order = Order()
    mark = order.mark

    def by_core(zero, one):
        return jnp.where(first_core, zero, one)

    def row_share(over, keep, recv):
        rows = 2 * shard_rows // over.count
        per = max(over.count // 2, 1)
        return lax.dynamic_slice_in_dim(
            jnp.where(over.own // per == core, keep, recv), over.own % per * rows, rows
        )

    def plane_of(step):
        return (plane + planes - step) % planes

    def column_half(side):
        return jnp.concatenate(
            [w[:, side * half : (side + 1) * half] for w in (w_query, w_key, w_value)], axis=1
        )

    half_zero, half_one = column_half(0), column_half(1)
    qkv_keep, qkv_send = by_core(half_zero, half_one), by_core(half_one, half_zero)
    qkv_recv = links.across(mark(qkv_send))
    ffn_keep, ffn_send = split_columns(at, order(w_gate), w_up, piece, padded)
    ffn_recv = links.across(mark(ffn_send))
    columns = width // reps
    out_share = pick([w_out[:, k * columns : (k + 1) * columns] for k in range(reps)], q)
    out_share = folded(out_share, 1, fold)
    packed_share = jnp.concatenate(
        [row_share(spread, order(qkv_keep), qkv_recv), out_share], axis=1
    )
    packed_steps = links.along_steps(mark(packed_share))
    small = jnp.concatenate([norm_attn, norm_ffn, bias_table.reshape(-1)])
    small_size = small.shape[0]
    small = jnp.pad(small, (0, -small_size % 1024)).reshape(-1, 128)
    small = mark(order(small))
    small_steps = links.along_steps(small)

    floats_in = order(tokens).astype(jnp.float32)
    scale_one = mark(
        lax.rsqrt(jnp.mean(floats_in * floats_in, axis=-1, keepdims=True) + EPSILON)
    )
    down_half = jnp.pad(
        lax.dynamic_slice_in_dim(order(w_down), wing * piece, piece), ((0, padded - piece), (0, 0))
    )
    down_share = mark(lax.dynamic_slice_in_dim(down_half, team.own * down_rows, down_rows))
    positions = lax.broadcasted_iota(jnp.int32, (bucket_count, buckets.shape[0] + 1), 0)
    turned_buckets = jnp.concatenate([order(buckets)[::-1], jnp.full((1,), -1, jnp.int32)])
    one_hot = mark((turned_buckets[None, :] == positions).astype(jnp.float32))

    small = mark(jnp.stack([order(small)] + small_steps))
    small_recv = links.across(small)
    packed_others = mark(jnp.concatenate([order(packed_steps[0])] + packed_steps[1:], axis=0))
    packed_shares, packed_owners = spread.gathered(packed_others)
    ffn_share = mark(row_share(team, order(ffn_keep), ffn_recv))
    f_ffn = lax.all_gather(ffn_share, ("plane", "team"), axis=0, tiled=True)
    f_down = lax.all_gather(
        tied(down_share, ffn_share), ("plane", "team"), axis=0, tiled=True
    )

    small = jnp.stack([order(small), small_recv])
    small = by_core(small, small[::-1])
    small = jnp.concatenate([small, small], axis=1)[:, ::-1]
    small = lax.dynamic_slice_in_dim(small, planes - 1 - plane, planes, axis=1)
    small = small.transpose(1, 0, 2, 3).reshape(group, -1)[:, :small_size]
    gain_one = small[:, :shard_rows].reshape(1, width).astype(jnp.float32)
    gain_two = small[:, shard_rows : 2 * shard_rows].reshape(1, width).astype(jnp.float32)
    full_table = small[:, 2 * shard_rows :].reshape(bucket_count, head_count)
    rel_bias = lax.dot_general(
        full_table.astype(jnp.float32),
        one_hot,
        (((0,), (0,)), ((), ())),
        precision=lax.Precision.HIGHEST,
    )
    bias_rows = mark(rel_bias.reshape(head_count // 2, 2, -1))
    normed_one = mark((order(floats_in) * scale_one * gain_one).astype(jnp.bfloat16))
    one_turned = mark(turn(normed_one, spread.slot_owners(), planes))

    wide = 3 * half
    cuts = [
        (0, 0, shard_rows, 0, 0, wide, (2 * plane + core) * shard_rows, 0),
        (1, 0, shard_rows, 0, 0, wide, (2 * plane + 1 - core) * shard_rows, 0),
        (2, 0, out_rows, 1, 0, width, plane * out_rows, 0),
    ]
    for number, owner in enumerate(packed_owners):
        for step in range(1, planes):
            start = (step - 1) * share_rows
            to = plane_of(step)
            row = to * 2 * shard_rows + owner * share_rows
            cuts.append((number + 3, start, share_rows, 0, 0, wide, row, 0))
            for k in range(fold):
                row = to * out_rows + k * share_rows
                cuts.append(
                    (
                        number + 3,
                        start,
                        share_rows,
                        1,
                        wide + k * columns,
                        columns,
                        row,
                        owner * columns,
                    )
                )
    qkv_half, out_mine = place(
        [order(qkv_keep), qkv_recv, w_out] + packed_shares,
        cuts,
        [(width, wide), (planes * out_rows, width)],
    )
    mark(qkv_half)
    qkv_other = links.across(qkv_half)
    out_theirs = links.across(out_mine)
    g_side = links.sideways(tied(cotangent, one_turned))
    own_qkv = mark(product([order(normed_one)], [qkv_half], most=384))
    other_qkv = mark(product([order(normed_one)], [qkv_other], most=384))
    qkv = mark(jnp.stack([by_core(order(own_qkv), other_qkv), by_core(other_qkv, own_qkv)]))
    context, context_turned, lse = run_forward(
        lengths, bias_rows, order(qkv), head_size
    )
    mark(context)
    (f_out,) = place(
        [order(out_mine), out_theirs],
        [
            (
                side,
                p * out_rows,
                out_rows,
                0,
                0,
                width,
                (2 * p + (core if side == 0 else 1 - core)) * out_rows,
                0,
            )
            for side in (0, 1)
            for p in range(planes)
        ],
        [(inner, width)],
    )
    attended = floats_in + nn(context, f_out)
    scale_two = lax.rsqrt(jnp.mean(attended * attended, axis=-1, keepdims=True) + EPSILON)
    unit_two = attended * scale_two
    normed_two = mark((unit_two * gain_two).astype(jnp.bfloat16))

    side_two = links.sideways(order(normed_two, g_side))
    core_two = links.across(normed_two)
    by_sides = context_turned.reshape(planes, 2, out_rows, length)
    context_own = by_core(order(by_sides)[:, 0], by_sides[:, 1]).reshape(-1, length)
    context_other = by_core(by_sides[:, 1], by_sides[:, 0]).reshape(-1, length)
    mark(context_own)
    g_core = links.across(order(cotangent))
    g_both = links.across(order(g_side))
    team_g = [cotangent, g_side, g_core, g_both]
    both_two = links.across(order(side_two))
    team_two = [normed_two, side_two, core_two, both_two]
    mark(order(both_two))
    hidden, hidden_turned, gate_slope, up_slope = gated([order(normed_two)] + team_two[1:], f_ffn)
    mark(hidden)

    two_turned = mark(turn_team([order(normed_two)] + team_two[1:]))
    d_pair = mark(gated_back([order(cotangent)] + team_g[1:], f_down, gate_slope, up_slope))
    d_own, d_side, d_sent = pair_back(order(d_pair), f_ffn)
    d_recv = links.across(mark(d_sent))

    d_side = mark((order(d_side) + d_recv[length:].astype(jnp.float32)).astype(jnp.bfloat16))
    d_theirs = links.sideways(d_side)
    ffn_sum = lax.psum_scatter(
        mark(pair_grad(order(two_turned), d_pair)),
        ("plane", "team"),
        scatter_dimension=0,
        tiled=True,
    )
    ffn_own, ffn_side, ffn_sent = product([order(hidden)], [f_down], kind="team")
    ffn_their = links.across(mark(ffn_sent))

    d_normed_two = (
        order(d_own) + d_recv[:length].astype(jnp.float32) + d_theirs.astype(jnp.float32)
    )
    ffn_gain_term = jnp.sum(d_normed_two * unit_two, axis=0)
    grad_in = cotangent.astype(jnp.float32)
    d_attended = grad_in + norm_back(d_normed_two, unit_two, scale_two, gain_two)
    d_branch = d_attended.astype(jnp.bfloat16)
    d_context = mark(product([d_branch], [f_out], across=True))
    ffn_side = mark((order(ffn_side) + ffn_their[length:].astype(jnp.float32)).astype(jnp.bfloat16))
    ffn_theirs = links.sideways(ffn_side)

    d_query, d_key, d_value, d_lined = run_backward(
        lengths, bias_rows, qkv, tied(d_context, ffn_side), lse, head_size
    )
    d_qkv = mark(jnp.concatenate([d_query, d_key, d_value], axis=2))
    d_mine = by_core(order(d_qkv)[0], d_qkv[1])
    d_other = by_core(d_qkv[1], d_qkv[0])
    owners = spread.slot_owners()
    d_normed_one = product(
        [order(d_mine), d_other], [qkv_half, qkv_other], across=True, kind="wide"
    )
    unit_one = floats_in * scale_one
    attn_gain_term = jnp.sum(d_normed_one * unit_one, axis=0)
    grad_tokens = mark(
        (d_attended + norm_back(d_normed_one, unit_one, scale_one, gain_one)).astype(jnp.bfloat16)
    )
    table_term = lax.dot_general(
        one_hot,
        order(d_lined).reshape(head_count, -1),
        (((1,), (1,)), ((), ())),
        precision=lax.Precision.HIGHEST,
    )
    terms = jnp.concatenate([attn_gain_term, ffn_gain_term, table_term.reshape(-1)])
    terms = mark(jnp.pad(terms, (0, -terms.shape[0] % 1024)).reshape(-1, 128))
    output = mark(
        (
            order(attended)
            + ffn_own
            + ffn_their[:length].astype(jnp.float32)
            + ffn_theirs.astype(jnp.float32)
        ).astype(jnp.bfloat16)
    )

    def packed(slots, grad, context_rows, added):
        return mark(
            packed_slots(
                one_turned,
                order(grad),
                context_rows,
                d_branch,
                slots,
                [owners[slot] for slot in slots],
                reps,
                planes,
                added,
            )
        )

    exchanges = links.spread_steps()

    def summed_on():
        nonlocal terms
        terms = mark(order(terms) + arrived_terms)

    back = packed([spread.turned_slot(slot) for slot in range(reps)], d_other, context_other, [])
    arrived_terms = exchanges.pop(0)(terms)
    arrived = [links.across(back)]
    low, high = reps // 2, reps
    for stage in range(spread.stages):
        summed_on()
        sent = packed(range(low, high), d_mine, context_own, [(value, low) for value in arrived])
        arrived_terms = exchanges.pop(0)(terms)
        arrived.append(spread.swap(sent, stage))
        if stage == 0:
            down_sum = lax.psum_scatter(
                mark(
                    column_slots(
                        order(hidden_turned), team_g, [jnp.int32(k) for k in range(reps)], width // reps
                    )
                ),
                ("plane", "team"),
                scatter_dimension=0,
                tiled=True,
            )
            order.last = (*order.last, ffn_sum)
        low, high = low // 2, low
    summed_on()
    sent = packed([0], d_mine, context_own, [(value, 0) for value in arrived])
    packed_parts = links.along_parts(sent, share_rows)
    ffn_steps = spread.gather_steps(order(ffn_sum))
    ffn_shares = next(ffn_steps)
    came = exchanges.pop(0)(terms)
    packed_total = mark(
        sum(
            part.astype(jnp.float32)
            for part in [order(packed_parts[0], ffn_shares[0][1])] + packed_parts[1:]
        ).astype(jnp.bfloat16)
    )
    packed_shares = spread.gathered(packed_total)
    for ffn_shares in ffn_steps:
        pass
    terms = tied(terms, packed_total) + came
    came = exchanges.pop(0)(terms)
    down_shares = spread.gathered(tied(down_sum, packed_shares[0][1]))
    terms = tied(terms, *packed_shares[0]) + came
    for exchange in exchanges:
        terms = terms + exchange(terms)
    terms = terms.reshape(-1)

    def by_owner(parts):
        per = len(parts) // 2
        low = jnp.concatenate(parts[:per], axis=0)
        high = jnp.concatenate(parts[per:], axis=0)
        return by_core(low, high), by_core(high, low)

    def wings_apart(parts):
        return parts[0::2] + parts[1::2]

    parts = in_order(None, *down_shares)
    grad_down = jnp.concatenate(
        [jnp.concatenate(parts[w::2], axis=0)[:piece] for w in (0, 1)], axis=0
    ).astype(jnp.float32)
    parts = in_order(None, *ffn_shares)
    per = reps // 2
    low, high = wings_apart(parts[:per]), wings_apart(parts[per:])
    low, high = jnp.concatenate(low, axis=0), jnp.concatenate(high, axis=0)
    ffn_mine, ffn_send = by_core(low, high), by_core(high, low)
    ffn_other = links.across(ffn_send)
    grad_gate, grad_up = join_columns(core, ffn_mine, ffn_other, piece, padded)

    parts = in_order(None, *packed_shares)
    grad_out = jnp.concatenate(
        [unfolded(part[:, wide:], fold) for part in parts], axis=1
    ).astype(jnp.float32)
    qkv_mine, qkv_send = by_owner([part[:, :wide] for part in parts])
    qkv_recv = links.across(qkv_send)
    grad_halves = (by_core(qkv_mine, qkv_recv), by_core(qkv_recv, qkv_mine))
    grad_query, grad_key, grad_value = [
        jnp.concatenate(
            [value[:, kind * half : (kind + 1) * half] for value in grad_halves], axis=1
        ).astype(jnp.float32)
        for kind in range(3)
    ]
    grad_norm_attn = lax.dynamic_slice_in_dim(terms, links.place * shard_rows, shard_rows)
    grad_norm_ffn = lax.dynamic_slice_in_dim(terms, width + links.place * shard_rows, shard_rows)
    table_size = bias_table.size
    grad_table = lax.dynamic_slice_in_dim(
        terms, 2 * width + links.place * table_size, table_size
    ).reshape(bias_table.shape)
    return (
        output,
        grad_tokens,
        grad_query,
        grad_key,
        grad_value,
        grad_out,
        grad_gate,
        grad_up,
        grad_down,
        grad_table,
        grad_norm_attn,
        grad_norm_ffn,
    )


def solution(mesh):
    reps, group = mesh.shape["rep"], mesh.shape["shard"]
    devices = mesh.devices.reshape(reps // 2, 2, group // 2, 2)
    rows, part = P(AXES[2:], None), P(AXES[2:])
    tokens = P(AXES, None)
    return jax.shard_map(
        functools.partial(layer, reps, group),
        mesh=jax.sharding.Mesh(devices, AXES),
        in_specs=(tokens, P(AXES), P()) + (rows,) * 8 + (part, part, tokens),
        out_specs=(tokens, tokens) + (rows,) * 8 + (part, part),
        check_vma=False,
    )
```

```python
import functools

import jax
import jax.numpy as jnp
from jax import lax
from jax.experimental import pallas as pl
from jax.experimental.pallas import tpu as pltpu
from jax.sharding import PartitionSpec as P

NEG_FILL = -1000000000.0
VMEM_LIMIT = 56 * 1024 * 1024
TOEP = 128
COST_SHARE = 1.0


def cost(flops):
    flops = int(flops * COST_SHARE)
    return pl.CostEstimate(flops=flops, bytes_accessed=flops // 512, transcendentals=0)


def dot_nn(a, b):
    return lax.dot_general(a, b, (((1,), (0,)), ((), ())), preferred_element_type=jnp.float32)


def dot_nt(a, b):
    return lax.dot_general(a, b, (((1,), (1,)), ((), ())), preferred_element_type=jnp.float32)


def dot_tn(a, b):
    return lax.dot_general(a, b, (((0,), (0,)), ((), ())), preferred_element_type=jnp.float32)


def biased_scores(rows_k, rows_q, bias_row, valid, length):
    steps = length // TOEP
    raw = dot_nt(rows_k, rows_q)
    width = bias_row.shape[-1]
    spread = jnp.broadcast_to(bias_row, (TOEP, width))
    table = pltpu.roll(spread, width - (TOEP - 1), 1, stride=1, stride_axis=0)
    blocks = []
    for step in range(steps):
        start = TOEP * (steps - 1 - step)
        row_at = lax.broadcasted_iota(jnp.int32, (TOEP, length), 0) + step * TOEP
        mask = jnp.where(row_at < valid, 0.0, NEG_FILL)
        blocks.append(
            raw[step * TOEP : (step + 1) * TOEP] + table[:, start : start + length] + mask
        )
    return jnp.concatenate(blocks, axis=0)


def attention_forward(valid_ref, bias_ref, q_ref, k_ref, v_ref, ctx_ref, turned_ref, lse_ref, *, head_size):
    length = q_ref.shape[1]
    pair = q_ref.shape[2] // head_size
    q, k, v = q_ref[0], k_ref[0], v_ref[0]
    lane_head = lax.broadcasted_iota(jnp.int32, q.shape, 1) // head_size
    v_turned = v.T
    outs = []
    for head in range(pair):
        own_q = jnp.where(lane_head == head, q, jnp.zeros_like(q))
        scores = biased_scores(k, own_q, bias_ref[0, head : head + 1], valid_ref[0], length)
        top = jnp.max(scores, axis=0, keepdims=True)
        terms = jnp.exp(scores - top)
        total = jnp.sum(terms, axis=0, keepdims=True)
        probs = (terms * (1.0 / total)).astype(jnp.bfloat16)
        lse_ref[0, head : head + 1] = top + jnp.log(total)
        outs.append(dot_nn(v_turned, probs)[head * head_size : (head + 1) * head_size])
    turned = jnp.concatenate(outs, axis=0)
    turned_ref[...] = turned.astype(jnp.bfloat16)
    ctx_ref[...] = turned.T.astype(jnp.bfloat16)


def attention_backward(
    valid_ref, bias_ref, q_ref, k_ref, v_ref, dctx_ref, lse_ref, dq_ref, dk_ref, dv_ref, rel_ref, *, head_size
):
    length = q_ref.shape[1]
    pair = q_ref.shape[2] // head_size
    steps = length // TOEP
    q, k, v, dctx = q_ref[0], k_ref[0], v_ref[0], dctx_ref[...]
    lane_head = lax.broadcasted_iota(jnp.int32, q.shape, 1) // head_size
    k_turned = k.T
    width = bias_ref.shape[-1]
    flip = (
        lax.broadcasted_iota(jnp.int32, (TOEP, TOEP), 0)
        + lax.broadcasted_iota(jnp.int32, (TOEP, TOEP), 1)
        == TOEP - 1
    ).astype(jnp.bfloat16)
    dq_parts = []
    dk = dv = None
    for head in range(pair):
        mine = lane_head == head
        own_q = jnp.where(mine, q, jnp.zeros_like(q))
        own_d = jnp.where(mine, dctx, jnp.zeros_like(dctx))
        scores = biased_scores(k, own_q, bias_ref[0, head : head + 1], valid_ref[0], length)
        probs = jnp.exp(scores - lse_ref[0, head : head + 1])
        d_probs = dot_nt(v, own_d)
        inner = jnp.sum(d_probs * probs, axis=0, keepdims=True)
        d_scores = (probs * (d_probs - inner)).astype(jnp.bfloat16)
        part_v = dot_nn(probs.astype(jnp.bfloat16), own_d)
        part_k = dot_nn(d_scores, own_q)
        dv = part_v if dv is None else dv + part_v
        dk = part_k if dk is None else dk + part_k
        dq_parts.append(dot_nn(k_turned, d_scores)[head * head_size : (head + 1) * head_size])
        fold = None
        for step in range(steps):
            start = TOEP * (steps - 1 - step)
            turned = dot_nn(flip, d_scores[step * TOEP : (step + 1) * TOEP])
            pieces = []
            if start:
                pieces.append(jnp.zeros((TOEP, start), jnp.float32))
            pieces.append(turned)
            if width - start - length:
                pieces.append(jnp.zeros((TOEP, width - start - length), jnp.float32))
            padded = jnp.concatenate(pieces, axis=1)
            fold = padded if fold is None else fold + padded
        lined = pltpu.roll(fold, 0, 1, stride=1, stride_axis=0)
        rel_ref[0, head : head + 1] = jnp.sum(lined, axis=0, keepdims=True)
    dq_ref[0] = jnp.concatenate(dq_parts, axis=0).T.astype(jnp.bfloat16)
    dk_ref[0] = dk.astype(jnp.bfloat16)
    dv_ref[0] = dv.astype(jnp.bfloat16)


def run_forward(valid, bias_rows, qkv, head_size):
    halves, length, wide = qkv.shape
    half = wide // 3
    per = half // 128
    pairs = halves * per
    width = bias_rows.shape[-1]
    spec = lambda kind: pl.BlockSpec((1, length, 128), lambda p: (p // per, 0, kind * per + p % per))
    return pl.pallas_call(
        functools.partial(attention_forward, head_size=head_size),
        grid=(pairs,),
        in_specs=[
            pl.BlockSpec(memory_space=pltpu.SMEM),
            pl.BlockSpec((1, 2, width), lambda p: (p, 0, 0)),
            spec(0), spec(1), spec(2),
        ],
        out_specs=[
            pl.BlockSpec((length, 128), lambda p: (0, p)),
            pl.BlockSpec((128, length), lambda p: (p, 0)),
            pl.BlockSpec((1, 2, length), lambda p: (p, 0, 0)),
        ],
        out_shape=[
            jax.ShapeDtypeStruct((length, halves * half), jnp.bfloat16),
            jax.ShapeDtypeStruct((halves * half, length), jnp.bfloat16),
            jax.ShapeDtypeStruct((pairs, 2, length), jnp.float32),
        ],
        compiler_params=pltpu.CompilerParams(vmem_limit_bytes=VMEM_LIMIT),
        name="attend",
        cost_estimate=cost(8 * pairs * 2 * length * length * 128),
    )(valid, bias_rows, qkv, qkv, qkv)


def run_backward(valid, bias_rows, qkv, d_context, lse, head_size):
    halves, length, wide = qkv.shape
    half = wide // 3
    per = half // 128
    pairs = halves * per
    width = bias_rows.shape[-1]
    spec = lambda kind: pl.BlockSpec((1, length, 128), lambda p: (p // per, 0, kind * per + p % per))
    out_spec = pl.BlockSpec((1, length, 128), lambda p: (p // per, 0, p % per))
    grad = jax.ShapeDtypeStruct((halves, length, half), jnp.bfloat16)
    row = pl.BlockSpec((1, 2, width), lambda p: (p, 0, 0))
    return pl.pallas_call(
        functools.partial(attention_backward, head_size=head_size),
        grid=(pairs,),
        in_specs=[
            pl.BlockSpec(memory_space=pltpu.SMEM),
            row,
            spec(0), spec(1), spec(2),
            pl.BlockSpec((length, 128), lambda p: (0, p)),
            pl.BlockSpec((1, 2, length), lambda p: (p, 0, 0)),
        ],
        out_specs=[out_spec, out_spec, out_spec, row],
        out_shape=[grad, grad, grad, jax.ShapeDtypeStruct((pairs, 2, width), jnp.float32)],
        compiler_params=pltpu.CompilerParams(vmem_limit_bytes=VMEM_LIMIT),
        name="attend_back",
        cost_estimate=cost(16 * pairs * 2 * length * length * 128),
    )(valid, bias_rows, qkv, qkv, qkv, d_context, lse)


EPSILON = 1e-06
AXES = ("team", "wing", "plane", "core")


def split_kernel(at_ref, gate_ref, up_ref, keep_ref, send_ref, *, cuts, piece, padded):
    rows = gate_ref.shape[0]
    first_wing, first_core = at_ref[0] == 0, at_ref[1] == 0
    filler = jnp.zeros((rows, padded - piece), jnp.float32)
    for number, ref in enumerate((gate_ref, up_ref)):
        w = ref[...].astype(jnp.float32)
        for cut in range(cuts):
            sides = []
            for side in (0, 1):
                zero, one = [
                    w[:, (4 * cut + 2 * side + wing) * piece :][:, :piece] for wing in (0, 1)
                ]
                chosen = jnp.where(first_wing, zero, one)
                sides.append(jnp.concatenate([chosen, filler], axis=1).astype(jnp.bfloat16))
            start = (number * cuts + cut) * padded
            to = slice(start, start + padded)
            keep_ref[:, to] = jnp.where(first_core, sides[0], sides[1])
            send_ref[:, to] = jnp.where(first_core, sides[1], sides[0])


def split_columns(at, w_gate, w_up, piece, padded):
    rows, wide = w_gate.shape
    cuts = wide // (4 * piece)
    out = jax.ShapeDtypeStruct((rows, 2 * cuts * padded), jnp.bfloat16)
    whole = pl.BlockSpec(memory_space=pltpu.VMEM)
    return pl.pallas_call(
        functools.partial(split_kernel, cuts=cuts, piece=piece, padded=padded),
        in_specs=[pl.BlockSpec(memory_space=pltpu.SMEM), whole, whole],
        out_specs=[whole, whole],
        out_shape=[out, out],
        compiler_params=pltpu.CompilerParams(vmem_limit_bytes=VMEM_LIMIT),
        name="split",
        cost_estimate=cost(512 * w_gate.size),
    )(at, w_gate, w_up)


def join_kernel(core_ref, mine_ref, other_ref, gate_ref, up_ref, *, cuts, piece, padded):
    rows = gate_ref.shape[0]
    first_core = core_ref[0] == 0
    for number, out_ref in enumerate((gate_ref, up_ref)):
        for cut in range(cuts):
            start = (number * cuts + cut) * padded
            at = slice(start, start + padded)
            for wing in (0, 1):
                of = slice(wing * rows, (wing + 1) * rows)
                mine, other = mine_ref[of, at], other_ref[of, at]
                for side in (0, 1):
                    value = jnp.where(first_core, *((mine, other) if side == 0 else (other, mine)))
                    to = (4 * cut + 2 * side + wing) * piece
                    out_ref[:, to : to + piece] = value.astype(jnp.float32)[:, :piece]


def join_columns(core, mine, other, piece, padded):
    rows = mine.shape[0] // 2
    cuts = mine.shape[1] // (2 * padded)
    out = jax.ShapeDtypeStruct((rows, 4 * cuts * piece), jnp.float32)
    whole = pl.BlockSpec(memory_space=pltpu.VMEM)
    return pl.pallas_call(
        functools.partial(join_kernel, cuts=cuts, piece=piece, padded=padded),
        in_specs=[pl.BlockSpec(memory_space=pltpu.SMEM), whole, whole],
        out_specs=[whole, whole],
        out_shape=[out, out],
        compiler_params=pltpu.CompilerParams(vmem_limit_bytes=VMEM_LIMIT),
        name="join",
        cost_estimate=cost(512 * mine.size),
    )(core[None], mine, other)


def turn_kernel(owners_ref, x_ref, out_ref, turned_ref, *, slots, rows):
    turned_ref[...] = x_ref[...].T
    for slot in range(slots):
        start = pl.multiple_of(owners_ref[slot] * rows, 16)
        out_ref[slot, 0] = turned_ref[pl.ds(start, rows)]


def turn(x, owners, planes):
    tokens, width = x.shape
    slots = len(owners)
    plane = width // planes
    rows = plane // slots
    if plane % 128 or rows % 16:
        blocks = x.T.reshape(planes, slots, rows, tokens)
        picked = [lax.dynamic_slice_in_dim(blocks, owner, 1, axis=1) for owner in owners]
        return jnp.concatenate(picked, axis=1).transpose(1, 0, 2, 3).reshape(width, tokens)
    return pl.pallas_call(
        functools.partial(turn_kernel, slots=slots, rows=rows),
        grid=(planes,),
        in_specs=[
            pl.BlockSpec(memory_space=pltpu.SMEM),
            pl.BlockSpec((tokens, plane), lambda p: (0, p)),
        ],
        out_specs=pl.BlockSpec((slots, 1, rows, tokens), lambda p: (0, p, 0, 0)),
        out_shape=jax.ShapeDtypeStruct((slots, planes, rows, tokens), x.dtype),
        scratch_shapes=[pltpu.VMEM((plane, tokens), x.dtype)],
        compiler_params=pltpu.CompilerParams(vmem_limit_bytes=VMEM_LIMIT),
        name="turn",
        cost_estimate=cost(512 * x.size),
    )(jnp.stack(owners), x).reshape(width, tokens)


def turn_team_kernel(*refs):
    out_ref = refs[-1]
    for number, ref in enumerate(refs[:-1]):
        rows = ref.shape[0]
        out_ref[:, number * rows : (number + 1) * rows] = ref[...].T


def turn_team(blocks):
    rows, width = blocks[0].shape
    tile = tile_of(width, 256)
    tokens = rows * len(blocks)
    return pl.pallas_call(
        turn_team_kernel,
        grid=(width // tile,),
        in_specs=[pl.BlockSpec((rows, tile), lambda j: (0, j))] * len(blocks),
        out_specs=pl.BlockSpec((tile, tokens), lambda j: (j, 0)),
        out_shape=jax.ShapeDtypeStruct((width, tokens), blocks[0].dtype),
        compiler_params=pltpu.CompilerParams(vmem_limit_bytes=VMEM_LIMIT),
        name="turn_team",
        cost_estimate=cost(512 * tokens * width),
    )(*blocks)


def place_kernel(at_ref, *refs, cuts, outs):
    sources, out_refs, sems = refs[: -1 - outs], refs[-1 - outs : -1], refs[-1]
    copies = []
    for number, (source, start, rows, of, column, wide) in enumerate(cuts):
        row_to = pl.multiple_of(at_ref[0, number], 16)
        column_to = pl.multiple_of(at_ref[1, number], 128)
        copies.append(
            pltpu.make_async_copy(
                sources[source].at[pl.ds(start, rows), pl.ds(column, wide)],
                out_refs[of].at[pl.ds(row_to, rows), pl.ds(column_to, wide)],
                sems.at[number],
            )
        )
    for copy in copies:
        copy.start()
    for copy in copies:
        copy.wait()


def place(sources, cuts, shapes):
    low = sources[0].dtype
    if any(cut[1] % 16 or cut[2] % 16 or cut[4] % 128 or cut[5] % 128 for cut in cuts):
        outs = [jnp.zeros(shape, low) for shape in shapes]
        for source, start, rows, of, column, wide, row_to, column_to in cuts:
            part = sources[source][start : start + rows, column : column + wide]
            outs[of] = lax.dynamic_update_slice(outs[of], part, (row_to, column_to))
        return outs
    places = jnp.stack(
        [jnp.stack([jnp.asarray(cut[k], jnp.int32) for cut in cuts]) for k in (6, 7)]
    )
    return pl.pallas_call(
        functools.partial(place_kernel, cuts=[cut[:6] for cut in cuts], outs=len(shapes)),
        in_specs=[pl.BlockSpec(memory_space=pltpu.SMEM)]
        + [pl.BlockSpec(memory_space=pl.ANY)] * len(sources),
        out_specs=[pl.BlockSpec(memory_space=pltpu.VMEM)] * len(shapes),
        out_shape=[jax.ShapeDtypeStruct(shape, low) for shape in shapes],
        scratch_shapes=[pltpu.SemaphoreType.DMA((len(cuts),))],
        compiler_params=pltpu.CompilerParams(vmem_limit_bytes=VMEM_LIMIT),
        name="place",
        cost_estimate=cost(512 * sum(a * b for a, b in shapes)),
    )(places, *sources)


def tile_of(size, most):
    for count in range(1, size // 128 + 1):
        if size % count == 0 and size // count % 128 == 0 and size // count <= most:
            return size // count
    return size


def product_kernel(*refs, pairs, across, kind):
    total = None
    for number in range(pairs):
        left, right = refs[2 * number][...], refs[2 * number + 1][...]
        term = dot_nt(left, right) if across else dot_nn(left, right)
        total = term if total is None else total + term
    outs = refs[2 * pairs :]
    if kind == "team":
        rows = outs[0].shape[0]
        outs[0][...] = total[:rows]
        outs[1][...] = total[rows : 2 * rows]
        outs[2][...] = total[2 * rows :].astype(jnp.bfloat16)
    else:
        outs[0][...] = total.astype(outs[0].dtype)


def product(lefts, rights, across=False, kind="low", most=512):
    rows = lefts[0].shape[0]
    wide = rights[0].shape[0 if across else 1]
    tile = tile_of(wide, most)
    operands, specs = [], []
    for left, right in zip(lefts, rights):
        depth = left.shape[1]
        operands += [left, right]
        specs.append(pl.BlockSpec((rows, depth), lambda j: (0, 0)))
        if across:
            specs.append(pl.BlockSpec((tile, depth), lambda j: (j, 0)))
        else:
            specs.append(pl.BlockSpec((depth, tile), lambda j: (0, j)))
    if kind == "team":
        shapes = [(rows // 4, jnp.float32), (rows // 4, jnp.float32), (rows // 2, jnp.bfloat16)]
    else:
        shapes = [(rows, jnp.bfloat16 if kind == "low" else jnp.float32)]
    outs = pl.pallas_call(
        functools.partial(product_kernel, pairs=len(lefts), across=across, kind=kind),
        grid=(wide // tile,),
        in_specs=specs,
        out_specs=[pl.BlockSpec((size, tile), lambda j: (0, j)) for size, _ in shapes],
        out_shape=[jax.ShapeDtypeStruct((size, wide), kept) for size, kept in shapes],
        compiler_params=pltpu.CompilerParams(vmem_limit_bytes=VMEM_LIMIT),
        name="product",
        cost_estimate=cost(2 * rows * depth * wide * len(lefts)),
    )(*operands)
    return outs if kind == "team" else outs[0]


def column_slot_kernel(at_ref, left_ref, *refs, count, added):
    right = jnp.concatenate([ref[...] for ref in refs[:count]], axis=0)
    total = dot_nn(left_ref[...], right)
    for ref in refs[count : count + added]:
        total = total + ref[...].astype(jnp.float32)
    refs[-1][...] = total.astype(jnp.bfloat16)


def column_slots(left, blocks, owners, wide, added=()):
    rows = left.shape[0]
    if wide % 128:
        whole = jnp.concatenate(blocks, axis=0)
        value = jnp.concatenate(
            [nn(left, lax.dynamic_slice_in_dim(whole, owner * wide, wide, axis=1)) for owner in owners],
            axis=1,
        )
        for array, first in added:
            value = value + array[:, first * wide : (first + len(owners)) * wide].astype(jnp.float32)
        return value.astype(jnp.bfloat16)
    tile = tile_of(wide, 512)
    per = wide // tile
    return pl.pallas_call(
        functools.partial(column_slot_kernel, count=len(blocks), added=len(added)),
        grid_spec=pltpu.PrefetchScalarGridSpec(
            num_scalar_prefetch=1,
            grid=(len(owners) * per,),
            in_specs=[pl.BlockSpec(left.shape, lambda j, at: (0, 0))]
            + [
                pl.BlockSpec((block.shape[0], tile), lambda j, at: (0, at[j // per] * per + j % per))
                for block in blocks
            ]
            + [
                pl.BlockSpec((rows, tile), lambda j, at, first=first: (0, first * per + j))
                for _, first in added
            ],
            out_specs=pl.BlockSpec((rows, tile), lambda j, at: (0, j)),
        ),
        out_shape=jax.ShapeDtypeStruct((rows, len(owners) * wide), jnp.bfloat16),
        compiler_params=pltpu.CompilerParams(vmem_limit_bytes=VMEM_LIMIT),
        name="column_slots",
        cost_estimate=cost(2 * left.size * wide * len(owners)),
    )(jnp.stack(owners), left, *blocks, *[array for array, _ in added])


def packed_slot_kernel(row_ref, at_ref, turned_ref, grad_ref, context_ref, branch_ref, *refs):
    out_ref = refs[-1]
    first = dot_nn(turned_ref[...], grad_ref[...])
    second = dot_nn(context_ref[...], branch_ref[...])
    wide = first.shape[1]
    for ref in refs[:-1]:
        first = first + ref[:, :wide].astype(jnp.float32)
        second = second + ref[:, wide:].astype(jnp.float32)
    out_ref[:, :wide] = first.astype(jnp.bfloat16)
    out_ref[:, wide:] = second.astype(jnp.bfloat16)


def packed_slots(turned, grad, context, branch, slots, owners, reps, planes, added=()):
    rows = turned.shape[0] // reps
    columns = branch.shape[1] // reps
    fold = context.shape[0] // rows
    wide = grad.shape[1] + fold * columns
    if fold != 1 or columns % 128:
        outs = []
        for slot, owner in zip(slots, owners):
            first = nn(turned[slot * rows : (slot + 1) * rows], grad)
            second = nn(context, lax.dynamic_slice_in_dim(branch, owner * columns, columns, axis=1))
            outs.append(jnp.concatenate([first, folded(second, planes, fold)], axis=1))
        value = jnp.concatenate(outs, axis=0)
        for array, start in added:
            value = value + array[start * rows :][: value.shape[0]].astype(jnp.float32)
        return value.astype(jnp.bfloat16)
    block = lambda start: pl.BlockSpec((rows, wide), lambda i, row, at: (start + i, 0))
    return pl.pallas_call(
        packed_slot_kernel,
        grid_spec=pltpu.PrefetchScalarGridSpec(
            num_scalar_prefetch=2,
            grid=(len(slots),),
            in_specs=[
                pl.BlockSpec((rows, turned.shape[1]), lambda i, row, at: (row[i], 0)),
                pl.BlockSpec(grad.shape, lambda i, row, at: (0, 0)),
                pl.BlockSpec(context.shape, lambda i, row, at: (0, 0)),
                pl.BlockSpec((branch.shape[0], columns), lambda i, row, at: (0, at[i])),
            ]
            + [block(start) for _, start in added],
            out_specs=block(0),
        ),
        out_shape=jax.ShapeDtypeStruct((len(slots) * rows, wide), jnp.bfloat16),
        compiler_params=pltpu.CompilerParams(vmem_limit_bytes=VMEM_LIMIT),
        name="packed_slots",
        cost_estimate=cost(2 * len(slots) * rows * turned.shape[1] * wide),
    )(
        jnp.array(slots, jnp.int32),
        jnp.stack(owners),
        turned,
        grad,
        context,
        branch,
        *[array for array, _ in added],
    )


def folded(value, planes, fold):
    rows, wide = value.shape
    split = value.reshape(planes, fold, rows // (planes * fold), wide)
    return split.transpose(0, 2, 1, 3).reshape(rows // fold, fold * wide)


def unfolded(value, fold):
    rows, wide = value.shape
    return value.reshape(rows, fold, wide // fold).transpose(1, 0, 2).reshape(rows * fold, -1)


GELU_RATE = 0.7978845608028654
GELU_CUBE = 0.044715


def gated_kernel(*refs, count):
    gate_ref, up_ref, hidden_ref, turned_ref, gate_slope_ref, up_slope_ref = refs[count:]
    for number in range(count):
        x = refs[number][...]
        rows = x.shape[0]
        at = slice(number * rows, (number + 1) * rows)
        gate = dot_nn(x, gate_ref[...])
        up = dot_nn(x, up_ref[...])
        square = gate * gate
        bent = jnp.tanh(GELU_RATE * gate * (1.0 + GELU_CUBE * square))
        share = 0.5 * (1.0 + bent)
        gelu = gate * share
        slope = share + 0.5 * gate * (1.0 - bent * bent) * (
            GELU_RATE * (1.0 + 3.0 * GELU_CUBE * square)
        )
        hidden = (gelu * up).astype(jnp.bfloat16)
        hidden_ref[at] = hidden
        turned_ref[:, at] = hidden.T
        gate_slope_ref[at] = (slope * up).astype(jnp.bfloat16)
        up_slope_ref[at] = gelu.astype(jnp.bfloat16)


def gated(blocks, f_both):
    rows, depth = blocks[0].shape
    tokens = rows * len(blocks)
    wide = f_both.shape[1] // 2
    tile = tile_of(wide, 256)
    steps = wide // tile
    out = pl.BlockSpec((tokens, tile), lambda j: (0, j))
    kept = jax.ShapeDtypeStruct((tokens, wide), jnp.bfloat16)
    return pl.pallas_call(
        functools.partial(gated_kernel, count=len(blocks)),
        grid=(steps,),
        in_specs=[pl.BlockSpec((rows, depth), lambda j: (0, 0))] * len(blocks)
        + [
            pl.BlockSpec((depth, tile), lambda j: (0, j)),
            pl.BlockSpec((depth, tile), lambda j: (0, steps + j)),
        ],
        out_specs=[out, pl.BlockSpec((tile, tokens), lambda j: (j, 0)), out, out],
        out_shape=[kept, jax.ShapeDtypeStruct((wide, tokens), jnp.bfloat16), kept, kept],
        compiler_params=pltpu.CompilerParams(vmem_limit_bytes=VMEM_LIMIT),
        name="gated",
        cost_estimate=cost(4 * tokens * depth * wide),
    )(*blocks, f_both, f_both)


def gated_back_kernel(*refs, count):
    down_ref, gate_slope_ref, up_slope_ref, out_ref = refs[count:]
    for number in range(count):
        rows = refs[number].shape[0]
        at = slice(number * rows, (number + 1) * rows)
        d_hidden = dot_nt(refs[number][...], down_ref[...])
        out_ref[0, at] = (d_hidden * gate_slope_ref[at].astype(jnp.float32)).astype(jnp.bfloat16)
        out_ref[1, at] = (d_hidden * up_slope_ref[at].astype(jnp.float32)).astype(jnp.bfloat16)


def gated_back(blocks, f_down, gate_slope, up_slope):
    rows, depth = blocks[0].shape
    tokens = rows * len(blocks)
    wide = f_down.shape[0]
    tile = tile_of(wide, 512)
    column = pl.BlockSpec((tokens, tile), lambda j: (0, j))
    return pl.pallas_call(
        functools.partial(gated_back_kernel, count=len(blocks)),
        grid=(wide // tile,),
        in_specs=[pl.BlockSpec((rows, depth), lambda j: (0, 0))] * len(blocks)
        + [pl.BlockSpec((tile, depth), lambda j: (j, 0)), column, column],
        out_specs=pl.BlockSpec((2, tokens, tile), lambda j: (0, 0, j)),
        out_shape=jax.ShapeDtypeStruct((2, tokens, wide), jnp.bfloat16),
        compiler_params=pltpu.CompilerParams(vmem_limit_bytes=VMEM_LIMIT),
        name="gated_back",
        cost_estimate=cost(2 * tokens * depth * wide),
    )(*blocks, f_down, gate_slope, up_slope)


def pair_grad_kernel(left_ref, right_ref, out_ref):
    out_ref[...] = dot_nn(left_ref[...], right_ref[0]).astype(jnp.bfloat16)


def pair_grad(left, pair):
    rows, depth = left.shape
    wide = pair.shape[2]
    tile = tile_of(wide, 512)
    steps = wide // tile
    return pl.pallas_call(
        pair_grad_kernel,
        grid=(2 * steps,),
        in_specs=[
            pl.BlockSpec((rows, depth), lambda j: (0, 0)),
            pl.BlockSpec((1, depth, tile), lambda j: (j // steps, 0, j % steps)),
        ],
        out_specs=pl.BlockSpec((rows, tile), lambda j: (0, j)),
        out_shape=jax.ShapeDtypeStruct((rows, 2 * wide), jnp.bfloat16),
        compiler_params=pltpu.CompilerParams(vmem_limit_bytes=VMEM_LIMIT),
        name="pair_grad",
        cost_estimate=cost(4 * rows * depth * wide),
    )(left, pair)


def pair_back_kernel(pair_ref, right_ref, own_ref, side_ref, sent_ref):
    wide = pair_ref.shape[2]
    rows = own_ref.shape[0]
    right = right_ref[...]
    total = dot_nt(pair_ref[0], right[:, :wide]) + dot_nt(pair_ref[1], right[:, wide:])
    own_ref[...] = total[:rows]
    side_ref[...] = total[rows : 2 * rows]
    sent_ref[...] = total[2 * rows :].astype(jnp.bfloat16)


def pair_back(pair, f_both):
    tokens, wide = pair.shape[1:]
    width = f_both.shape[0]
    tile = tile_of(width, 512)
    shapes = [(tokens // 4, jnp.float32), (tokens // 4, jnp.float32), (tokens // 2, jnp.bfloat16)]
    return pl.pallas_call(
        pair_back_kernel,
        grid=(width // tile,),
        in_specs=[
            pl.BlockSpec(pair.shape, lambda j: (0, 0, 0), pipeline_mode=pl.Buffered(1)),
            pl.BlockSpec((tile, 2 * wide), lambda j: (j, 0)),
        ],
        out_specs=[pl.BlockSpec((size, tile), lambda j: (0, j)) for size, _ in shapes],
        out_shape=[jax.ShapeDtypeStruct((size, width), kept) for size, kept in shapes],
        compiler_params=pltpu.CompilerParams(vmem_limit_bytes=VMEM_LIMIT),
        name="pair_back",
        cost_estimate=cost(4 * tokens * wide * width),
    )(pair, f_both)


def norm_back(upstream, unit_rows, scale_rows, gain_rows):
    scaled = upstream * gain_rows
    return scale_rows * (scaled - unit_rows * jnp.mean(scaled * unit_rows, axis=-1, keepdims=True))


def tied(value, *after):
    return lax.optimization_barrier((value, *after))[0]


class Order:
    def __init__(self):
        self.last = ()

    def __call__(self, value, *after):
        return tied(value, *self.last, *after) if self.last or after else value

    def mark(self, value):
        self.last = (value,)
        return value


class Links:
    def __init__(self, reps, group):
        self.reps, self.group, self.planes = reps, group, group // 2
        self.team, self.wing, self.plane, self.core = map(lax.axis_index, AXES)
        self.q = 2 * self.team + self.wing
        self.place = 2 * self.plane + self.core

    def move(self, value, target):
        pairs = []
        for r in range(self.reps):
            for s in range(self.group):
                to_r, to_s = target(r, s)
                pairs.append((r * self.group + s, to_r * self.group + to_s))
        return lax.ppermute(value, AXES, pairs)

    def across(self, value):
        return self.move(value, lambda r, s: (r, s ^ 1))

    def sideways(self, value):
        return self.move(value, lambda r, s: (r ^ 1, s))

    def along(self, value, step):
        return self.move(value, lambda r, s: (r, (s + 2 * step) % self.group))

    def along_parts(self, value, rows):
        parts = [lax.dynamic_slice_in_dim(value, self.plane * rows, rows)]
        for step in range(1, self.planes):
            to = (self.plane + step) % self.planes
            parts.append(self.along(lax.dynamic_slice_in_dim(value, to * rows, rows), step))
        return parts

    def along_steps(self, share):
        return [self.along(share, k) for k in range(1, self.planes)]

    def spread_steps(self):
        steps = [(0, 1 << k) for k in range(self.group.bit_length() - 1)]
        steps += [(1 << k, 0) for k in range(self.reps.bit_length() - 1)]
        return [
            lambda value, r_step=r_step, s_step=s_step: self.move(
                value, lambda r, s: (r ^ r_step, s ^ s_step)
            )
            for r_step, s_step in steps
        ]


class Spread:
    def __init__(self, links, low):
        self.links, self.low = links, low
        self.count = links.reps >> low
        self.stages = self.count.bit_length() - 1
        self.own = links.q >> low

    def bit_of(self, stage, core):
        return 1 << (stage if core == 0 else self.stages - 1 - stage)

    def swap(self, value, stage):
        return self.links.move(
            value, lambda r, s: (r ^ (self.bit_of(stage, s % 2) << self.low), s)
        )

    def bit(self, stage):
        return jnp.where(self.links.core == 0, self.bit_of(stage, 0), self.bit_of(stage, 1))

    def gathered(self, value):
        parts, offsets = [value], [jnp.int32(0)]
        for stage in range(self.stages):
            parts += [self.swap(part, stage) for part in parts]
            offsets += [offset ^ self.bit(stage) for offset in offsets]
        return parts, [self.own ^ offset for offset in offsets]

    def gather_steps(self, value):
        parts, offsets = [value], [jnp.int32(0)]
        for stage in range(self.stages):
            added = [self.swap(part, stage) for part in parts]
            parts, offsets = parts + added, offsets + [offset ^ self.bit(stage) for offset in offsets]
            yield parts, [self.own ^ offset for offset in offsets]

    def turned_slot(self, slot):
        return sum(((slot >> k) & 1) << (self.stages - 1 - k) for k in range(self.stages))

    def slot_owners(self):
        owners = []
        for slot in range(self.count):
            owner = self.own
            for stage in range(self.stages):
                if (slot >> (self.stages - 1 - stage)) & 1:
                    owner = owner ^ self.bit(stage)
            owners.append(owner)
        return owners


def pick(blocks, index):
    value = blocks[0]
    for k in range(1, len(blocks)):
        value = jnp.where(index == k, blocks[k], value)
    return value


def in_order(first, parts, owners):
    parts = [parts[0] if first is None else first] + parts[1:]
    ordered = []
    for k in range(len(parts)):
        value = parts[0]
        for part, owner in zip(parts[1:], owners[1:]):
            value = jnp.where(owner == k, part, value)
        ordered.append(value)
    return ordered


def nn(left, right):
    return jnp.dot(left, right, preferred_element_type=jnp.float32)


def layer(
    reps,
    group,
    tokens,
    lengths,
    buckets,
    w_query,
    w_key,
    w_value,
    w_out,
    w_gate,
    w_up,
    w_down,
    bias_table,
    norm_attn,
    norm_ffn,
    cotangent,
):
    links = Links(reps, group)
    planes, core, plane, wing, q = links.planes, links.core, links.plane, links.wing, links.q
    spread, team = Spread(links, 0), Spread(links, 1)
    first_core = core == 0
    length, width = tokens.shape
    shard_rows, inner = w_query.shape
    head_count = bias_table.shape[1]
    head_size = inner // head_count
    bucket_count = bias_table.shape[0] * group
    half = inner // 2
    piece = w_down.shape[0] // 2
    unit = max(128, 16 * team.count)
    padded = (piece + unit - 1) // unit * unit
    at = jnp.stack([wing, core])
    share_rows = 2 * shard_rows // reps
    team_rows = 2 * shard_rows // team.count
    down_rows = padded // team.count
    out_rows = w_out.shape[0]
    fold = out_rows // share_rows
    order = Order()
    mark = order.mark

    def by_core(zero, one):
        return jnp.where(first_core, zero, one)

    def row_share(over, keep, recv):
        rows = 2 * shard_rows // over.count
        per = max(over.count // 2, 1)
        return lax.dynamic_slice_in_dim(
            jnp.where(over.own // per == core, keep, recv), over.own % per * rows, rows
        )

    def plane_of(step):
        return (plane + planes - step) % planes

    def column_half(side):
        return jnp.concatenate(
            [w[:, side * half : (side + 1) * half] for w in (w_query, w_key, w_value)], axis=1
        )

    half_zero, half_one = column_half(0), column_half(1)
    qkv_keep, qkv_send = by_core(half_zero, half_one), by_core(half_one, half_zero)
    qkv_recv = links.across(mark(qkv_send))
    ffn_keep, ffn_send = split_columns(at, order(w_gate), w_up, piece, padded)
    ffn_recv = links.across(mark(ffn_send))
    columns = width // reps
    out_share = pick([w_out[:, k * columns : (k + 1) * columns] for k in range(reps)], q)
    out_share = folded(out_share, 1, fold)
    packed_share = jnp.concatenate(
        [row_share(spread, order(qkv_keep), qkv_recv), out_share], axis=1
    )
    packed_steps = links.along_steps(mark(packed_share))
    small = jnp.concatenate([norm_attn, norm_ffn, bias_table.reshape(-1)])
    small_size = small.shape[0]
    small = jnp.pad(small, (0, -small_size % 1024)).reshape(-1, 128)
    small = mark(order(small))
    small_steps = links.along_steps(small)

    floats_in = order(tokens).astype(jnp.float32)
    scale_one = mark(
        lax.rsqrt(jnp.mean(floats_in * floats_in, axis=-1, keepdims=True) + EPSILON)
    )
    down_half = jnp.pad(
        lax.dynamic_slice_in_dim(order(w_down), wing * piece, piece), ((0, padded - piece), (0, 0))
    )
    down_share = mark(lax.dynamic_slice_in_dim(down_half, team.own * down_rows, down_rows))
    positions = lax.broadcasted_iota(jnp.int32, (bucket_count, buckets.shape[0] + 1), 0)
    turned_buckets = jnp.concatenate([order(buckets)[::-1], jnp.full((1,), -1, jnp.int32)])
    one_hot = mark((turned_buckets[None, :] == positions).astype(jnp.float32))

    small = mark(jnp.stack([order(small)] + small_steps))
    small_recv = links.across(small)
    packed_others = mark(jnp.concatenate([order(packed_steps[0])] + packed_steps[1:], axis=0))
    packed_shares, packed_owners = spread.gathered(packed_others)
    ffn_share = mark(row_share(team, order(ffn_keep), ffn_recv))
    f_ffn = lax.all_gather(ffn_share, ("plane", "team"), axis=0, tiled=True)
    f_down = lax.all_gather(
        tied(down_share, ffn_share), ("plane", "team"), axis=0, tiled=True
    )

    small = jnp.stack([order(small), small_recv])
    small = by_core(small, small[::-1])
    small = jnp.concatenate([small, small], axis=1)[:, ::-1]
    small = lax.dynamic_slice_in_dim(small, planes - 1 - plane, planes, axis=1)
    small = small.transpose(1, 0, 2, 3).reshape(group, -1)[:, :small_size]
    gain_one = small[:, :shard_rows].reshape(1, width).astype(jnp.float32)
    gain_two = small[:, shard_rows : 2 * shard_rows].reshape(1, width).astype(jnp.float32)
    full_table = small[:, 2 * shard_rows :].reshape(bucket_count, head_count)
    rel_bias = lax.dot_general(
        full_table.astype(jnp.float32),
        one_hot,
        (((0,), (0,)), ((), ())),
        precision=lax.Precision.HIGHEST,
    )
    bias_rows = mark(rel_bias.reshape(head_count // 2, 2, -1))
    normed_one = mark((order(floats_in) * scale_one * gain_one).astype(jnp.bfloat16))
    one_turned = mark(turn(normed_one, spread.slot_owners(), planes))

    wide = 3 * half
    cuts = [
        (0, 0, shard_rows, 0, 0, wide, (2 * plane + core) * shard_rows, 0),
        (1, 0, shard_rows, 0, 0, wide, (2 * plane + 1 - core) * shard_rows, 0),
        (2, 0, out_rows, 1, 0, width, plane * out_rows, 0),
    ]
    for number, owner in enumerate(packed_owners):
        for step in range(1, planes):
            start = (step - 1) * share_rows
            to = plane_of(step)
            row = to * 2 * shard_rows + owner * share_rows
            cuts.append((number + 3, start, share_rows, 0, 0, wide, row, 0))
            for k in range(fold):
                row = to * out_rows + k * share_rows
                cuts.append(
                    (
                        number + 3,
                        start,
                        share_rows,
                        1,
                        wide + k * columns,
                        columns,
                        row,
                        owner * columns,
                    )
                )
    qkv_half, out_mine = place(
        [order(qkv_keep), qkv_recv, w_out] + packed_shares,
        cuts,
        [(width, wide), (planes * out_rows, width)],
    )
    mark(qkv_half)
    qkv_other = links.across(qkv_half)
    out_theirs = links.across(out_mine)
    g_side = links.sideways(tied(cotangent, one_turned))
    own_qkv = mark(product([order(normed_one)], [qkv_half], most=384))
    other_qkv = mark(product([order(normed_one)], [qkv_other], most=384))
    qkv = mark(jnp.stack([by_core(order(own_qkv), other_qkv), by_core(other_qkv, own_qkv)]))
    context, context_turned, lse = run_forward(
        lengths, bias_rows, order(qkv), head_size
    )
    mark(context)
    (f_out,) = place(
        [order(out_mine), out_theirs],
        [
            (
                side,
                p * out_rows,
                out_rows,
                0,
                0,
                width,
                (2 * p + (core if side == 0 else 1 - core)) * out_rows,
                0,
            )
            for side in (0, 1)
            for p in range(planes)
        ],
        [(inner, width)],
    )
    attended = floats_in + nn(context, f_out)
    scale_two = lax.rsqrt(jnp.mean(attended * attended, axis=-1, keepdims=True) + EPSILON)
    unit_two = attended * scale_two
    normed_two = mark((unit_two * gain_two).astype(jnp.bfloat16))

    side_two = links.sideways(order(normed_two, g_side))
    core_two = links.across(normed_two)
    by_sides = context_turned.reshape(planes, 2, out_rows, length)
    context_own = by_core(order(by_sides)[:, 0], by_sides[:, 1]).reshape(-1, length)
    context_other = by_core(by_sides[:, 1], by_sides[:, 0]).reshape(-1, length)
    mark(context_own)
    g_core = links.across(order(cotangent))
    g_both = links.across(order(g_side))
    team_g = [cotangent, g_side, g_core, g_both]
    both_two = links.across(order(side_two))
    team_two = [normed_two, side_two, core_two, both_two]
    mark(order(both_two))
    hidden, hidden_turned, gate_slope, up_slope = gated([order(normed_two)] + team_two[1:], f_ffn)
    mark(hidden)

    two_turned = mark(turn_team([order(normed_two)] + team_two[1:]))
    d_pair = mark(gated_back([order(cotangent)] + team_g[1:], f_down, gate_slope, up_slope))
    d_own, d_side, d_sent = pair_back(order(d_pair), f_ffn)
    d_recv = links.across(mark(d_sent))

    d_side = mark((order(d_side) + d_recv[length:].astype(jnp.float32)).astype(jnp.bfloat16))
    d_theirs = links.sideways(d_side)
    ffn_sum = lax.psum_scatter(
        mark(pair_grad(order(two_turned), d_pair)),
        ("plane", "team"),
        scatter_dimension=0,
        tiled=True,
    )
    ffn_own, ffn_side, ffn_sent = product([order(hidden)], [f_down], kind="team")
    ffn_their = links.across(mark(ffn_sent))

    d_normed_two = (
        order(d_own) + d_recv[:length].astype(jnp.float32) + d_theirs.astype(jnp.float32)
    )
    ffn_gain_term = jnp.sum(d_normed_two * unit_two, axis=0)
    grad_in = cotangent.astype(jnp.float32)
    d_attended = grad_in + norm_back(d_normed_two, unit_two, scale_two, gain_two)
    d_branch = d_attended.astype(jnp.bfloat16)
    d_context = mark(product([d_branch], [f_out], across=True))
    ffn_side = mark((order(ffn_side) + ffn_their[length:].astype(jnp.float32)).astype(jnp.bfloat16))
    ffn_theirs = links.sideways(ffn_side)

    d_query, d_key, d_value, d_lined = run_backward(
        lengths, bias_rows, qkv, tied(d_context, ffn_side), lse, head_size
    )
    d_qkv = mark(jnp.concatenate([d_query, d_key, d_value], axis=2))
    d_mine = by_core(order(d_qkv)[0], d_qkv[1])
    d_other = by_core(d_qkv[1], d_qkv[0])
    owners = spread.slot_owners()
    d_normed_one = product(
        [order(d_mine), d_other], [qkv_half, qkv_other], across=True, kind="wide"
    )
    unit_one = floats_in * scale_one
    attn_gain_term = jnp.sum(d_normed_one * unit_one, axis=0)
    grad_tokens = mark(
        (d_attended + norm_back(d_normed_one, unit_one, scale_one, gain_one)).astype(jnp.bfloat16)
    )
    table_term = lax.dot_general(
        one_hot,
        order(d_lined).reshape(head_count, -1),
        (((1,), (1,)), ((), ())),
        precision=lax.Precision.HIGHEST,
    )
    terms = jnp.concatenate([attn_gain_term, ffn_gain_term, table_term.reshape(-1)])
    terms = mark(jnp.pad(terms, (0, -terms.shape[0] % 1024)).reshape(-1, 128))
    output = mark(
        (
            order(attended)
            + ffn_own
            + ffn_their[:length].astype(jnp.float32)
            + ffn_theirs.astype(jnp.float32)
        ).astype(jnp.bfloat16)
    )

    def packed(slots, grad, context_rows, added):
        return mark(
            packed_slots(
                one_turned,
                order(grad),
                context_rows,
                d_branch,
                slots,
                [owners[slot] for slot in slots],
                reps,
                planes,
                added,
            )
        )

    exchanges = links.spread_steps()

    def summed_on():
        nonlocal terms
        terms = mark(order(terms) + arrived_terms)

    back = packed([spread.turned_slot(slot) for slot in range(reps)], d_other, context_other, [])
    arrived_terms = exchanges.pop(0)(terms)
    arrived = [links.across(back)]
    low, high = reps // 2, reps
    for stage in range(spread.stages):
        summed_on()
        sent = packed(range(low, high), d_mine, context_own, [(value, low) for value in arrived])
        arrived_terms = exchanges.pop(0)(terms)
        arrived.append(spread.swap(sent, stage))
        if stage == 0:
            down_sum = lax.psum_scatter(
                mark(
                    column_slots(
                        order(hidden_turned), team_g, [jnp.int32(k) for k in range(reps)], width // reps
                    )
                ),
                ("plane", "team"),
                scatter_dimension=0,
                tiled=True,
            )
            order.last = (*order.last, ffn_sum)
        low, high = low // 2, low
    summed_on()
    sent = packed([0], d_mine, context_own, [(value, 0) for value in arrived])
    packed_parts = links.along_parts(sent, share_rows)
    ffn_steps = spread.gather_steps(order(ffn_sum))
    ffn_shares = next(ffn_steps)
    came = exchanges.pop(0)(terms)
    packed_total = mark(
        sum(
            part.astype(jnp.float32)
            for part in [order(packed_parts[0], ffn_shares[0][1])] + packed_parts[1:]
        ).astype(jnp.bfloat16)
    )
    packed_shares = spread.gathered(packed_total)
    for ffn_shares in ffn_steps:
        pass
    terms = tied(terms, packed_total) + came
    came = exchanges.pop(0)(terms)
    down_shares = spread.gathered(tied(down_sum, packed_shares[0][1]))
    terms = tied(terms, *packed_shares[0]) + came
    for exchange in exchanges:
        terms = terms + exchange(terms)
    terms = terms.reshape(-1)

    def by_owner(parts):
        per = len(parts) // 2
        low = jnp.concatenate(parts[:per], axis=0)
        high = jnp.concatenate(parts[per:], axis=0)
        return by_core(low, high), by_core(high, low)

    def wings_apart(parts):
        return parts[0::2] + parts[1::2]

    parts = in_order(None, *down_shares)
    grad_down = jnp.concatenate(
        [jnp.concatenate(parts[w::2], axis=0)[:piece] for w in (0, 1)], axis=0
    ).astype(jnp.float32)
    parts = in_order(None, *ffn_shares)
    per = reps // 2
    low, high = wings_apart(parts[:per]), wings_apart(parts[per:])
    low, high = jnp.concatenate(low, axis=0), jnp.concatenate(high, axis=0)
    ffn_mine, ffn_send = by_core(low, high), by_core(high, low)
    ffn_other = links.across(ffn_send)
    grad_gate, grad_up = join_columns(core, ffn_mine, ffn_other, piece, padded)

    parts = in_order(None, *packed_shares)
    grad_out = jnp.concatenate(
        [unfolded(part[:, wide:], fold) for part in parts], axis=1
    ).astype(jnp.float32)
    qkv_mine, qkv_send = by_owner([part[:, :wide] for part in parts])
    qkv_recv = links.across(qkv_send)
    grad_halves = (by_core(qkv_mine, qkv_recv), by_core(qkv_recv, qkv_mine))
    grad_query, grad_key, grad_value = [
        jnp.concatenate(
            [value[:, kind * half : (kind + 1) * half] for value in grad_halves], axis=1
        ).astype(jnp.float32)
        for kind in range(3)
    ]
    grad_norm_attn = lax.dynamic_slice_in_dim(terms, links.place * shard_rows, shard_rows)
    grad_norm_ffn = lax.dynamic_slice_in_dim(terms, width + links.place * shard_rows, shard_rows)
    table_size = bias_table.size
    grad_table = lax.dynamic_slice_in_dim(
        terms, 2 * width + links.place * table_size, table_size
    ).reshape(bias_table.shape)
    return (
        output,
        grad_tokens,
        grad_query,
        grad_key,
        grad_value,
        grad_out,
        grad_gate,
        grad_up,
        grad_down,
        grad_table,
        grad_norm_attn,
        grad_norm_ffn,
    )


def solution(mesh):
    reps, group = mesh.shape["rep"], mesh.shape["shard"]
    devices = mesh.devices.reshape(reps // 2, 2, group // 2, 2)
    rows, part = P(AXES[2:], None), P(AXES[2:])
    tokens = P(AXES, None)
    return jax.shard_map(
        functools.partial(layer, reps, group),
        mesh=jax.sharding.Mesh(devices, AXES),
        in_specs=(tokens, P(AXES), P()) + (rows,) * 8 + (part, part, tokens),
        out_specs=(tokens, tokens) + (rows,) * 8 + (part, part),
        check_vma=False,
    )
```
